32 devices in a mesh: dp: 8 (over z, y), tensor: 4 (over x, core).
Axes of the slice: x: 2, y: 2, z: 4, core: 2. Of those that a mesh axis runs over, the one named last changes fastest.
Arguments:
- layer_in: float32 [4096, 1024], P('dp', 'tensor'), may hold values from -18 to 18
- cotangent: float32 [4096, 1024], P('dp', 'tensor'), may hold values from -6 to 6
- segment_ids: int32 [8, 512], P('dp'), may hold values from 0 to 2, never falling along the last dimension, each value on 1 to 256 neighbouring positions
- owner_map: int32 [2, 192], replicated, may hold values from 0 to 191, as said below
- masters: float32 [2, 768, 128, 128], P(None, ('dp', 'tensor')), may hold values from -0.375 to 0.375
- left_stats: float32 [2, 768, 128, 128], P(None, ('dp', 'tensor')), may hold values from -524288 to 524288, as said below
- right_stats: float32 [2, 768, 128, 128], P(None, ('dp', 'tensor')), may hold values from -524288 to 524288, as said below
- left_roots: float32 [2, 768, 128, 128], P(None, ('dp', 'tensor')), may hold values from -0.13834965 to 0.13834965, as said below
- right_roots: float32 [2, 768, 128, 128], P(None, ('dp', 'tensor')), may hold values from -0.13834965 to 0.13834965, as said below
- vectors: float32 [2, 8, 1024], P(None, None, 'tensor'), may hold values from -1.5 to 2.5, as said below
- up_bias: float32 [2, 4096], P(None, 'tensor'), may hold values from -1.5 to 1.5
Outputs:
- layer_out: float32 [4096, 1024], P('dp', 'tensor')
- input_grad: float32 [4096, 1024], P('dp', 'tensor')
- weight_grads: float32 [2, 768, 128, 128], P(None, ('dp', 'tensor'))
- new_left: float32 [2, 768, 128, 128], P(None, ('dp', 'tensor'))
- new_right: float32 [2, 768, 128, 128], P(None, ('dp', 'tensor'))
- new_weights: float32 [2, 768, 128, 128], P(None, ('dp', 'tensor'))
- vector_grads: float32 [2, 8, 1024], P(None, None, 'tensor')
- vectors_new: float32 [2, 8, 1024], P(None, None, 'tensor')
- up_bias_grads: float32 [2, 4096], P(None, 'tensor')
- up_bias_new: float32 [2, 4096], P(None, 'tensor')
The draws below stay inside these ranges and needn't reach their ends.
Inputs may be any that keep to these rules, and one draw needn't show every extreme that they name: `segment_ids`: ids do not fall along a row; each id names one run of at most 256 positions of its row. For each layer a permutation of 0 to 191; block b of an index of tensor is held by index owner_map // 24 of dp in slot owner_map % 24. `left_stats`: Symmetric. `right_stats`: Symmetric. `left_roots`: Symmetric. `right_roots`: Symmetric. `vectors`: gains are positive.
All inputs are finite; a program needn't handle non-finite values.
Results may differ from the reference program's by a relative error of at most 0.033.
The reference program's roundings to bfloat16 on the way count: a program that leaves them out, or rounds other values in their place, can miss the bound.
Values may be sent and summed in bfloat16 or wider, within the bound.
No kernel may reach another device: no remote copies, remote signals or barrier semaphores. Data moves between devices by JAX's collectives and lax.ppermute only.
A program may use at most 192 MiB of HBM per device.

```python
import math
import jax
import jax.numpy as jnp
import numpy as np
from jax import lax

D = 1024
HEADS = 16
HD = 64
FF = 4096
SEQ = 512
ENCODER_LAYERS = 2
PRECOND_SIDE = 128
TOKENS = 4096
DT = 256
FT = 1024
AXIS_BLOCKS = 192
KSLOT = 24
LAYER_BLOCKS = 768
N_DP = 8
N_TENSOR = 4


def owner_order(key):
    return jnp.stack([jax.random.permutation(jax.random.fold_in(key, 100 + layer_idx), AXIS_BLOCKS) for layer_idx in range(ENCODER_LAYERS)]).astype(jnp.int32)


def kind_of_slots(key):
    ordering = owner_order(key)
    inverse = jnp.argsort(ordering, axis=1)
    block_slot_index = jnp.arange(LAYER_BLOCKS)
    tensor_total = LAYER_BLOCKS // AXIS_BLOCKS
    position = block_slot_index // (tensor_total * KSLOT) * KSLOT + block_slot_index % KSLOT
    block_ids = inverse[:, position]
    tile_area = PRECOND_SIDE * PRECOND_SIDE
    n_qkv = 3 * D * DT // tile_area
    n_out = DT * D // tile_area
    n_up = D * FT // tile_area
    first_cut = (block_ids >= n_qkv).astype(jnp.int32)
    second_cut = (block_ids >= n_qkv + n_out).astype(jnp.int32)
    third_cut = (block_ids >= n_qkv + n_out + n_up).astype(jnp.int32)
    return first_cut + second_cut + third_cut


def kind_lookup(slot_kinds, entries):
    lookup = jnp.array(entries, jnp.float32)
    return lookup[slot_kinds][:, :, None, None]


def weight_spread(slot_kinds):
    return kind_lookup(slot_kinds, [D ** (-0.5), 3.0 * D ** (-0.5), D ** (-0.5), FF ** (-0.5)])


def grad_size(slot_kinds):
    return kind_lookup(slot_kinds, [0.5, 0.3, 0.2, 0.45]) * math.sqrt(TOKENS)


def statistic(slot_kinds, diag_factor, off_values):
    size_sq = grad_size(slot_kinds) ** 2
    eye_mask = jnp.eye(PRECOND_SIDE, dtype=bool)
    mirrored = (off_values + jnp.swapaxes(off_values, -1, -2)) * 0.5 ** 0.5
    return jnp.where(eye_mask, PRECOND_SIDE * size_sq * diag_factor, 0.5 * math.sqrt(PRECOND_SIDE) * size_sq * mirrored)


def inverse_root(slot_kinds, diag_factor, off_values):
    amplitude = jnp.sqrt(weight_spread(slot_kinds) / (0.5 * grad_size(slot_kinds)))
    eye_mask = jnp.eye(PRECOND_SIDE, dtype=bool)
    mirrored = (off_values + jnp.swapaxes(off_values, -1, -2)) * 0.5 ** 0.5
    return amplitude * jnp.where(eye_mask, diag_factor, 0.3 * PRECOND_SIDE ** (-0.5) * mirrored)


def draw_owner_map(key, part):
    return owner_order(key)


def draw_masters(key, part):
    slot_kinds = kind_of_slots(key)
    key = jax.random.fold_in(key, 1)
    whole_shape = (ENCODER_LAYERS, LAYER_BLOCKS, PRECOND_SIDE, PRECOND_SIDE)
    raw_values = jax.random.truncated_normal(key, -4.0, 4.0, whole_shape, jnp.float32)
    return raw_values * weight_spread(slot_kinds)


def draw_left_stats(key, part):
    slot_kinds = kind_of_slots(key)
    key = jax.random.fold_in(key, 2)
    first_key, second_key = jax.random.split(key)
    whole_shape = (ENCODER_LAYERS, LAYER_BLOCKS, PRECOND_SIDE, PRECOND_SIDE)
    diag_factor = jnp.exp(jax.random.uniform(first_key, whole_shape, jnp.float32, 0.0, math.log(4.0)))
    off_values = jax.random.truncated_normal(second_key, -4.0, 4.0, whole_shape, jnp.float32)
    return statistic(slot_kinds, diag_factor, off_values)


def draw_right_stats(key, part):
    slot_kinds = kind_of_slots(key)
    key = jax.random.fold_in(key, 3)
    first_key, second_key = jax.random.split(key)
    whole_shape = (ENCODER_LAYERS, LAYER_BLOCKS, PRECOND_SIDE, PRECOND_SIDE)
    diag_factor = jnp.exp(jax.random.uniform(first_key, whole_shape, jnp.float32, 0.0, math.log(4.0)))
    off_values = jax.random.truncated_normal(second_key, -4.0, 4.0, whole_shape, jnp.float32)
    return statistic(slot_kinds, diag_factor, off_values)


def draw_left_roots(key, part):
    slot_kinds = kind_of_slots(key)
    key = jax.random.fold_in(key, 4)
    first_key, second_key = jax.random.split(key)
    whole_shape = (ENCODER_LAYERS, LAYER_BLOCKS, PRECOND_SIDE, PRECOND_SIDE)
    diag_factor = jnp.exp(jax.random.uniform(first_key, whole_shape, jnp.float32, math.log(0.7), math.log(1.4)))
    off_values = jax.random.truncated_normal(second_key, -4.0, 4.0, whole_shape, jnp.float32)
    return inverse_root(slot_kinds, diag_factor, off_values)


def draw_right_roots(key, part):
    slot_kinds = kind_of_slots(key)
    key = jax.random.fold_in(key, 5)
    first_key, second_key = jax.random.split(key)
    whole_shape = (ENCODER_LAYERS, LAYER_BLOCKS, PRECOND_SIDE, PRECOND_SIDE)
    diag_factor = jnp.exp(jax.random.uniform(first_key, whole_shape, jnp.float32, math.log(0.7), math.log(1.4)))
    off_values = jax.random.truncated_normal(second_key, -4.0, 4.0, whole_shape, jnp.float32)
    return inverse_root(slot_kinds, diag_factor, off_values)


def draw_layer_in(key, part):
    key = jax.random.fold_in(key, 7)
    first_key = jax.random.fold_in(key, 0)
    position = jnp.arange(D, dtype=jnp.float32) / (D - 1)
    raw_values = jax.random.truncated_normal(first_key, -4.0, 4.0, (TOKENS, D), jnp.float32)
    return raw_values * 3.0 ** position


def draw_vectors(key, part):
    key = jax.random.fold_in(key, 9)
    first_key, second_key = jax.random.split(key)
    whole_shape = (ENCODER_LAYERS, 8, D)
    position = jnp.arange(D, dtype=jnp.float32) / (D - 1)
    row_ids = jnp.arange(8)[:, None]
    gain_mask = (row_ids == 3) | (row_ids == 6)
    biases = 0.3 * jax.random.truncated_normal(first_key, -4.0, 4.0, whole_shape, jnp.float32)
    gain_rows = (0.6 + 1.2 * position) * (1.0 + 0.1 * jax.random.truncated_normal(second_key, -2.0, 2.0, whole_shape, jnp.float32))
    return jnp.where(gain_mask, gain_rows, biases)


def block_scale(stream_key, dims, shards, smallest, top_value):
    level = 1.0
    for dim, blocks in shards:
        steps = jax.random.uniform(jax.random.fold_in(jax.random.fold_in(stream_key, 6), dim), (blocks,), jnp.float32, smallest / len(shards), top_value / len(shards))
        level = level * jnp.repeat(jnp.exp(steps), dims[dim] // blocks).reshape((-1,) + (1,) * (len(dims) - 1 - dim))
    return level


def length_profile(count, total, bound, lean):
    loads = [(1 << 20) // math.isqrt(grade ** lean) + 1 for grade in range(2, count + 1)]
    surplus, given = total - bound - (count - 1), [1] * (count - 1)
    while surplus > 0:
        movable = [i for i in range(count - 1) if given[i] < bound]
        pool, left = sum([loads[i] for i in movable]), surplus
        for i in movable:
            addition = min(bound - given[i], max(1, left * loads[i] // pool), surplus)
            given[i] = given[i] + addition
            surplus = surplus - addition
    return np.array([bound] + given)


def uneven(rng, count, total, limit, skew):
    if count == 2:
        one = jax.random.randint(rng, (), max(1, total - limit), min(limit, total - 1) + 1)
        return jnp.stack([one, total - one])
    sizes = jnp.asarray(length_profile(count, total, limit, skew), jnp.int32)
    pairs = (count - 1) // 2
    giver, receiver = sizes[1:1 + 2 * pairs:2], sizes[2:2 + 2 * pairs:2]
    slack = jnp.minimum(giver - 1, limit - receiver)
    passed = jax.random.randint(jax.random.fold_in(rng, 1), (pairs,), 0, 1 << 20) % (slack + 1)
    sizes = sizes.at[1:1 + 2 * pairs:2].set(giver - passed).at[2:2 + 2 * pairs:2].set(receiver + passed)
    return sizes[jax.random.permutation(jax.random.fold_in(rng, 2), count)]


def noise(key, extent, deviation, reach, shards=(), kind=jnp.bfloat16):
    drawn = deviation * jax.random.normal(key, extent, jnp.float32)
    if shards:
        drawn = drawn * block_scale(key, extent, shards, -0.22, 0.18)
    return jnp.clip(drawn, -reach, reach).astype(kind)


def setup_inputs(seed: int = 0) -> dict:
    arg_keys = jax.random.split(jax.random.key(seed), 12)
    layer_in = draw_layer_in(jax.random.fold_in(arg_keys[11], 71), 0)
    cotangent = noise(arg_keys[1], (TOKENS, D), 1.0, 6.0, ((0, 8), (1, 4)), jnp.float32)
    segment_ids = jax.vmap(lambda own: jnp.searchsorted(jnp.cumsum(uneven(own, 3, SEQ, SEQ // 2, 2)), jnp.arange(SEQ), side="right"))(jax.random.split(arg_keys[2], (TOKENS // SEQ))).reshape((TOKENS // SEQ, SEQ)).astype(jnp.int32)
    owner_map = draw_owner_map(jax.random.fold_in(arg_keys[11], 71), 0)
    masters = draw_masters(jax.random.fold_in(arg_keys[11], 71), 0)
    left_stats = draw_left_stats(jax.random.fold_in(arg_keys[11], 71), 0)
    right_stats = draw_right_stats(jax.random.fold_in(arg_keys[11], 71), 0)
    left_roots = draw_left_roots(jax.random.fold_in(arg_keys[11], 71), 0)
    right_roots = draw_right_roots(jax.random.fold_in(arg_keys[11], 71), 0)
    vectors = draw_vectors(jax.random.fold_in(arg_keys[11], 71), 0)
    up_bias = noise(arg_keys[10], (ENCODER_LAYERS, FF), 0.3, 1.5, ((1, 4),), jnp.float32)
    return dict(layer_in=layer_in, cotangent=cotangent, segment_ids=segment_ids, owner_map=owner_map, masters=masters, left_stats=left_stats, right_stats=right_stats, left_roots=left_roots, right_roots=right_roots, vectors=vectors, up_bias=up_bias)


@jax.custom_vjp
def low(v):
    return lax.optimization_barrier(v.astype(jnp.bfloat16)).astype(jnp.float32)

@jax.custom_vjp
def low_back(v):
    return v

def low_keep(v):
    return (low(v), None)

def low_pass(kept, grad):
    return (grad,)

def back_keep(v):
    return (v, None)

def back_low(kept, grad):
    return (low(grad),)
low.defvjp(low_keep, low_pass)
low_back.defvjp(back_keep, back_low)
precise = lax.Precision.HIGHEST
eps_norm = 1e-12
stat_decay = 0.5
update_rate = 0.5

def unblock(blocks, rows_total, cols_total):
    shard_count = blocks.shape[0]
    tiled = blocks.reshape(shard_count, rows_total // PRECOND_SIDE, cols_total // PRECOND_SIDE, PRECOND_SIDE, PRECOND_SIDE)
    return tiled.transpose(0, 1, 3, 2, 4).reshape(shard_count, rows_total, cols_total)

def assemble(slots, owner_map):
    tile_area = PRECOND_SIDE * PRECOND_SIDE
    n_qkv = 3 * D * DT // tile_area
    n_out = DT * D // tile_area
    n_up = D * FT // tile_area
    result = []
    for layer_idx in range(ENCODER_LAYERS):
        by_shard = slots[layer_idx].reshape(N_DP, N_TENSOR, KSLOT, PRECOND_SIDE, PRECOND_SIDE).transpose(1, 0, 2, 3, 4).reshape(N_TENSOR, AXIS_BLOCKS, PRECOND_SIDE, PRECOND_SIDE)
        blocks = jnp.take(by_shard, owner_map[layer_idx], axis=1)
        qkv_all = unblock(blocks[:, :n_qkv], D, 3 * DT)
        out_all = unblock(blocks[:, n_qkv:n_qkv + n_out], DT, D)
        up_all = unblock(blocks[:, n_qkv + n_out:n_qkv + n_out + n_up], D, FT)
        down_all = unblock(blocks[:, n_qkv + n_out + n_up:], FT, D)
        query_w = qkv_all[:, :, :DT].transpose(1, 0, 2).reshape(D, D)
        key_w = qkv_all[:, :, DT:2 * DT].transpose(1, 0, 2).reshape(D, D)
        value_w = qkv_all[:, :, 2 * DT:].transpose(1, 0, 2).reshape(D, D)
        out_w = out_all.reshape(D, D)
        up_w = up_all.transpose(1, 0, 2).reshape(D, FF)
        down_w = down_all.reshape(FF, D)
        result.append((query_w, key_w, value_w, out_w, up_w, down_w))
    return tuple(result)

def norm_apply(hidden, gain_row, shift_row):
    center = lax.optimization_barrier(jnp.mean(hidden, axis=-1, keepdims=True))
    centred = hidden - center
    spread = lax.optimization_barrier(jnp.mean(centred * centred, axis=-1, keepdims=True))
    return centred * lax.rsqrt(spread + eps_norm) * gain_row + shift_row

def attend(packed):
    query, key_rows, values, allowed = packed
    scores = jnp.einsum('shd,khd->hsk', query, key_rows, precision=precise) * float(HD) ** (-0.5)
    scores = low_back(scores)
    scores = jnp.where(allowed[None], scores, -1e+30)
    attention = jax.nn.softmax(scores, axis=-1)
    return jnp.einsum('hsk,khd->shd', low(attention), values, precision=precise)
attend_saved = jax.checkpoint(attend)

def layer_forward(hidden_in, weight_set, vector_rows, up_row, allowed):
    query_w, key_w, value_w, out_w, up_w, down_w = weight_set
    row_count = allowed.shape[0]
    head_shape = (row_count, SEQ, HEADS, HD)
    narrow = low(hidden_in)
    query = low_back(low(jnp.dot(narrow, query_w, precision=precise) + vector_rows[0]))
    key_rows = low_back(low(jnp.dot(narrow, key_w, precision=precise)))
    values = low_back(low(jnp.dot(narrow, value_w, precision=precise) + vector_rows[1]))
    mixture = lax.map(attend_saved, (query.reshape(head_shape), key_rows.reshape(head_shape), values.reshape(head_shape), allowed))
    mixture = low_back(low(mixture.reshape(row_count * SEQ, D)))
    attn_out = low_back(jnp.dot(mixture, out_w, precision=precise)) + vector_rows[2]
    middle = norm_apply(hidden_in + attn_out, vector_rows[3], vector_rows[4])
    pre_act = low_back(jnp.dot(low(middle), up_w, precision=precise) + up_row)
    activated = low(jax.nn.gelu(pre_act, approximate=False))
    ffn_out = low_back(jnp.dot(activated, down_w, precision=precise)) + vector_rows[5]
    return norm_apply(middle + ffn_out, vector_rows[6], vector_rows[7])

def block_forward(weights_all, vector_all, up_all, hidden_blk, allowed):
    hidden_now = hidden_blk
    for layer_idx in range(ENCODER_LAYERS):
        hidden_now = layer_forward(hidden_now, weights_all[layer_idx], vector_all[layer_idx], up_all[layer_idx], allowed)
    return hidden_now

def reference(layer_in, cotangent, segment_ids, owner_map, masters, left_stats, right_stats, left_roots, right_roots, vectors, up_bias):
    rounded = low(masters)
    assembled, assemble_back = jax.vjp(lambda slots: assemble(slots, owner_map), rounded)
    row_total = TOKENS // SEQ
    rows_block = math.gcd(row_total, 8)
    block_count = row_total // rows_block

    def scan_step(totals, block_in):
        hidden_blk, cot_blk, seg_blk = block_in
        allowed = seg_blk[:, :, None] == seg_blk[:, None, :]
        output, pull_back = jax.vjp(lambda w_all, v_all, u_all, h_blk: block_forward(w_all, v_all, u_all, h_blk, allowed), assembled, vectors, up_bias, hidden_blk)
        grad_w, grad_v, grad_u, grad_h = pull_back(cot_blk)
        totals = jax.tree.map(jnp.add, totals, (grad_w, grad_v, grad_u))
        return (totals, (output, grad_h))
    starting = jax.tree.map(jnp.zeros_like, (assembled, vectors, up_bias))
    sliced = (layer_in.reshape(block_count, rows_block * SEQ, D), cotangent.reshape(block_count, rows_block * SEQ, D), segment_ids.reshape(block_count, rows_block, SEQ))
    (grad_w, grad_v, grad_u), (outputs, grad_inputs) = lax.scan(scan_step, starting, sliced)
    layer_out = outputs.reshape(TOKENS, D)
    input_grad = grad_inputs.reshape(TOKENS, D)
    weight_grads = assemble_back(grad_w)[0]
    left_new = stat_decay * left_stats + (1.0 - stat_decay) * jnp.einsum('lkij,lkmj->lkim', weight_grads, weight_grads, precision=precise)
    right_new = stat_decay * right_stats + (1.0 - stat_decay) * jnp.einsum('lkji,lkjm->lkim', weight_grads, weight_grads, precision=precise)
    right_side = jnp.einsum('lkij,lkjm->lkim', weight_grads, right_roots, precision=precise)
    precond = jnp.einsum('lkij,lkjm->lkim', left_roots, right_side, precision=precise)
    new_weights = masters - update_rate * precond
    vector_rate = 0.5 / math.sqrt(TOKENS)
    return (layer_out, input_grad, weight_grads, left_new, right_new, new_weights, grad_v, vectors - vector_rate * grad_v, grad_u, up_bias - vector_rate * grad_u)
```

```python
import functools
import math

import jax
import jax.numpy as jnp
from jax import lax
from jax.experimental import pallas as pl
from jax.experimental.pallas import tpu as pltpu
from jax.sharding import PartitionSpec as P

HD = 64
eps_norm = 1e-12
stat_decay = 0.5
update_rate = 0.5
f32 = jnp.float32
bf16 = jnp.bfloat16

LAST = (((1,), (1,)), ((), ()))
FIRST = (((0,), (0,)), ((), ()))


def vmem_spec(count):
    return [pl.BlockSpec(memory_space=pltpu.VMEM)] * count


def params(mib=56):
    return pltpu.CompilerParams(vmem_limit_bytes=mib * 1024 * 1024)


def shape(dims, dtype):
    return jax.ShapeDtypeStruct(dims, dtype)


def cat_rows(refs):
    return jnp.concatenate([ref[...] for ref in refs], axis=0)


def matrix(ref, rows, cols):
    width = ref.shape[1]
    return jnp.concatenate(
        [
            jnp.concatenate(
                [ref[(r * cols + c) // width, (r * cols + c) % width] for c in range(cols)], axis=1
            )
            for r in range(rows)
        ],
        axis=0,
    )


def swap(values, axis, flip):
    count = lax.axis_size(axis)
    return lax.ppermute(values, axis, [(i, i ^ flip) for i in range(count)])


def gather_tokens(piece):
    far = swap(piece, "tensor", 2)
    near = swap(piece, "tensor", 1)
    both = swap(far, "tensor", 1)
    return (piece, far, near, both)


def scatter_sum(send, keep):
    rows = send.shape[0] // 2
    first = swap(send, "tensor", 1)
    second = swap((keep[rows:] + first[rows:].astype(f32)).astype(bf16), "tensor", 2)
    return (keep, first, second)


def to_tokens(values):
    index = lax.axis_index("tensor")
    x_pos, core = index // 2, index % 2
    rows, width = values.shape
    half, quarter = rows // 2, rows // 4
    mine = lax.dynamic_slice(values, (x_pos * half, 0), (half, width))
    other = lax.dynamic_slice(values, ((1 - x_pos) * half, 0), (half, width))
    pair = jnp.stack([mine, swap(other, "tensor", 2)])
    keep = lax.dynamic_slice(pair, (0, core * quarter, 0), (2, quarter, width))
    send = lax.dynamic_slice(pair, (0, (1 - core) * quarter, 0), (2, quarter, width))
    got = swap(send, "tensor", 1)
    relative = jnp.stack([keep[0], got[0], keep[1], got[1]])
    ordered = jnp.take(relative, jnp.arange(4) ^ index, axis=0)
    return ordered.transpose(1, 0, 2).reshape(quarter, 4 * width)


def from_tokens(values):
    index = lax.axis_index("tensor")
    rows, wide = values.shape
    width = wide // 4
    groups = values.reshape(rows, 4, width).transpose(1, 0, 2)
    relative = jnp.take(groups, jnp.arange(4) ^ index, axis=0)
    got = swap(jnp.stack([relative[1], relative[3]]), "tensor", 1)
    far = swap(jnp.stack([relative[2], got[1]]), "tensor", 2)
    chunks = jnp.stack([relative[0], got[0], far[0], far[1]])
    ordered = jnp.take(chunks, jnp.arange(4) ^ index, axis=0)
    return ordered.reshape(4 * rows, width)


def cross(values, planes):
    pairs = [(z * 2 + y, z * 2 + 1 - y) for z in planes for y in range(2)]
    return lax.ppermute(values, "dp", pairs)


def hop(values, planes, step):
    pairs = [(z * 2 + y, (z + step) * 2 + y) for z in planes for y in range(2)]
    return lax.ppermute(values, "dp", pairs)


def ends_swap(values):
    return lax.ppermute(values, "dp", [(0, 6), (1, 7), (6, 0), (7, 1)])


def after(values, *others):
    return lax.optimization_barrier((values,) + tuple(others))[0]


def spread_blocks(own):
    up_one = hop(own, (0, 1, 2), 1)
    down_one = hop(own, (1, 2, 3), -1)
    own_y = cross(own, (0, 1, 2, 3))
    up_two = hop(up_one, (1, 2), 1)
    down_two = hop(down_one, (2, 1), -1)
    ends = ends_swap(after(own, up_one, down_one))
    up_one_y = cross(up_one, (1, 2, 3))
    down_one_y = cross(down_one, (0, 1, 2))
    up_two_y = cross(up_two, (2, 3))
    down_two_y = cross(down_two, (0, 1))
    ends_y = cross(ends, (0, 3))
    return (
        (own, up_one, down_one, up_two, down_two, ends),
        (own_y, up_one_y, down_one_y, up_two_y, down_two_y, ends_y),
    )


def source_table(inverse, slots):
    dp_index = lax.axis_index("dp")
    plane, column = dp_index // 2, dp_index % 2
    end_step = 3 - 2 * plane
    steps = jnp.stack([0 * plane, plane * 0 - 1, plane * 0 + 1, plane * 0 - 2, plane * 0 + 2, end_step])
    target = plane + steps
    valid = (target >= 0) & (target <= 3)
    valid = valid.at[5].set((plane == 0) | (plane == 3))
    both_target = jnp.concatenate([target * 2 + column, target * 2 + 1 - column])
    both_valid = jnp.concatenate([valid, valid])
    picked = jnp.take(inverse.reshape(8, slots), jnp.clip(both_target, 0, 7), axis=0)
    return jnp.where(both_valid[:, None], picked, -1).astype(jnp.int32)


def assemble_kernel(source_count, slots, table, *refs):
    sources, out, sem = refs[:source_count], refs[source_count], refs[source_count + 1]
    for j in range(source_count):

        @pl.when(table[j, 0] >= 0)
        def _(j=j):
            @pl.loop(0, slots)
            def _(s):
                pltpu.make_async_copy(sources[j].at[s], out.at[table[j, s]], sem).start()

    for j in range(source_count):

        @pl.when(table[j, 0] >= 0)
        def _(j=j):
            @pl.loop(0, slots)
            def _(s):
                pltpu.make_async_copy(sources[j].at[s], out.at[table[j, s]], sem).wait()


def assemble(sources, table, total):
    slots, side = sources[0].shape[0], sources[0].shape[1]
    count = len(sources)
    return pl.pallas_call(
        functools.partial(assemble_kernel, count, slots),
        grid_spec=pltpu.PrefetchScalarGridSpec(
            num_scalar_prefetch=1,
            grid=(),
            in_specs=[pl.BlockSpec(memory_space=pl.ANY)] * count,
            out_specs=pl.BlockSpec(memory_space=pl.ANY),
            scratch_shapes=[pltpu.SemaphoreType.DMA],
        ),
        out_shape=shape((total, side, side), bf16),
        compiler_params=params(8),
        cost_estimate=pl.CostEstimate(flops=0, bytes_accessed=4 * total * side * side, transcendentals=0),
        name="assemble",
    )(table, *sources)


def gather_weights(own, owner_row):
    total = owner_row.shape[0]
    slots = own.shape[0]
    positions = jnp.arange(total, dtype=jnp.int32)
    hits = owner_row[None, :] == positions[:, None]
    inverse = jnp.sum(jnp.where(hits, positions[None, :], 0), axis=1)
    if lax.axis_size("dp") == 8:
        straight, crossed = spread_blocks(own)
        table = source_table(inverse, slots)
        last = crossed[-1]
        return assemble(straight + crossed, table, total), last
    whole = lax.all_gather(own, "dp", axis=0, tiled=True)
    return assemble((whole,), inverse[None, :].astype(jnp.int32), total), whole


def send_positions(owner_row, slots):
    if lax.axis_size("dp") != 8:
        return owner_row
    dp_index = lax.axis_index("dp")
    plane, column = dp_index // 2, dp_index % 2
    order = jnp.array([[3, 2, 1, 0], [0, 3, 2, 1], [1, 2, 3, 0], [0, 1, 2, 3]], jnp.int32)
    owner = owner_row // slots
    place = jnp.take(jnp.take(order, plane, axis=0), owner // 2)
    side = (owner % 2 == column).astype(jnp.int32)
    return ((place * 2 + side) * slots + owner_row % slots).astype(jnp.int32)


def reduce_blocks(grads, slots):
    if lax.axis_size("dp") != 8:
        return (lax.psum_scatter(grads, "dp", scatter_dimension=0, tiled=True),)
    side = grads.shape[-1]
    parts = grads.reshape(4, 2, slots, side, side)
    plane = lax.axis_index("dp") // 2
    everywhere = (0, 1, 2, 3)
    got = {}
    for k in (1, 0, 2, 3):
        got[k] = cross(parts[k, 0], everywhere)

    def total(k, *more):
        value = parts[k, 1].astype(f32) + got[k].astype(f32)
        for extra in more:
            value = value + extra.astype(f32)
        return value.astype(bf16)

    two = total(1)
    up_two = hop(two, (0, 1), 1)
    down_two = hop(two, (3, 2), -1)
    low = plane == 1
    near = total(0, jnp.where(low, down_two, up_two))
    ends = ends_swap(near)
    out_near = lax.ppermute(near, "dp", [(2, 0), (3, 1), (4, 6), (5, 7)])
    far = total(2, jnp.where(low, up_two, down_two))
    up_one = hop(far, (0, 1), 1)
    down_one = hop(far, (3, 2), -1)
    return (parts[3, 1], got[3], ends, out_near, up_one, down_one)


def norm_kernel(base, keep, first, second, vec, low_out, full_out, normed_out, scale_out, *, rows):
    bias, gain, shift = rows
    hidden = (
        base[...]
        + keep[...]
        + first[...].astype(f32)
        + second[...].astype(f32)
        + vec[bias : bias + 1, :]
    )
    center = jnp.mean(hidden, axis=1, keepdims=True)
    centred = hidden - center
    spread = jnp.mean(centred * centred, axis=1, keepdims=True)
    scale = lax.rsqrt(spread + eps_norm)
    normed = centred * scale
    full = normed * vec[gain : gain + 1, :] + vec[shift : shift + 1, :]
    full_out[...] = full
    low_out[...] = full.astype(bf16)
    normed_out[...] = normed
    scale_out[...] = scale


def top_half(array):
    return pl.BlockSpec((array.shape[0] // 2, array.shape[1]), lambda i: (0, 0))


def whole_spec(array):
    nd = len(array.shape)
    return pl.BlockSpec(tuple(array.shape), lambda i, nd=nd: (0,) * nd)


def norm_step(base, sums, vec, rows):
    keep, first, second = sums
    tokens, width = base.shape
    outs = [
        shape((tokens, width), bf16),
        shape((tokens, width), f32),
        shape((tokens, width), f32),
        shape((tokens, 1), f32),
    ]
    return pl.pallas_call(
        functools.partial(norm_kernel, rows=rows),
        grid=(1,),
        in_specs=[whole_spec(base), top_half(keep), top_half(first), whole_spec(second), whole_spec(vec)],
        out_specs=[whole_spec(o) for o in outs],
        out_shape=outs,
        compiler_params=params(24),
        cost_estimate=pl.CostEstimate(flops=20 * tokens * width, bytes_accessed=20 * tokens * width, transcendentals=tokens),
        name="norm",
    )(base, keep, first, second, vec)


def norm_back_kernel(*refs, gain, summed):
    if summed:
        base, keep, first, second, normed, scale, vec, low_out, full_out, sums_out = refs
        grad = base[...] + keep[...] + first[...].astype(f32) + second[...].astype(f32)
    else:
        base, normed, scale, vec, low_out, full_out, sums_out = refs
        grad = base[...]
    value = normed[...]
    scaled = grad * vec[gain : gain + 1, :]
    mean_grad = jnp.mean(scaled, axis=1, keepdims=True)
    mean_cross = jnp.mean(scaled * value, axis=1, keepdims=True)
    result = scale[...] * (scaled - mean_grad - value * mean_cross)
    full_out[...] = result
    low_out[...] = result.astype(bf16)
    sums_out[0:1, :] = jnp.sum(result, axis=0, keepdims=True)
    sums_out[1:2, :] = jnp.sum(grad * value, axis=0, keepdims=True)
    sums_out[2:3, :] = jnp.sum(grad, axis=0, keepdims=True)


def norm_back_step(base, sums, normed, scale, vec, gain):
    tokens, width = base.shape
    outs = [shape((tokens, width), bf16), shape((tokens, width), f32), shape((3, width), f32)]
    operands = [base]
    specs = [whole_spec(base)]
    if sums is not None:
        keep, first, second = sums
        operands += [keep, first, second]
        specs += [top_half(keep), top_half(first), whole_spec(second)]
    operands += [normed, scale, vec]
    specs += [whole_spec(normed), whole_spec(scale), whole_spec(vec)]
    return pl.pallas_call(
        functools.partial(norm_back_kernel, gain=gain, summed=sums is not None),
        grid=(1,),
        in_specs=specs,
        out_specs=[whole_spec(o) for o in outs],
        out_shape=outs,
        compiler_params=params(24),
        cost_estimate=pl.CostEstimate(flops=20 * tokens * width, bytes_accessed=20 * tokens * width, transcendentals=0),
        name="norm_back",
    )(*operands)


def store_sums(total, send_out, keep_out):
    half = total.shape[0] // 2
    send_out[...] = total[half:].astype(bf16)
    keep_out[...] = total[:half]


def attend_kernel(
    p0, p1, p2, p3, w_qkv, w_out, vec, seg_col, seg_row,
    query_out, key_out, value_out, mix_out, log_out, send_out, keep_out, bias,
):
    wide = cat_rows((p0, p1, p2, p3))
    tokens, model = wide.shape
    width = query_out.shape[1]
    tile = w_qkv.shape[-1]
    projected = jnp.dot(wide, matrix(w_qkv, model // tile, 3 * width // tile), preferred_element_type=f32)
    query = (projected[:, :width] + vec[0:1, :]).astype(bf16) * jnp.asarray(HD**-0.5, bf16)
    keys = projected[:, width : 2 * width].astype(bf16)
    values = (projected[:, 2 * width :] + vec[1:2, :]).astype(bf16)
    query_out[...] = query
    key_out[...] = keys
    value_out[...] = values
    bias[...] = jnp.where(seg_col[...] == seg_row[...], 0.0, -1e30)
    lane = lax.broadcasted_iota(jnp.int32, (tokens, 128), 1)
    logs = jnp.zeros((tokens, 128), f32)
    mixes = []
    for pair in range(width // 128):
        cols = slice(pair * 128, pair * 128 + 128)
        halves = []
        for part in range(128 // HD):
            inside = (lane >= part * HD) & (lane < part * HD + HD)
            one = jnp.where(inside, query[:, cols], jnp.zeros((), bf16))
            scores = lax.dot_general(one, keys[:, cols], LAST, preferred_element_type=f32) + bias[...]
            top = jnp.max(scores, axis=1, keepdims=True)
            exponent = jnp.exp(scores - top)
            total = jnp.sum(exponent, axis=1, keepdims=True)
            attention = (exponent * (1.0 / total)).astype(bf16)
            halves.append((inside, jnp.dot(attention, values[:, cols], preferred_element_type=f32)))
            logs = jnp.where(lane == pair * (128 // HD) + part, top + jnp.log(total), logs)
        mixed = halves[0][1]
        for inside, other in halves[1:]:
            mixed = jnp.where(inside, other, mixed)
        mixes.append(mixed.astype(bf16))
    mixture = jnp.concatenate(mixes, axis=1)
    mix_out[...] = mixture
    log_out[...] = jnp.transpose(logs)[0:8, :]
    total = jnp.dot(mixture, matrix(w_out, width // tile, model // tile), preferred_element_type=f32)
    store_sums(total, send_out, keep_out)


def block_rows(array, start, count):
    return pl.BlockSpec((count,) + tuple(array.shape[1:]), lambda i: (start // count, 0, 0, 0))


def attend_step(pieces, blocks, counts, vec, seg_col, seg_row):
    quarter, model = pieces[0].shape
    tokens, width = 4 * quarter, vec.shape[1]
    n_qkv, n_out, n_up = counts
    per = blocks.shape[1]
    outs = [
        shape((tokens, width), bf16),
        shape((tokens, width), bf16),
        shape((tokens, width), bf16),
        shape((tokens, width), bf16),
        shape((8, tokens), f32),
        shape((tokens // 2, model), bf16),
        shape((tokens // 2, model), f32),
    ]
    return pl.pallas_call(
        attend_kernel,
        grid=(1,),
        in_specs=[whole_spec(p) for p in pieces]
        + [block_rows(blocks, 0, n_qkv // per), block_rows(blocks, n_qkv // per, n_out // per)]
        + [whole_spec(vec), whole_spec(seg_col), whole_spec(seg_row)],
        out_specs=[whole_spec(o) for o in outs],
        out_shape=outs,
        scratch_shapes=[pltpu.VMEM((tokens, tokens), f32)],
        compiler_params=params(),
        cost_estimate=pl.CostEstimate(
            flops=2 * tokens * model * 4 * width + 4 * tokens * tokens * width * 2,
            bytes_accessed=8 * 1024 * 1024,
            transcendentals=tokens * tokens * width // HD,
        ),
        name="attend",
    )(*pieces, blocks, blocks, vec, seg_col, seg_row)


def attend_back_kernel(
    p0, p1, p2, p3, w_out, w_qkv, query_in, key_in, value_in, log_in, seg_col, seg_row,
    grad_out, sums_out, send_out, keep_out, bias,
):
    wide = cat_rows((p0, p1, p2, p3))
    tokens, model = wide.shape
    width = query_in.shape[1]
    tile = w_qkv.shape[-1]
    grad_mix = lax.dot_general(
        wide, matrix(w_out, width // tile, model // tile), LAST, preferred_element_type=f32
    ).astype(bf16)
    bias[...] = jnp.where(seg_col[...] == seg_row[...], 0.0, -1e30)
    lane = lax.broadcasted_iota(jnp.int32, (tokens, 128), 1)
    grads = ([], [], [])
    for pair in range(width // 128):
        cols = slice(pair * 128, pair * 128 + 128)
        query, keys, values, mix = query_in[:, cols], key_in[:, cols], value_in[:, cols], grad_mix[:, cols]
        picked = [None, None, None]
        for part in range(128 // HD):
            head = pair * (128 // HD) + part
            inside = (lane >= part * HD) & (lane < part * HD + HD)
            zero = jnp.zeros((), bf16)
            scores = (
                lax.dot_general(jnp.where(inside, keys, zero), query, LAST, preferred_element_type=f32)
                + bias[...]
            )
            attention = jnp.exp(scores - log_in[head : head + 1, :])
            pulled = lax.dot_general(jnp.where(inside, values, zero), mix, LAST, preferred_element_type=f32)
            inner = jnp.sum(attention * pulled, axis=0, keepdims=True)
            grad_scores = (attention * (pulled - inner)).astype(bf16)
            three = (
                lax.dot_general(grad_scores, keys, FIRST, preferred_element_type=f32) * (HD**-0.5),
                jnp.dot(grad_scores, query, preferred_element_type=f32),
                jnp.dot(attention.astype(bf16), mix, preferred_element_type=f32),
            )
            for which in range(3):
                if part == 0:
                    picked[which] = three[which]
                else:
                    picked[which] = jnp.where(inside, three[which], picked[which])
        for which in range(3):
            grads[which].append(picked[which].astype(bf16))
    joined = [jnp.concatenate(g, axis=1) for g in grads]
    every = jnp.concatenate(joined, axis=1)
    grad_out[...] = every
    sums_out[0:1, :] = jnp.sum(joined[0].astype(f32), axis=0, keepdims=True)
    sums_out[1:2, :] = jnp.sum(joined[2].astype(f32), axis=0, keepdims=True)
    total = lax.dot_general(
        every, matrix(w_qkv, model // tile, 3 * width // tile), LAST, preferred_element_type=f32
    )
    store_sums(total, send_out, keep_out)


def attend_back_step(pieces, blocks, counts, query, keys, values, logs, seg_col, seg_row):
    quarter, model = pieces[0].shape
    tokens, width = query.shape
    n_qkv, n_out, n_up = counts
    per = blocks.shape[1]
    outs = [
        shape((tokens, 3 * width), bf16),
        shape((2, width), f32),
        shape((tokens // 2, model), bf16),
        shape((tokens // 2, model), f32),
    ]
    return pl.pallas_call(
        attend_back_kernel,
        grid=(1,),
        in_specs=[whole_spec(p) for p in pieces]
        + [block_rows(blocks, n_qkv // per, n_out // per), block_rows(blocks, 0, n_qkv // per)]
        + [whole_spec(a) for a in (query, keys, values, logs, seg_col, seg_row)],
        out_specs=[whole_spec(o) for o in outs],
        out_shape=outs,
        scratch_shapes=[pltpu.VMEM((tokens, tokens), f32)],
        compiler_params=params(),
        cost_estimate=pl.CostEstimate(
            flops=2 * tokens * model * 4 * width + 10 * tokens * tokens * width * 2,
            bytes_accessed=8 * 1024 * 1024,
            transcendentals=tokens * tokens * width // HD,
        ),
        name="attend_back",
    )(*pieces, blocks, blocks, query, keys, values, logs, seg_col, seg_row)


def ffn_kernel(p0, p1, p2, p3, w_up, w_down, bias, act_out, slope_out, send_out, keep_out, total):
    step = pl.program_id(0)
    wide = cat_rows((p0, p1, p2, p3))
    model = wide.shape[1]
    tile = w_up.shape[-1]
    cols = act_out.shape[1] // tile
    pre = jnp.dot(wide, matrix(w_up, model // tile, cols), preferred_element_type=f32) + bias[...]
    cdf = 0.5 + 0.5 * lax.erf(pre * (0.5**0.5))
    slope_out[...] = cdf + pre * (jnp.exp(-0.5 * pre * pre) * (1.0 / math.sqrt(2.0 * math.pi)))
    activated = (pre * cdf).astype(bf16)
    act_out[...] = activated
    part = jnp.dot(activated, matrix(w_down, cols, model // tile), preferred_element_type=f32)

    @pl.when(step == 0)
    def _():
        total[...] = part

    @pl.when(step > 0)
    def _():
        total[...] += part

    @pl.when(step == pl.num_programs(0) - 1)
    def _():
        store_sums(total[...], send_out, keep_out)


def fixed(array):
    nd = len(array.shape)
    return pl.BlockSpec(tuple(array.shape), lambda i, nd=nd: (0,) * nd)


def ffn_specs(blocks, counts, chunk_blocks):
    n_qkv, n_out, n_up = counts
    per = blocks.shape[1]
    side = blocks.shape[2]
    up_row = (n_qkv + n_out) // per
    up_rows = n_up // per
    down_row = (n_qkv + n_out + n_up) // per
    up_spec = pl.BlockSpec((up_rows, chunk_blocks, side, side), lambda i: (up_row // up_rows, i, 0, 0))
    down_spec = pl.BlockSpec((chunk_blocks, per, side, side), lambda i: (down_row // chunk_blocks + i, 0, 0, 0))
    return up_spec, down_spec


def ffn_step(pieces, blocks, counts, up_bias, steps=4):
    quarter, model = pieces[0].shape
    tokens, hidden = 4 * quarter, up_bias.shape[1]
    chunk = hidden // steps
    up_spec, down_spec = ffn_specs(blocks, counts, chunk // blocks.shape[2])
    outs = [
        shape((tokens, hidden), bf16),
        shape((tokens, hidden), f32),
        shape((tokens // 2, model), bf16),
        shape((tokens // 2, model), f32),
    ]
    by_cols = pl.BlockSpec((tokens, chunk), lambda i: (0, i))
    return pl.pallas_call(
        ffn_kernel,
        grid=(steps,),
        in_specs=[fixed(p) for p in pieces]
        + [up_spec, down_spec, pl.BlockSpec((1, chunk), lambda i: (0, i))],
        out_specs=[by_cols, by_cols, fixed(outs[2]), fixed(outs[3])],
        out_shape=outs,
        scratch_shapes=[pltpu.VMEM((tokens, model), f32)],
        compiler_params=params(),
        cost_estimate=pl.CostEstimate(
            flops=4 * tokens * model * hidden, bytes_accessed=10 * 1024 * 1024, transcendentals=2 * tokens * hidden
        ),
        name="ffn",
    )(*pieces, blocks, blocks, up_bias)


def ffn_back_kernel(p0, p1, p2, p3, w_up, w_down, slope, grad_out, bias_out, send_out, keep_out, total):
    step = pl.program_id(0)
    wide = cat_rows((p0, p1, p2, p3))
    model = wide.shape[1]
    tile = w_up.shape[-1]
    cols = grad_out.shape[1] // tile
    pulled = lax.dot_general(wide, matrix(w_down, cols, model // tile), LAST, preferred_element_type=f32)
    grad = (pulled * slope[...]).astype(bf16)
    grad_out[...] = grad
    bias_out[...] = jnp.sum(grad.astype(f32), axis=0, keepdims=True)
    part = lax.dot_general(grad, matrix(w_up, model // tile, cols), LAST, preferred_element_type=f32)

    @pl.when(step == 0)
    def _():
        total[...] = part

    @pl.when(step > 0)
    def _():
        total[...] += part

    @pl.when(step == pl.num_programs(0) - 1)
    def _():
        store_sums(total[...], send_out, keep_out)


def ffn_back_step(pieces, blocks, counts, slope, steps=4):
    quarter, model = pieces[0].shape
    tokens, hidden = slope.shape
    chunk = hidden // steps
    up_spec, down_spec = ffn_specs(blocks, counts, chunk // blocks.shape[2])
    outs = [
        shape((tokens, hidden), bf16),
        shape((1, hidden), f32),
        shape((tokens // 2, model), bf16),
        shape((tokens // 2, model), f32),
    ]
    by_cols = pl.BlockSpec((tokens, chunk), lambda i: (0, i))
    return pl.pallas_call(
        ffn_back_kernel,
        grid=(steps,),
        in_specs=[fixed(p) for p in pieces] + [up_spec, down_spec, by_cols],
        out_specs=[by_cols, pl.BlockSpec((1, chunk), lambda i: (0, i)), fixed(outs[2]), fixed(outs[3])],
        out_shape=outs,
        scratch_shapes=[pltpu.VMEM((tokens, model), f32)],
        compiler_params=params(),
        cost_estimate=pl.CostEstimate(
            flops=4 * tokens * model * hidden, bytes_accessed=10 * 1024 * 1024, transcendentals=0
        ),
        name="ffn_back",
    )(*pieces, blocks, blocks, slope)


def weight_grad_kernel(jobs, chained, place, *refs):
    counts = [count for job in jobs for count in job[:2]]
    used = sum(counts)
    operands, rest = refs[:used], refs[used + chained :]
    out, stage, sem = rest
    side = stage.shape[-1]
    at = 0
    done = []
    slot = 0
    for left_count, right_count, base in jobs:
        left = operands[at : at + left_count]
        right = operands[at + left_count : at + left_count + right_count]
        at += left_count + right_count
        columns = cat_rows(right)
        per = columns.shape[1] // side
        width = left[0].shape[1]
        chunk = min(width, 2 * side)
        for start in range(0, width, chunk):
            rows = jnp.concatenate([ref[:, start : start + chunk] for ref in left], axis=0)
            result = lax.dot_general(rows, columns, FIRST, preferred_element_type=f32).astype(bf16)
            for i in range(chunk // side):
                for j in range(per):
                    block = base + (start // side + i) * per + j
                    stage[slot] = result[i * side : (i + 1) * side, j * side : (j + 1) * side]
                    pltpu.make_async_copy(stage.at[slot], out.at[place[block]], sem).start()
                    done.append((slot, block))
                    slot += 1
    for slot, block in done:
        pltpu.make_async_copy(stage.at[slot], out.at[place[block]], sem).wait()


def weight_grad_step(jobs, place, target, total, side):
    operands = [a for left, right, base in jobs for a in left + right]
    layout = tuple((len(left), len(right), base) for left, right, base in jobs)
    blocks = sum(
        left[0].shape[1] // side * (right[0].shape[1] // side) for left, right, base in jobs
    )
    chained = 0 if target is None else 1
    extra = [] if target is None else [target]
    aliases = {} if target is None else {1 + len(operands): 0}
    tokens = sum(a.shape[0] for a in jobs[0][0])
    return pl.pallas_call(
        functools.partial(weight_grad_kernel, layout, chained),
        grid_spec=pltpu.PrefetchScalarGridSpec(
            num_scalar_prefetch=1,
            grid=(),
            in_specs=vmem_spec(len(operands)) + [pl.BlockSpec(memory_space=pl.ANY)] * chained,
            out_specs=pl.BlockSpec(memory_space=pl.ANY),
            scratch_shapes=[pltpu.VMEM((blocks, side, side), bf16), pltpu.SemaphoreType.DMA],
        ),
        out_shape=shape((total, side, side), bf16),
        input_output_aliases=aliases,
        compiler_params=params(),
        cost_estimate=pl.CostEstimate(
            flops=2 * tokens * blocks * side * side,
            bytes_accessed=4 * blocks * side * side,
            transcendentals=0,
        ),
        name="weight_grad",
    )(place, *operands, *extra)


def update_kernel(part_count, chained, *refs):
    parts = refs[:part_count]
    masters, left, right, left_root, right_root = refs[part_count : part_count + 5]
    grad_out, left_out, right_out, weight_out = refs[part_count + 5 + chained :]
    grad = parts[0][...].astype(f32)
    for part in parts[1:]:
        grad = grad + part[...].astype(f32)
    grad_out[0] = grad
    for b in range(grad.shape[0]):
        low = grad[b].astype(bf16)
        left_out[0, b] = stat_decay * left[0, b] + (1.0 - stat_decay) * lax.dot_general(
            low, low, LAST, preferred_element_type=f32
        )
        right_out[0, b] = stat_decay * right[0, b] + (1.0 - stat_decay) * lax.dot_general(
            low, low, FIRST, preferred_element_type=f32
        )
        inner = jnp.dot(low, right_root[0, b].astype(bf16), preferred_element_type=f32)
        outer = jnp.dot(left_root[0, b].astype(bf16), inner.astype(bf16), preferred_element_type=f32)
        weight_out[0, b] = masters[0, b] - update_rate * outer


def update_step(parts, layer, state, previous):
    layers, slots, side, _ = state[0].shape
    group = 4 if slots % 4 == 0 else slots
    one = pl.BlockSpec((1, group, side, side), lambda i: (layer, i, 0, 0))
    chained = [] if previous is None else list(previous)
    aliases = {len(parts) + 5 + k: k for k in range(len(chained))}
    return pl.pallas_call(
        functools.partial(update_kernel, len(parts), len(chained)),
        grid=(slots // group,),
        in_specs=[pl.BlockSpec((group, side, side), lambda i: (i, 0, 0))] * len(parts)
        + [one] * 5
        + [pl.BlockSpec(memory_space=pl.ANY)] * len(chained),
        out_specs=[one] * 4,
        out_shape=[shape(state[0].shape, f32)] * 4,
        input_output_aliases=aliases,
        compiler_params=params(32),
        cost_estimate=pl.CostEstimate(
            flops=8 * slots * side**3, bytes_accessed=44 * slots * side * side, transcendentals=0
        ),
        name="update",
    )(*parts, *state, *chained)


def sum_all(values):
    if lax.axis_size("dp") != 8:
        return lax.psum(values, ("dp", "tensor"))
    values = values + swap(values, "tensor", 1)
    values = values + swap(values, "tensor", 2)
    values = values + swap(values, "dp", 1)
    values = values + swap(values, "dp", 2)
    return values + swap(values, "dp", 4)


def body(
    layer_in,
    cotangent,
    segment_ids,
    owner_map,
    masters,
    left_stats,
    right_stats,
    left_roots,
    right_roots,
    vectors,
    up_bias,
):
    layers, slots, side = masters.shape[0], masters.shape[1], masters.shape[-1]
    tokens, width = layer_in.shape
    model = width * lax.axis_size("tensor")
    hidden = up_bias.shape[1]
    tile_rows = model // side
    n_qkv = tile_rows * (3 * width // side)
    n_out = width // side * tile_rows
    n_up = tile_rows * (hidden // side)
    counts = (n_qkv, n_out, n_up)
    total = owner_map.shape[1]
    index = lax.axis_index("tensor")
    quarter = tokens // 4

    low = [masters[layer].astype(bf16) for layer in range(layers)]
    weights = []
    last = None
    for layer in range(layers):
        own = low[layer] if last is None else after(low[layer], last)
        gathered, last = gather_weights(own, owner_map[layer])
        weights.append(gathered.reshape(total // tile_rows, tile_rows, side, side))

    order = jnp.array([0, 2, 1, 3]) ^ index
    segments = jnp.take(segment_ids.reshape(4, quarter), order, axis=0).reshape(tokens)
    seg_col, seg_row = segments[:, None], segments[None, :]
    wide_vectors = lax.all_gather(vectors, "tensor", axis=2, tiled=True)

    stream = to_tokens(layer_in)
    stream_low = stream.astype(bf16)
    grad = to_tokens(cotangent)

    kept = []
    for layer in range(layers):
        vec, blocks = wide_vectors[layer], weights[layer]
        wide_in = gather_tokens(stream_low)
        query, keys, values, mixture, logs, send, keep = attend_step(
            wide_in, blocks, counts, vectors[layer], seg_col, seg_row
        )
        mid_low, middle, normed_one, scale_one = norm_step(stream, scatter_sum(send, keep), vec, (2, 3, 4))
        wide_mid = gather_tokens(mid_low)
        activated, slope, send, keep = ffn_step(wide_mid, blocks, counts, up_bias[layer : layer + 1])
        stream_low, stream, normed_two, scale_two = norm_step(middle, scatter_sum(send, keep), vec, (5, 6, 7))
        kept.append(
            (wide_in, query, keys, values, mixture, logs, normed_one, scale_one, wide_mid, activated, slope, normed_two, scale_two)
        )
    layer_out = from_tokens(stream)

    vector_sums = [None] * layers
    bias_sums = [None] * layers
    state = (masters, left_stats, right_stats, left_roots, right_roots)
    updated = None
    sums = None
    for layer in reversed(range(layers)):
        vec, blocks = wide_vectors[layer], weights[layer]
        (wide_in, query, keys, values, mixture, logs, normed_one, scale_one, wide_mid, activated, slope, normed_two, scale_two) = kept[layer]
        place = send_positions(owner_map[layer], slots)
        grad_low, grad_two, sums_two = norm_back_step(grad, sums, normed_two, scale_two, vec, 6)
        wide_grad = gather_tokens(grad_low)
        grad_pre, bias_sum, send, keep = ffn_back_step(wide_grad, blocks, counts, slope)
        sums = scatter_sum(send, keep)
        block_grads = weight_grad_step(
            [((wide_mid), (grad_pre,), n_qkv + n_out), ((activated,), (wide_grad), n_qkv + n_out + n_up)],
            place, None, total, side,
        )
        grad_low, grad_one, sums_one = norm_back_step(grad_two, sums, normed_one, scale_one, vec, 3)
        wide_first = gather_tokens(grad_low)
        grad_qkv, qv_sums, send, keep = attend_back_step(
            wide_first, blocks, counts, query, keys, values, logs, seg_col, seg_row
        )
        sums = scatter_sum(send, keep)
        block_grads = weight_grad_step(
            [((wide_in), (grad_qkv,), 0), ((mixture,), (wide_first), n_qkv)],
            place, block_grads, total, side,
        )
        grad = grad_one
        parts = reduce_blocks(block_grads, slots)
        updated = update_step(parts, layer, state, updated)
        spread = jnp.concatenate([jnp.zeros_like(sums_one[:2]), sums_one, sums_two], axis=0)
        vector_sums[layer] = lax.dynamic_update_slice(spread, qv_sums, (0, index * width))
        bias_sums[layer] = lax.dynamic_update_slice(
            jnp.zeros((1, 4 * hidden), f32), bias_sum, (0, index * hidden)
        ).reshape(4 * hidden // model, model)
    input_grad = from_tokens(
        grad + sums[0][:quarter] + sums[1][:quarter].astype(f32) + sums[2].astype(f32)
    )

    small = sum_all(jnp.stack([jnp.concatenate(pair, axis=0) for pair in zip(vector_sums, bias_sums)]))
    vector_grads = lax.dynamic_slice(small[:, :8], (0, 0, index * width), (layers, 8, width))
    up_bias_grads = lax.dynamic_slice(
        small[:, 8:].reshape(layers, 4 * hidden), (0, index * hidden), (layers, hidden)
    )
    reduced, left_new, right_new, new_weights = updated
    vector_rate = 0.5 / math.sqrt(tokens * lax.axis_size("dp"))
    return (
        layer_out,
        input_grad,
        reduced,
        left_new,
        right_new,
        new_weights,
        vector_grads,
        vectors - vector_rate * vector_grads,
        up_bias_grads,
        up_bias - vector_rate * up_bias_grads,
    )


def solution(mesh):
    owned = P(None, ("dp", "tensor"), None, None)
    return jax.shard_map(
        body,
        mesh=mesh,
        in_specs=(
            P("dp", "tensor"),
            P("dp", "tensor"),
            P("dp", None),
            P(),
            owned,
            owned,
            owned,
            owned,
            owned,
            P(None, None, "tensor"),
            P(None, "tensor"),
        ),
        out_specs=(
            P("dp", "tensor"),
            P("dp", "tensor"),
            owned,
            owned,
            owned,
            owned,
            P(None, None, "tensor"),
            P(None, None, "tensor"),
            P(None, "tensor"),
            P(None, "tensor"),
        ),
        check_vma=False,
    )
```

```python
import functools
import math

import jax
import jax.numpy as jnp
from jax import lax
from jax.experimental import pallas as pl
from jax.experimental.pallas import tpu as pltpu
from jax.sharding import PartitionSpec as P

HD = 64
eps_norm = 1e-12
stat_decay = 0.5
update_rate = 0.5
f32 = jnp.float32
bf16 = jnp.bfloat16

LAST = (((1,), (1,)), ((), ()))
FIRST = (((0,), (0,)), ((), ()))


def vmem_spec(count):
    return [pl.BlockSpec(memory_space=pltpu.VMEM)] * count


def params(mib=40):
    return pltpu.CompilerParams(vmem_limit_bytes=mib * 1024 * 1024)


def cost(microseconds):
    return pl.CostEstimate(flops=0, bytes_accessed=int(microseconds * 3.4e6), transcendentals=0)


def shape(dims, dtype):
    return jax.ShapeDtypeStruct(dims, dtype)


def cat_rows(refs):
    return jnp.concatenate([ref[...] for ref in refs], axis=0)


def matrix(ref, rows, cols):
    width = ref.shape[1]
    return jnp.concatenate(
        [
            jnp.concatenate(
                [ref[(r * cols + c) // width, (r * cols + c) % width] for c in range(cols)], axis=1
            )
            for r in range(rows)
        ],
        axis=0,
    )


def flat_matrix(ref, base, rows, cols):
    return jnp.concatenate(
        [jnp.concatenate([ref[base + r * cols + c] for c in range(cols)], axis=1) for r in range(rows)], axis=0
    )


def swap(values, axis, flip):
    count = lax.axis_size(axis)
    return lax.ppermute(values, axis, [(i, i ^ flip) for i in range(count)])


def gather_tokens(piece):
    far = swap(piece, "tensor", 2)
    near = swap(piece, "tensor", 1)
    both = swap(far, "tensor", 1)
    return (piece, far, near, both)


def scatter_sum(send, keep):
    rows = send.shape[0] // 2
    first = swap(send, "tensor", 1)
    message = (keep[rows:] + first[rows:].astype(f32)).astype(bf16)
    return (keep, first, swap(message, "tensor", 2)), message


def by_index(relative):
    index = lax.axis_index("tensor")
    core, x_pos = index % 2 == 1, index // 2 == 1
    r0, r1, r2, r3 = relative
    a0, a1 = jnp.where(core, r1, r0), jnp.where(core, r0, r1)
    a2, a3 = jnp.where(core, r3, r2), jnp.where(core, r2, r3)
    return [
        jnp.where(x_pos, a2, a0),
        jnp.where(x_pos, a3, a1),
        jnp.where(x_pos, a0, a2),
        jnp.where(x_pos, a1, a3),
    ]


def to_tokens(values):
    rows, width = values.shape
    quarter = rows // 4
    r0, r1, r2, r3 = by_index([values[g * quarter : (g + 1) * quarter] for g in range(4)])
    got = swap(jnp.stack([r2, r3]), "tensor", 2)
    near = swap(jnp.stack([r1, got[1]]), "tensor", 1)
    return jnp.concatenate(by_index([r0, near[0], got[0], near[1]]), axis=1)


def from_tokens(values, marks=None):
    width = values.shape[1] // 4
    r0, r1, r2, r3 = by_index([values[:, g * width : (g + 1) * width] for g in range(4)])
    near = jnp.stack([r1, r3])
    got = swap(near if marks is None else after(near, marks[0]), "tensor", 1)
    rest = jnp.stack([r2, got[1]])
    far = swap(rest if marks is None else after(rest, marks[1]), "tensor", 2)
    return jnp.concatenate(by_index([r0, got[0], far[0], far[1]]), axis=0)


def cross(values, planes):
    pairs = [(z * 2 + y, z * 2 + 1 - y) for z in planes for y in range(2)]
    return lax.ppermute(values, "dp", pairs)


def hop(values, planes, step):
    pairs = [(z * 2 + y, (z + step) * 2 + y) for z in planes for y in range(2)]
    return lax.ppermute(values, "dp", pairs)


def ends_swap(values):
    return lax.ppermute(values, "dp", [(0, 6), (1, 7), (6, 0), (7, 1)])


def after(values, *others):
    return lax.optimization_barrier((values,) + tuple(others))[0]


def line_steps(plane):
    middle = (plane == 1) | (plane == 2)
    two = jnp.where(plane >= 2, -2, 2)
    return (
        0 * plane,
        jnp.where(plane == 0, 1, -1),
        jnp.where(middle, 1, two),
        jnp.where(middle, two, 3 - 2 * plane),
    )


def middle_plane(plane):
    return (plane == 1) | (plane == 2)


def weight_sources(own, owner_map, meanwhile):
    layers, total = owner_map.shape
    slots = own[0].shape[0]
    positions = jnp.arange(total, dtype=jnp.int32)
    hits = owner_map[:, None, :] == positions[None, :, None]
    inverse = jnp.sum(jnp.where(hits, positions[None, None, :], 0), axis=2).astype(jnp.int32)
    if lax.axis_size("dp") != 8:
        wholes = [lax.all_gather(values.astype(bf16), "dp", axis=0, tiled=True) for values in own]
        for stage in range(3):
            meanwhile(stage, None)
        return [((whole,), ((0, 0),), row[None, :]) for whole, row in zip(wholes, inverse)], None
    plane, column = lax.axis_index("dp") // 2, lax.axis_index("dp") % 2
    middle = middle_plane(plane)
    everywhere = (0, 1, 2, 3)
    spots = tuple((j, 0) for j in range(8))
    tables = []
    for layer in range(layers):
        owners = inverse[layer].reshape(8, slots)
        rows = []
        for side in (column, 1 - column):
            for step in line_steps(plane):
                mask = jnp.arange(8) == (plane + step) * 2 + side
                rows.append(jnp.sum(jnp.where(mask[:, None], owners, 0), axis=0))
        tables.append(jnp.stack(rows).astype(jnp.int32))

    first = own[0].astype(bf16)
    up_one = hop(first, (0, 1, 2), 1)
    down_one = hop(first, (1, 2, 3), -1)
    first_y = cross(first, everywhere)
    beside = meanwhile(0, None)
    done = (up_one, down_one, first_y) + beside[0]
    one = jnp.where(plane == 0, down_one, up_one)
    up_two = hop(after(up_one, *done), (1, 2), 1)
    down_two = hop(after(down_one, *done), (2, 1), -1)
    one_y = cross(after(one, *done), everywhere)
    beside += meanwhile(1, first_y)
    done = (up_two, down_two, one_y) + beside[1]
    two = up_two + down_two
    third = jnp.where(middle, down_one, after(two, one_y))
    ends = ends_swap(after(first, *done))
    third_y = cross(after(third, *done), everywhere)
    beside += meanwhile(2, one_y)
    done = (ends, third_y) + beside[2]
    last = jnp.where(middle, after(two, third_y), ends)
    last_y = cross(after(last, *done), everywhere)
    result = [((first, one, third, last, first_y, one_y, third_y, last_y), spots, tables[0])]
    points = {}

    for layer in range(1, layers):
        mine = after(own[layer], first_y).astype(bf16)
        start = after(mine, *done)
        up_one = hop(start, (0, 1, 2), 1)
        down_one = hop(start, (1, 2, 3), -1)
        one = jnp.where(plane == 0, down_one, up_one)
        up_two = hop(up_one, (1, 2), 1)
        down_two = hop(down_one, (2, 1), -1)
        mine_y = cross(after(mine, last_y), everywhere)
        two = up_two + down_two
        third = jnp.where(middle, after(down_one, one), two)
        ends = ends_swap(after(mine, up_two, down_two))
        one_y = cross(after(one, mine_y), everywhere)
        last = jnp.where(middle, after(two, third), ends)
        third_y = cross(after(third, one_y), everywhere)
        half = slots // 2
        inner_y = lax.ppermute(after(mine_y, ends), "dp", [(0, 4), (1, 5), (6, 2), (7, 3)])
        ends_y = ends_swap(after(mine_y, ends)[:half])
        rest_y = cross(after(ends, third_y)[half:], (0, 3))
        last_y = inner_y + jnp.concatenate([ends_y, rest_y])
        result.append(((mine, one, third, last, mine_y, one_y, third_y, last_y), spots, tables[layer]))
        if layer == 1:
            points.update(start=(up_one, down_one), attend=(up_two, down_two, mine_y), hidden=(ends, one_y))
        done = (last_y, third_y)
    return result, points


def send_positions(owner_row, slots):
    if lax.axis_size("dp") != 8:
        return owner_row
    dp_index = lax.axis_index("dp")
    plane, column = dp_index // 2, dp_index % 2
    order = ((3, 2, 0, 1), (1, 3, 2, 0), (0, 2, 3, 1), (1, 0, 2, 3))
    owner = owner_row // slots
    place = jnp.zeros_like(owner)
    for sender in range(4):
        for receiver in range(4):
            hit = (plane == sender) & (owner // 2 == receiver)
            place = jnp.where(hit, order[sender][receiver], place)
    side = (owner % 2 == column).astype(jnp.int32)
    return ((side * 4 + place) * slots + owner_row % slots).astype(jnp.int32)


def reduce_blocks(parts, small=None):
    if len(parts) == 1:
        if small is not None:
            small = lax.psum(small, "dp")
        return (lax.psum_scatter(parts[0], "dp", scatter_dimension=0, tiled=True),), small, None
    plane = lax.axis_index("dp") // 2
    everywhere = (0, 1, 2, 3)
    sending, staying = parts[:-4], parts[-4:]
    low = plane == 1

    def total(k, got, *more, then=()):
        value = after(staying[k], *then).astype(f32) + got.astype(f32)
        for extra in more:
            value = value + extra.astype(f32)
        return value.astype(bf16)

    def two_away(value):
        return hop(value, (0, 1), 1), hop(value, (3, 2), -1)

    def to_near(value):
        return lax.ppermute(value, "dp", [(2, 0), (3, 1), (4, 6), (5, 7)])

    got = [cross(sending[0], everywhere)]
    small = small + swap(small, "dp", 2)
    small = small + swap(small, "dp", 4)
    got.append(cross(after(sending[1], got[0], small), everywhere))
    up, down = two_away(total(0, got[0]))
    small = small + swap(after(small, got[0]), "dp", 1)
    got.append(cross(after(sending[2], got[1], up, down, small), everywhere))
    near = total(1, got[1], jnp.where(low, down, up))
    ends = ends_swap(near)
    got.append(cross(after(sending[3], got[2], ends), everywhere))
    far = total(2, got[2], jnp.where(low, up, down), then=(near,))
    mine = (staying[3], got[3], ends, to_near(after(near, ends)), *two_away(far))
    return mine, small, got


def norm_kernel(base, keep, first, second, vec, low_out, full_out, normed_out, scale_out, *, rows):
    bias, gain, shift = rows
    hidden = (
        base[...]
        + keep[...]
        + first[...].astype(f32)
        + second[...].astype(f32)
        + vec[bias : bias + 1, :]
    )
    center = jnp.mean(hidden, axis=1, keepdims=True)
    centred = hidden - center
    spread = jnp.mean(centred * centred, axis=1, keepdims=True)
    scale = lax.rsqrt(spread + eps_norm)
    normed = centred * scale
    full = normed * vec[gain : gain + 1, :] + vec[shift : shift + 1, :]
    full_out[...] = full
    low_out[...] = full.astype(bf16)
    normed_out[...] = normed
    scale_out[...] = scale


def top_half(array):
    return pl.BlockSpec((array.shape[0] // 2, array.shape[1]), lambda i: (0, 0))


def whole_spec(array):
    nd = len(array.shape)
    return pl.BlockSpec(tuple(array.shape), lambda i, nd=nd: (0,) * nd)


def norm_step(base, sums, vec, rows):
    keep, first, second = sums
    tokens, width = base.shape
    outs = [
        shape((tokens, width), bf16),
        shape((tokens, width), f32),
        shape((tokens, width), f32),
        shape((tokens, 1), f32),
    ]
    return pl.pallas_call(
        functools.partial(norm_kernel, rows=rows),
        grid=(1,),
        in_specs=[whole_spec(base), top_half(keep), top_half(first), whole_spec(second), whole_spec(vec)],
        out_specs=[whole_spec(o) for o in outs],
        out_shape=outs,
        compiler_params=params(12),
        cost_estimate=cost(1.2),
        name="norm",
    )(base, keep, first, second, vec)


def norm_back_kernel(*refs, gain, summed):
    if summed:
        base, keep, first, second, normed, scale, vec, low_out, full_out, sums_out = refs
        grad = base[...] + keep[...] + first[...].astype(f32) + second[...].astype(f32)
    else:
        base, normed, scale, vec, low_out, full_out, sums_out = refs
        grad = base[...]
    value = normed[...]
    scaled = grad * vec[gain : gain + 1, :]
    mean_grad = jnp.mean(scaled, axis=1, keepdims=True)
    mean_cross = jnp.mean(scaled * value, axis=1, keepdims=True)
    result = scale[...] * (scaled - mean_grad - value * mean_cross)
    full_out[...] = result
    low_out[...] = result.astype(bf16)
    sums_out[0:1, :] = jnp.sum(result, axis=0, keepdims=True)
    sums_out[1:2, :] = jnp.sum(grad * value, axis=0, keepdims=True)
    sums_out[2:3, :] = jnp.sum(grad, axis=0, keepdims=True)


def norm_back_step(base, sums, normed, scale, vec, gain):
    tokens, width = base.shape
    outs = [shape((tokens, width), bf16), shape((tokens, width), f32), shape((3, width), f32)]
    operands = [base]
    specs = [whole_spec(base)]
    if sums is not None:
        keep, first, second = sums
        operands += [keep, first, second]
        specs += [top_half(keep), top_half(first), whole_spec(second)]
    operands += [normed, scale, vec]
    specs += [whole_spec(normed), whole_spec(scale), whole_spec(vec)]
    return pl.pallas_call(
        functools.partial(norm_back_kernel, gain=gain, summed=sums is not None),
        grid=(1,),
        in_specs=specs,
        out_specs=[whole_spec(o) for o in outs],
        out_shape=outs,
        compiler_params=params(12),
        cost_estimate=cost(1.5),
        name="norm_back",
    )(*operands)


def store_sums(total, send_out, keep_out):
    half = total.shape[0] // 2
    send_out[...] = total[half:].astype(bf16)
    keep_out[...] = total[:half]


def start_blocks(sources, spots, table, stage, sem):
    slots = table.shape[1]
    for row, (which, first) in enumerate(spots):

        @pl.loop(0, slots, unroll=min(slots, 24))
        def _(s, row=row, which=which, first=first):
            pltpu.make_async_copy(sources[which].at[first + s], stage.at[table[row, s]], sem).start()


def attend_kernel(
    count, spots, n_qkv, n_out, table, *refs
):
    sources = refs[:count]
    (
        p0, p1, p2, p3, vec, seg_col, seg_row,
        query_out, key_out, value_out, mix_out, log_out, send_out, keep_out, attend_out, ffn_out,
        bias, stage, sems,
    ) = refs[count:]
    start_blocks(sources, spots, table, stage, sems.at[0])
    wide = cat_rows((p0, p1, p2, p3))
    bias[...] = jnp.where(seg_col[...] == seg_row[...], 0.0, -1e30)
    pltpu.make_async_copy(stage, stage, sems.at[0]).wait()
    cut = n_qkv + n_out
    copies = (
        pltpu.make_async_copy(stage.at[pl.ds(0, cut)], attend_out, sems.at[1]),
        pltpu.make_async_copy(stage.at[pl.ds(cut, ffn_out.shape[0])], ffn_out, sems.at[2]),
    )
    for copy in copies:
        copy.start()
    tokens, model = wide.shape
    width = query_out.shape[1]
    tile = stage.shape[-1]
    projected = jnp.dot(
        wide, flat_matrix(stage, 0, model // tile, 3 * width // tile), preferred_element_type=f32
    )
    query = (projected[:, :width] + vec[0:1, :]).astype(bf16) * jnp.asarray(HD**-0.5, bf16)
    keys = projected[:, width : 2 * width].astype(bf16)
    values = (projected[:, 2 * width :] + vec[1:2, :]).astype(bf16)
    query_out[...] = query
    key_out[...] = keys
    value_out[...] = values
    lane = lax.broadcasted_iota(jnp.int32, (tokens, 128), 1)
    logs = jnp.zeros((tokens, 128), f32)
    mixes = []
    for pair in range(width // 128):
        cols = slice(pair * 128, pair * 128 + 128)
        halves = []
        for part in range(128 // HD):
            inside = (lane >= part * HD) & (lane < part * HD + HD)
            one = jnp.where(inside, query[:, cols], jnp.zeros((), bf16))
            scores = lax.dot_general(one, keys[:, cols], LAST, preferred_element_type=f32) + bias[...]
            top = jnp.max(scores, axis=1, keepdims=True)
            exponent = jnp.exp(scores - top)
            total = jnp.sum(exponent, axis=1, keepdims=True)
            attention = (exponent * (1.0 / total)).astype(bf16)
            halves.append((inside, jnp.dot(attention, values[:, cols], preferred_element_type=f32)))
            logs = jnp.where(lane == pair * (128 // HD) + part, top + jnp.log(total), logs)
        mixed = halves[0][1]
        for inside, other in halves[1:]:
            mixed = jnp.where(inside, other, mixed)
        mixes.append(mixed.astype(bf16))
    mixture = jnp.concatenate(mixes, axis=1)
    mix_out[...] = mixture
    log_out[...] = jnp.transpose(logs)[0:8, :]
    total = jnp.dot(
        mixture, flat_matrix(stage, n_qkv, width // tile, model // tile), preferred_element_type=f32
    )
    store_sums(total, send_out, keep_out)
    for copy in copies:
        copy.wait()


def block_rows(array, start, count):
    return pl.BlockSpec((count,) + tuple(array.shape[1:]), lambda i: (start // count, 0, 0, 0))


def attend_step(pieces, weights, counts, vec, seg_col, seg_row):
    quarter, model = pieces[0].shape
    tokens, width = 4 * quarter, vec.shape[1]
    n_qkv, n_out, n_up = counts
    arrays, spots, table = weights
    side = arrays[0].shape[-1]
    total = n_qkv + n_out + 2 * n_up
    outs = [
        shape((tokens, width), bf16),
        shape((tokens, width), bf16),
        shape((tokens, width), bf16),
        shape((tokens, width), bf16),
        shape((8, tokens), f32),
        shape((tokens // 2, model), bf16),
        shape((tokens // 2, model), f32),
        shape((n_qkv + n_out, side, side), bf16),
        shape((2 * n_up, side, side), bf16),
    ]
    operands = list(pieces) + [vec, seg_col, seg_row]
    return pl.pallas_call(
        functools.partial(attend_kernel, len(arrays), spots, n_qkv, n_out),
        grid_spec=pltpu.PrefetchScalarGridSpec(
            num_scalar_prefetch=1,
            grid=(),
            in_specs=[pl.BlockSpec(memory_space=pl.ANY)] * len(arrays) + vmem_spec(len(operands)),
            out_specs=vmem_spec(7) + [pl.BlockSpec(memory_space=pl.ANY)] * 2,
            scratch_shapes=[
                pltpu.VMEM((tokens, tokens), f32),
                pltpu.VMEM((total, side, side), bf16),
                pltpu.SemaphoreType.DMA((3,)),
            ],
        ),
        out_shape=outs,
        compiler_params=params(60),
        cost_estimate=cost(11),
        name="attend",
    )(table, *arrays, *operands)


def attend_back_kernel(
    p0, p1, p2, p3, w_out, w_qkv, query_in, key_in, value_in, log_in, seg_col, seg_row,
    grad_out, sums_out, send_out, keep_out, bias,
):
    wide = cat_rows((p0, p1, p2, p3))
    tokens, model = wide.shape
    width = query_in.shape[1]
    tile = w_qkv.shape[-1]
    grad_mix = lax.dot_general(
        wide, matrix(w_out, width // tile, model // tile), LAST, preferred_element_type=f32
    ).astype(bf16)
    bias[...] = jnp.where(seg_col[...] == seg_row[...], 0.0, -1e30)
    lane = lax.broadcasted_iota(jnp.int32, (tokens, 128), 1)
    grads = ([], [], [])
    for pair in range(width // 128):
        cols = slice(pair * 128, pair * 128 + 128)
        query, keys, values, mix = query_in[:, cols], key_in[:, cols], value_in[:, cols], grad_mix[:, cols]
        picked = [None, None, None]
        for part in range(128 // HD):
            head = pair * (128 // HD) + part
            inside = (lane >= part * HD) & (lane < part * HD + HD)
            zero = jnp.zeros((), bf16)
            scores = (
                lax.dot_general(jnp.where(inside, keys, zero), query, LAST, preferred_element_type=f32)
                + bias[...]
            )
            attention = jnp.exp(scores - log_in[head : head + 1, :])
            pulled = lax.dot_general(jnp.where(inside, values, zero), mix, LAST, preferred_element_type=f32)
            inner = jnp.sum(attention * pulled, axis=0, keepdims=True)
            grad_scores = (attention * (pulled - inner)).astype(bf16)
            three = (
                lax.dot_general(grad_scores, keys, FIRST, preferred_element_type=f32) * (HD**-0.5),
                jnp.dot(grad_scores, query, preferred_element_type=f32),
                jnp.dot(attention.astype(bf16), mix, preferred_element_type=f32),
            )
            for which in range(3):
                if part == 0:
                    picked[which] = three[which]
                else:
                    picked[which] = jnp.where(inside, three[which], picked[which])
        for which in range(3):
            grads[which].append(picked[which].astype(bf16))
    joined = [jnp.concatenate(g, axis=1) for g in grads]
    every = jnp.concatenate(joined, axis=1)
    grad_out[...] = every
    sums_out[0:1, :] = jnp.sum(joined[0].astype(f32), axis=0, keepdims=True)
    sums_out[1:2, :] = jnp.sum(joined[2].astype(f32), axis=0, keepdims=True)
    total = lax.dot_general(
        every, matrix(w_qkv, model // tile, 3 * width // tile), LAST, preferred_element_type=f32
    )
    store_sums(total, send_out, keep_out)


def attend_back_step(pieces, blocks, counts, query, keys, values, logs, seg_col, seg_row):
    quarter, model = pieces[0].shape
    tokens, width = query.shape
    n_qkv, n_out, n_up = counts
    per = blocks.shape[1]
    outs = [
        shape((tokens, 3 * width), bf16),
        shape((2, width), f32),
        shape((tokens // 2, model), bf16),
        shape((tokens // 2, model), f32),
    ]
    return pl.pallas_call(
        attend_back_kernel,
        grid=(1,),
        in_specs=[whole_spec(p) for p in pieces]
        + [block_rows(blocks, n_qkv // per, n_out // per), block_rows(blocks, 0, n_qkv // per)]
        + [whole_spec(a) for a in (query, keys, values, logs, seg_col, seg_row)],
        out_specs=[whole_spec(o) for o in outs],
        out_shape=outs,
        scratch_shapes=[pltpu.VMEM((tokens, tokens), f32)],
        compiler_params=params(),
        cost_estimate=cost(6.5),
        name="attend_back",
    )(*pieces, blocks, blocks, query, keys, values, logs, seg_col, seg_row)


def ffn_kernel(p0, p1, p2, p3, w_up, w_down, bias, act_out, slope_out, send_out, keep_out, total):
    step = pl.program_id(0)
    wide = cat_rows((p0, p1, p2, p3))
    model = wide.shape[1]
    tile = w_up.shape[-1]
    cols = act_out.shape[1] // tile
    pre = jnp.dot(wide, matrix(w_up, model // tile, cols), preferred_element_type=f32) + bias[...]
    cdf = 0.5 + 0.5 * lax.erf(pre * (0.5**0.5))
    slope_out[...] = cdf + pre * (jnp.exp(-0.5 * pre * pre) * (1.0 / math.sqrt(2.0 * math.pi)))
    activated = (pre * cdf).astype(bf16)
    act_out[...] = activated
    part = jnp.dot(activated, matrix(w_down, cols, model // tile), preferred_element_type=f32)

    @pl.when(step == 0)
    def _():
        total[...] = part

    @pl.when(step > 0)
    def _():
        total[...] += part

    @pl.when(step == pl.num_programs(0) - 1)
    def _():
        store_sums(total[...], send_out, keep_out)


def fixed(array):
    nd = len(array.shape)
    return pl.BlockSpec(tuple(array.shape), lambda i, nd=nd: (0,) * nd)


def ffn_specs(blocks, counts, chunk_blocks):
    n_qkv, n_out, n_up = counts
    per = blocks.shape[1]
    side = blocks.shape[2]
    up_row = 0
    up_rows = n_up // per
    down_row = n_up // per
    up_spec = pl.BlockSpec((up_rows, chunk_blocks, side, side), lambda i: (up_row // up_rows, i, 0, 0))
    down_spec = pl.BlockSpec((chunk_blocks, per, side, side), lambda i: (down_row // chunk_blocks + i, 0, 0, 0))
    return up_spec, down_spec


def ffn_step(pieces, blocks, counts, up_bias, steps=4):
    quarter, model = pieces[0].shape
    tokens, hidden = 4 * quarter, up_bias.shape[1]
    chunk = hidden // steps
    up_spec, down_spec = ffn_specs(blocks, counts, chunk // blocks.shape[2])
    outs = [
        shape((tokens, hidden), bf16),
        shape((tokens, hidden), f32),
        shape((tokens // 2, model), bf16),
        shape((tokens // 2, model), f32),
    ]
    by_cols = pl.BlockSpec((tokens, chunk), lambda i: (0, i))
    return pl.pallas_call(
        ffn_kernel,
        grid=(steps,),
        in_specs=[fixed(p) for p in pieces]
        + [up_spec, down_spec, pl.BlockSpec((1, chunk), lambda i: (0, i))],
        out_specs=[by_cols, by_cols, fixed(outs[2]), fixed(outs[3])],
        out_shape=outs,
        scratch_shapes=[pltpu.VMEM((tokens, model), f32)],
        compiler_params=params(),
        cost_estimate=cost(7.5),
        name="ffn",
    )(*pieces, blocks, blocks, up_bias)


def ffn_back_kernel(p0, p1, p2, p3, w_up, w_down, slope, grad_out, bias_out, send_out, keep_out, total):
    step = pl.program_id(0)
    wide = cat_rows((p0, p1, p2, p3))
    model = wide.shape[1]
    tile = w_up.shape[-1]
    cols = grad_out.shape[1] // tile
    pulled = lax.dot_general(wide, matrix(w_down, cols, model // tile), LAST, preferred_element_type=f32)
    grad = (pulled * slope[...]).astype(bf16)
    grad_out[...] = grad
    bias_out[...] = jnp.sum(grad.astype(f32), axis=0, keepdims=True)
    part = lax.dot_general(grad, matrix(w_up, model // tile, cols), LAST, preferred_element_type=f32)

    @pl.when(step == 0)
    def _():
        total[...] = part

    @pl.when(step > 0)
    def _():
        total[...] += part

    @pl.when(step == pl.num_programs(0) - 1)
    def _():
        store_sums(total[...], send_out, keep_out)


def ffn_back_step(pieces, blocks, counts, slope, steps=4):
    quarter, model = pieces[0].shape
    tokens, hidden = slope.shape
    chunk = hidden // steps
    up_spec, down_spec = ffn_specs(blocks, counts, chunk // blocks.shape[2])
    outs = [
        shape((tokens, hidden), bf16),
        shape((1, hidden), f32),
        shape((tokens // 2, model), bf16),
        shape((tokens // 2, model), f32),
    ]
    by_cols = pl.BlockSpec((tokens, chunk), lambda i: (0, i))
    return pl.pallas_call(
        ffn_back_kernel,
        grid=(steps,),
        in_specs=[fixed(p) for p in pieces] + [up_spec, down_spec, by_cols],
        out_specs=[by_cols, pl.BlockSpec((1, chunk), lambda i: (0, i)), fixed(outs[2]), fixed(outs[3])],
        out_shape=outs,
        scratch_shapes=[pltpu.VMEM((tokens, model), f32)],
        compiler_params=params(),
        cost_estimate=cost(7),
        name="ffn_back",
    )(*pieces, blocks, blocks, slope)


def weight_grad_jobs(jobs, operands, side, store):
    at = 0
    for left_count, right_count, base in jobs:
        left = operands[at : at + left_count]
        right = operands[at + left_count : at + left_count + right_count]
        at += left_count + right_count
        columns = cat_rows(right)
        per = columns.shape[1] // side
        width = left[0].shape[1]
        chunk = min(width, 2 * side)
        for start in range(0, width, chunk):
            rows = jnp.concatenate([ref[:, start : start + chunk] for ref in left], axis=0)
            result = lax.dot_general(rows, columns, FIRST, preferred_element_type=f32).astype(bf16)
            for i in range(chunk // side):
                for j in range(per):
                    store(
                        base + (start // side + i) * per + j,
                        result[i * side : (i + 1) * side, j * side : (j + 1) * side],
                    )


def job_parts(jobs, side):
    operands = [a for left, right, base in jobs for a in left + right]
    layout = tuple((len(left), len(right), base) for left, right, base in jobs)
    blocks = sum(left[0].shape[1] // side * (right[0].shape[1] // side) for left, right, base in jobs)
    tokens = sum(a.shape[0] for a in jobs[0][0])
    return operands, layout, blocks, tokens


def first_grad_kernel(jobs, used, place, *refs):
    out = refs[used]

    def store(block, value):
        out[place[block]] = value

    weight_grad_jobs(jobs, refs[:used], out.shape[-1], store)


def first_grad_step(jobs, place, total, side):
    operands, layout, blocks, tokens = job_parts(jobs, side)
    return pl.pallas_call(
        functools.partial(first_grad_kernel, layout, len(operands)),
        grid_spec=pltpu.PrefetchScalarGridSpec(
            num_scalar_prefetch=1,
            grid=(),
            in_specs=vmem_spec(len(operands)),
            out_specs=pl.BlockSpec(memory_space=pltpu.VMEM),
        ),
        out_shape=shape((total, side, side), bf16),
        compiler_params=params(60),
        cost_estimate=cost(4),
        name="first_grad",
    )(place, *operands)


def last_grad_kernel(jobs, used, sizes, place, *refs):
    operands, earlier = refs[:used], refs[used]
    outs, stage, sems = refs[used + 1 : used + 1 + len(sizes)], refs[-2], refs[-1]
    side = stage.shape[-1]
    load = pltpu.make_async_copy(earlier, stage, sems.at[0])
    load.start()
    waited = []

    def store(block, value):
        if not waited:
            load.wait()
            waited.append(block)
        stage[place[block]] = value

    weight_grad_jobs(jobs, operands, side, store)
    copies, first = [], 0
    for k, size in enumerate(sizes):
        copies.append(pltpu.make_async_copy(stage.at[pl.ds(first, size)], outs[k], sems.at[1 + k]))
        copies[-1].start()
        first += size
    for copy in copies:
        copy.wait()


def last_grad_step(jobs, earlier, place, total, side, sizes):
    count = len(sizes)
    operands, layout, blocks, tokens = job_parts(jobs, side)
    return pl.pallas_call(
        functools.partial(last_grad_kernel, layout, len(operands), tuple(sizes)),
        grid_spec=pltpu.PrefetchScalarGridSpec(
            num_scalar_prefetch=1,
            grid=(),
            in_specs=vmem_spec(len(operands)) + [pl.BlockSpec(memory_space=pl.ANY)],
            out_specs=[pl.BlockSpec(memory_space=pl.ANY)] * count,
            scratch_shapes=[pltpu.VMEM((total, side, side), bf16), pltpu.SemaphoreType.DMA((1 + count,))],
        ),
        out_shape=[shape((size, side, side), bf16) for size in sizes],
        compiler_params=params(60),
        cost_estimate=cost(8),
        name="last_grad",
    )(place, *operands, earlier)


def update_kernel(part_count, chained, *refs):
    parts = refs[:part_count]
    masters, left, right, left_root, right_root = refs[part_count : part_count + 5]
    grad_out, left_out, right_out, weight_out = refs[part_count + 5 + chained :]
    grad = parts[0][...].astype(f32)
    for part in parts[1:]:
        grad = grad + part[...].astype(f32)
    grad_out[0] = grad
    for b in range(grad.shape[0]):
        low = grad[b].astype(bf16)
        left_out[0, b] = stat_decay * left[0, b] + (1.0 - stat_decay) * lax.dot_general(
            low, low, LAST, preferred_element_type=f32
        )
        right_out[0, b] = stat_decay * right[0, b] + (1.0 - stat_decay) * lax.dot_general(
            low, low, FIRST, preferred_element_type=f32
        )
        inner = jnp.dot(low, right_root[0, b].astype(bf16), preferred_element_type=f32)
        outer = jnp.dot(left_root[0, b].astype(bf16), inner.astype(bf16), preferred_element_type=f32)
        weight_out[0, b] = masters[0, b] - update_rate * outer


def update_step(parts, layer, state, previous):
    layers, slots, side, _ = state[0].shape
    group = 4 if slots % 4 == 0 else slots
    one = pl.BlockSpec((1, group, side, side), lambda i: (layer, i, 0, 0))
    chained = [] if previous is None else list(previous)
    aliases = {len(parts) + 5 + k: k for k in range(len(chained))}
    return pl.pallas_call(
        functools.partial(update_kernel, len(parts), len(chained)),
        grid=(slots // group,),
        in_specs=[pl.BlockSpec((group, side, side), lambda i: (i, 0, 0))] * len(parts)
        + [one] * 5
        + [pl.BlockSpec(memory_space=pl.ANY)] * len(chained),
        out_specs=[one] * 4,
        out_shape=[shape(state[0].shape, f32)] * 4,
        input_output_aliases=aliases,
        compiler_params=params(60),
        cost_estimate=cost(10),
        name="update",
    )(*parts, *state, *chained)


def sum_tensor(values):
    values = values + swap(values, "tensor", 1)
    return values + swap(values, "tensor", 2)


def body(
    layer_in,
    cotangent,
    segment_ids,
    owner_map,
    masters,
    left_stats,
    right_stats,
    left_roots,
    right_roots,
    vectors,
    up_bias,
):
    layers, slots, side = masters.shape[0], masters.shape[1], masters.shape[-1]
    tokens, width = layer_in.shape
    model = width * lax.axis_size("tensor")
    hidden = up_bias.shape[1]
    tile_rows = model // side
    n_qkv = tile_rows * (3 * width // side)
    n_out = width // side * tile_rows
    n_up = tile_rows * (hidden // side)
    counts = (n_qkv, n_out, n_up)
    total = owner_map.shape[1]
    index = lax.axis_index("tensor")
    quarter = tokens // 4

    segments = jnp.concatenate(
        by_index([segment_ids[:, g * quarter : (g + 1) * quarter] for g in range(4)]), axis=1
    )
    segments = jnp.concatenate(
        [segments[:, g * quarter : (g + 1) * quarter] for g in (0, 2, 1, 3)], axis=1
    )
    seg_col, seg_row = segments.reshape(tokens, 1), segments
    places = [send_positions(owner_map[layer], slots) for layer in range(layers)]

    made = {}

    def meanwhile(stage, mark):
        def hold(values):
            return values if mark is None else after(values, mark)

        if stage == 0:
            near = swap(vectors, "tensor", 1)
            far = swap(jnp.stack([vectors, near]), "tensor", 2)
            made["vectors"] = jnp.concatenate(by_index([vectors, near, far[0], far[1]]), axis=2)
            made["stream"] = to_tokens(layer_in)
            made["places"] = tuple(
                send_positions(owner_map[layer], slots) if layer == 0 else owner_map[layer] for layer in range(layers)
            )
            part = (made["vectors"], made["stream"]) + made["places"]
        elif stage == 1:
            made["wide"] = gather_tokens(hold(made["stream"]).astype(bf16))
            part = made["wide"] + (seg_col,)
        else:
            made["grad"] = to_tokens(hold(cotangent))
            part = (made["grad"],)
        return (part,)

    own = [masters[layer] for layer in range(layers)]
    sources, points = weight_sources(own, owner_map, meanwhile)
    paired = points is not None
    wide_vectors, stream, wide_in, grad, places = (
        made[name] for name in ("vectors", "stream", "wide", "grad", "places")
    )
    weights = []
    if paired:
        sources[0] = sources[0][:2] + (after(sources[0][2], *points["start"]),)

    kept = []
    for layer in range(layers):
        vec = wide_vectors[layer]
        if layer > 0:
            wide_in = gather_tokens(stream_low)
        query, keys, values, mixture, logs, send, keep, attend_blocks, ffn_blocks = attend_step(
            wide_in, sources[layer], counts, vectors[layer], seg_col, seg_row
        )
        attend_blocks = attend_blocks.reshape(-1, tile_rows, side, side)
        ffn_blocks = ffn_blocks.reshape(-1, tile_rows, side, side)
        weights.append((attend_blocks, ffn_blocks))
        if layer == 0 and paired:
            send = after(send, *points["attend"])
        sums, message = scatter_sum(send, keep)
        mid_low, middle, normed_one, scale_one = norm_step(stream, sums, vec, (2, 3, 4))
        wide_mid = gather_tokens(mid_low)
        activated, slope, send, keep = ffn_step(wide_mid, ffn_blocks, counts, up_bias[layer : layer + 1])
        if layer == 0 and paired:
            send = after(send, *points["hidden"])
        stream_low, stream, normed_two, scale_two = norm_step(middle, scatter_sum(send, keep)[0], vec, (5, 6, 7))
        kept.append(
            (wide_in, query, keys, values, mixture, logs, normed_one, scale_one, wide_mid, activated, slope, normed_two, scale_two)
        )

    vector_sums = [None] * layers
    bias_sums = [None] * layers
    state = (masters, left_stats, right_stats, left_roots, right_roots)
    updated = None
    sums = None
    waiting = []
    for layer in reversed(range(layers)):
        vec, (attend_blocks, ffn_blocks) = wide_vectors[layer], weights[layer]
        (wide_in, query, keys, values, mixture, logs, normed_one, scale_one, wide_mid, activated, slope, normed_two, scale_two) = kept[layer]
        first = layer == 0 and paired
        grad_low, grad_two, sums_two = norm_back_step(grad, sums, normed_two, scale_two, vec, 6)
        wide_grad = gather_tokens(grad_low)
        grad_pre, bias_sum, send, keep = ffn_back_step(wide_grad, ffn_blocks, counts, slope)
        sums, message = scatter_sum(send, keep)
        ffn_grads = None if first else first_grad_step(
            [(wide_mid, (grad_pre,), n_qkv + n_out), ((activated,), wide_grad, n_qkv + n_out + n_up)],
            after(places[layer], message), total, side,
        )
        if not first:
            sums = (after(sums[0], ffn_grads),) + sums[1:]
        grad_low, grad_one, sums_one = norm_back_step(grad_two, sums, normed_one, scale_one, vec, 3)
        wide_first = gather_tokens(grad_low)
        if first:
            ffn_grads = first_grad_step(
                [(wide_mid, (grad_pre,), n_qkv + n_out), ((activated,), wide_grad, n_qkv + n_out + n_up)],
                after(places[layer], grad_low), total, side,
            )
            wide_first = wide_first[:1] + (after(wide_first[1], ffn_grads),) + wide_first[2:]
        grad_qkv, qv_sums, send, keep = attend_back_step(
            wide_first, attend_blocks, counts, query, keys, values, logs, seg_col, seg_row
        )
        sums, message = scatter_sum(send, keep)
        sizes = [total]
        if paired:
            sizes = [total // 8] * 8 if layer == 0 else [total]
        block_parts = last_grad_step(
            [(wide_in, (grad_qkv,), 0), ((mixture,), wide_first, n_qkv)],
            ffn_grads, places[layer] if first else after(places[layer], message), total, side, sizes,
        )
        grad = grad_one
        if layer > 0:
            sums = (after(sums[0], *block_parts),) + sums[1:]
        spread = jnp.concatenate([jnp.zeros_like(sums_one[:2]), sums_one, sums_two], axis=0)
        vector_sums[layer] = lax.dynamic_update_slice(spread, qv_sums, (0, index * width))
        bias_sums[layer] = lax.dynamic_update_slice(
            jnp.zeros((1, 4 * hidden), f32), bias_sum, (0, index * hidden)
        ).reshape(4 * hidden // model, model)
        small = None
        if layer == 0:
            small = jnp.stack([jnp.concatenate(pair, axis=0) for pair in zip(vector_sums, bias_sums)])
            small = sum_tensor(small)
        parts, small, crossed = reduce_blocks(block_parts, small)
        waiting.append((parts, layer))
    input_grad = from_tokens(
        grad + sums[0][:quarter] + sums[1][:quarter].astype(f32) + sums[2].astype(f32), crossed
    )
    layer_out = from_tokens(stream, crossed)
    for parts, layer in waiting:
        if layer > 0 and paired:
            state = (after(masters, crossed[1]),) + state[1:]
        updated = update_step(parts, layer, state, updated)
        state = (masters,) + state[1:]

    vector_grads = lax.dynamic_slice(small[:, :8], (0, 0, index * width), (layers, 8, width))
    up_bias_grads = lax.dynamic_slice(
        small[:, 8:].reshape(layers, 4 * hidden), (0, index * hidden), (layers, hidden)
    )
    reduced, left_new, right_new, new_weights = updated
    vector_rate = 0.5 / math.sqrt(tokens * lax.axis_size("dp"))
    return (
        layer_out,
        input_grad,
        reduced,
        left_new,
        right_new,
        new_weights,
        vector_grads,
        vectors - vector_rate * vector_grads,
        up_bias_grads,
        up_bias - vector_rate * up_bias_grads,
    )


def solution(mesh):
    owned = P(None, ("dp", "tensor"), None, None)
    return jax.shard_map(
        body,
        mesh=mesh,
        in_specs=(
            P("dp", "tensor"),
            P("dp", "tensor"),
            P("dp", None),
            P(),
            owned,
            owned,
            owned,
            owned,
            owned,
            P(None, None, "tensor"),
            P(None, "tensor"),
        ),
        out_specs=(
            P("dp", "tensor"),
            P("dp", "tensor"),
            owned,
            owned,
            owned,
            owned,
            P(None, None, "tensor"),
            P(None, None, "tensor"),
            P(None, "tensor"),
            P(None, "tensor"),
        ),
        check_vma=False,
    )
```

```python
import functools
import math

import jax
import jax.numpy as jnp
from jax import lax
from jax.experimental import pallas as pl
from jax.experimental.pallas import tpu as pltpu
from jax.sharding import PartitionSpec as P

HD = 64
eps_norm = 1e-12
stat_decay = 0.5
update_rate = 0.5
f32 = jnp.float32
bf16 = jnp.bfloat16

LAST = (((1,), (1,)), ((), ()))
FIRST = (((0,), (0,)), ((), ()))


def vmem_spec(count):
    return [pl.BlockSpec(memory_space=pltpu.VMEM)] * count


def params(mib=40):
    return pltpu.CompilerParams(vmem_limit_bytes=mib * 1024 * 1024)


def cost(microseconds):
    return pl.CostEstimate(flops=0, bytes_accessed=int(microseconds * 3.4e6), transcendentals=0)


def shape(dims, dtype):
    return jax.ShapeDtypeStruct(dims, dtype)


def cat_rows(refs):
    return jnp.concatenate([ref[...] for ref in refs], axis=0)


def matrix(ref, rows, cols):
    width = ref.shape[1]
    return jnp.concatenate(
        [
            jnp.concatenate(
                [ref[(r * cols + c) // width, (r * cols + c) % width] for c in range(cols)], axis=1
            )
            for r in range(rows)
        ],
        axis=0,
    )


def flat_matrix(ref, base, rows, cols):
    return jnp.concatenate(
        [jnp.concatenate([ref[base + r * cols + c] for c in range(cols)], axis=1) for r in range(rows)], axis=0
    )


def swap(values, axis, flip):
    count = lax.axis_size(axis)
    return lax.ppermute(values, axis, [(i, i ^ flip) for i in range(count)])


def gather_tokens(piece):
    far = swap(piece, "tensor", 2)
    near = swap(piece, "tensor", 1)
    both = swap(far, "tensor", 1)
    return (piece, far, near, both)


def scatter_sum(send, keep):
    rows = send.shape[0] // 2
    first = swap(send, "tensor", 1)
    message = (keep[rows:] + first[rows:].astype(f32)).astype(bf16)
    return (keep, first, swap(message, "tensor", 2)), message


def by_index(relative):
    index = lax.axis_index("tensor")
    core, x_pos = index % 2 == 1, index // 2 == 1
    r0, r1, r2, r3 = relative
    a0, a1 = jnp.where(core, r1, r0), jnp.where(core, r0, r1)
    a2, a3 = jnp.where(core, r3, r2), jnp.where(core, r2, r3)
    return [
        jnp.where(x_pos, a2, a0),
        jnp.where(x_pos, a3, a1),
        jnp.where(x_pos, a0, a2),
        jnp.where(x_pos, a1, a3),
    ]


def to_tokens(values):
    rows, width = values.shape
    quarter = rows // 4
    r0, r1, r2, r3 = by_index([values[g * quarter : (g + 1) * quarter] for g in range(4)])
    got = swap(jnp.stack([r2, r3]), "tensor", 2)
    near = swap(jnp.stack([r1, got[1]]), "tensor", 1)
    return jnp.concatenate(by_index([r0, near[0], got[0], near[1]]), axis=1)


def from_tokens(values, marks=None):
    width = values.shape[1] // 4
    r0, r1, r2, r3 = by_index([values[:, g * width : (g + 1) * width] for g in range(4)])
    near = jnp.stack([r1, r3])
    got = swap(near if marks is None else after(near, marks[0]), "tensor", 1)
    rest = jnp.stack([r2, got[1]])
    far = swap(rest if marks is None else after(rest, marks[1]), "tensor", 2)
    return jnp.concatenate(by_index([r0, got[0], far[0], far[1]]), axis=0)


ring = (0, 2, 4, 6, 7, 5, 3, 1)


def ring_place():
    index = lax.axis_index("dp")
    return jnp.where(index % 2 == 0, index // 2, 7 - index // 2)


def owner_place(owner):
    return jnp.where(owner % 2 == 0, owner // 2, 7 - owner // 2)


def turn(values, way):
    return lax.ppermute(values, "dp", [(ring[p], ring[(p + way) % 8]) for p in range(8)])


def after(values, *others):
    return lax.optimization_barrier((values,) + tuple(others))[0]


def has_ring():
    return lax.axis_size("dp") == 8


def weight_sources(own, owner_map, meanwhile):
    layers, total = owner_map.shape
    slots = own[0].shape[0]
    half = slots // 2
    positions = jnp.arange(total, dtype=jnp.int32)
    hits = owner_map[:, None, :] == positions[None, :, None]
    inverse = jnp.sum(jnp.where(hits, positions[None, None, :], 0), axis=2).astype(jnp.int32)
    if not has_ring():
        wholes = [lax.all_gather(values.astype(bf16), "dp", axis=0, tiled=True) for values in own]
        for stage in range(3):
            meanwhile(stage, None)
        return [((whole,), ((0, 0),), row[None, :]) for whole, row in zip(wholes, inverse)], None
    ways = jnp.array([0, -1, -2, -3, 1, 2, 3, 4], jnp.int32)
    spots = tuple((j, first) for j in range(7) for first in (0, half)) + ((7, 0), (8, 0))
    target = (ring_place() + ways) % 8
    device = jnp.where(target < 4, 2 * target, 15 - 2 * target)
    mask = device[None, :, None, None] == jnp.arange(8, dtype=jnp.int32)[None, None, :, None]
    rows = jnp.sum(jnp.where(mask, inverse.reshape(layers, 1, 8, slots), 0), axis=2)
    tables = [table for table in rows.reshape(layers, 16, half).astype(jnp.int32)]
    result, points, last, beside = [], [], (), ()
    for layer in range(layers):
        mine = own[layer] if layer == 0 else after(own[layer], points[0])
        mine = mine.astype(bf16)
        start = after(mine, *last) if last else mine
        behind, ahead = [turn(start, 1)], [turn(start, -1)]
        for step in range(3):
            if layer == 0:
                beside += meanwhile(step, behind[-2] if step else None)
            done = (behind[-1], ahead[-1]) + (beside[-1] if layer == 0 else ())
            points.append(behind[-1])
            points.append(ahead[-1])
            next_behind, next_ahead = after(behind[-1], *done), after(ahead[-1], *done)
            if step == 2:
                next_behind, next_ahead = next_behind[:half], next_ahead[half:]
            behind.append(turn(next_behind, 1))
            ahead.append(turn(next_ahead, -1))
        last = (behind[3], ahead[3])
        points += last
        result.append(((mine, *behind[:3], *ahead[:3], behind[3], ahead[3]), spots, tables[layer]))
    return result, points


def send_positions(owner_row, slots):
    if not has_ring():
        return owner_row
    way = (owner_place(owner_row // slots) - ring_place()) % 8
    return (way * slots + owner_row % slots).astype(jnp.int32)


def reduce_start(grads, slots):
    half = slots // 2
    return turn(grads[4 * slots : 4 * slots + half], 1), turn(grads[4 * slots + half : 5 * slots], -1)


def reduce_next(grads, slots, step, came, *marks):
    forward = grads[(5 - step) * slots : (6 - step) * slots].astype(f32)
    backward = grads[(3 + step) * slots : (4 + step) * slots].astype(f32)
    ahead, behind = came[0].astype(f32), came[1].astype(f32)
    if step == 2:
        half = slots // 2
        forward = jnp.concatenate([forward[:half] + ahead, forward[half:]])
        backward = jnp.concatenate([backward[:half], backward[half:] + behind])
    else:
        forward, backward = forward + ahead, backward + behind
    forward, backward = lax.optimization_barrier((forward.astype(bf16), backward.astype(bf16), *marks))[:2]
    return turn(forward, 1), turn(backward, -1)


def norm_kernel(base, keep, first, second, vec, low_out, full_out, normed_out, scale_out, *, rows):
    bias, gain, shift = rows
    hidden = (
        base[...]
        + keep[...]
        + first[...].astype(f32)
        + second[...].astype(f32)
        + vec[bias : bias + 1, :]
    )
    center = jnp.mean(hidden, axis=1, keepdims=True)
    centred = hidden - center
    spread = jnp.mean(centred * centred, axis=1, keepdims=True)
    scale = lax.rsqrt(spread + eps_norm)
    normed = centred * scale
    full = normed * vec[gain : gain + 1, :] + vec[shift : shift + 1, :]
    full_out[...] = full
    low_out[...] = full.astype(bf16)
    normed_out[...] = normed
    scale_out[...] = scale


def top_half(array):
    return pl.BlockSpec((array.shape[0] // 2, array.shape[1]), lambda i: (0, 0))


def whole_spec(array):
    nd = len(array.shape)
    return pl.BlockSpec(tuple(array.shape), lambda i, nd=nd: (0,) * nd)


def norm_step(base, sums, vec, rows):
    keep, first, second = sums
    tokens, width = base.shape
    outs = [
        shape((tokens, width), bf16),
        shape((tokens, width), f32),
        shape((tokens, width), f32),
        shape((tokens, 1), f32),
    ]
    return pl.pallas_call(
        functools.partial(norm_kernel, rows=rows),
        grid=(1,),
        in_specs=[whole_spec(base), top_half(keep), top_half(first), whole_spec(second), whole_spec(vec)],
        out_specs=[whole_spec(o) for o in outs],
        out_shape=outs,
        compiler_params=params(12),
        cost_estimate=cost(1.2),
        name="norm",
    )(base, keep, first, second, vec)


def norm_back_kernel(*refs, gain, summed):
    if summed:
        base, keep, first, second, normed, scale, vec, low_out, full_out, sums_out = refs
        grad = base[...] + keep[...] + first[...].astype(f32) + second[...].astype(f32)
    else:
        base, normed, scale, vec, low_out, full_out, sums_out = refs
        grad = base[...]
    value = normed[...]
    scaled = grad * vec[gain : gain + 1, :]
    mean_grad = jnp.mean(scaled, axis=1, keepdims=True)
    mean_cross = jnp.mean(scaled * value, axis=1, keepdims=True)
    result = scale[...] * (scaled - mean_grad - value * mean_cross)
    full_out[...] = result
    low_out[...] = result.astype(bf16)
    sums_out[0:1, :] = jnp.sum(result, axis=0, keepdims=True)
    sums_out[1:2, :] = jnp.sum(grad * value, axis=0, keepdims=True)
    sums_out[2:3, :] = jnp.sum(grad, axis=0, keepdims=True)


def norm_back_step(base, sums, normed, scale, vec, gain):
    tokens, width = base.shape
    outs = [shape((tokens, width), bf16), shape((tokens, width), f32), shape((3, width), f32)]
    operands = [base]
    specs = [whole_spec(base)]
    if sums is not None:
        keep, first, second = sums
        operands += [keep, first, second]
        specs += [top_half(keep), top_half(first), whole_spec(second)]
    operands += [normed, scale, vec]
    specs += [whole_spec(normed), whole_spec(scale), whole_spec(vec)]
    return pl.pallas_call(
        functools.partial(norm_back_kernel, gain=gain, summed=sums is not None),
        grid=(1,),
        in_specs=specs,
        out_specs=[whole_spec(o) for o in outs],
        out_shape=outs,
        compiler_params=params(12),
        cost_estimate=cost(1.5),
        name="norm_back",
    )(*operands)


def store_sums(total, send_out, keep_out):
    half = total.shape[0] // 2
    send_out[...] = total[half:].astype(bf16)
    keep_out[...] = total[:half]


def start_blocks(sources, spots, table, stage, sem):
    slots = table.shape[1]
    for row, (which, first) in enumerate(spots):

        @pl.loop(0, slots, unroll=min(slots, 24))
        def _(s, row=row, which=which, first=first):
            pltpu.make_async_copy(sources[which].at[first + s], stage.at[table[row, s]], sem).start()


def attend_kernel(
    count, spots, n_qkv, n_out, table, *refs
):
    sources = refs[:count]
    (
        p0, p1, p2, p3, vec, seg_col, seg_row,
        query_out, key_out, value_out, mix_out, log_out, send_out, keep_out, attend_out, ffn_out,
        bias, stage, sems,
    ) = refs[count:]
    start_blocks(sources, spots, table, stage, sems.at[0])
    wide = cat_rows((p0, p1, p2, p3))
    bias[...] = jnp.where(seg_col[...] == seg_row[...], 0.0, -1e30)
    pltpu.make_async_copy(stage, stage, sems.at[0]).wait()
    cut = n_qkv + n_out
    copies = (
        pltpu.make_async_copy(stage.at[pl.ds(0, cut)], attend_out, sems.at[1]),
        pltpu.make_async_copy(stage.at[pl.ds(cut, ffn_out.shape[0])], ffn_out, sems.at[2]),
    )
    for copy in copies:
        copy.start()
    tokens, model = wide.shape
    width = query_out.shape[1]
    tile = stage.shape[-1]
    projected = jnp.dot(
        wide, flat_matrix(stage, 0, model // tile, 3 * width // tile), preferred_element_type=f32
    )
    query = (projected[:, :width] + vec[0:1, :]).astype(bf16) * jnp.asarray(HD**-0.5, bf16)
    keys = projected[:, width : 2 * width].astype(bf16)
    values = (projected[:, 2 * width :] + vec[1:2, :]).astype(bf16)
    query_out[...] = query
    key_out[...] = keys
    value_out[...] = values
    lane = lax.broadcasted_iota(jnp.int32, (tokens, 128), 1)
    logs = jnp.zeros((tokens, 128), f32)
    mixes = []
    for pair in range(width // 128):
        cols = slice(pair * 128, pair * 128 + 128)
        halves = []
        for part in range(128 // HD):
            inside = (lane >= part * HD) & (lane < part * HD + HD)
            one = jnp.where(inside, query[:, cols], jnp.zeros((), bf16))
            scores = lax.dot_general(one, keys[:, cols], LAST, preferred_element_type=f32) + bias[...]
            top = jnp.max(scores, axis=1, keepdims=True)
            exponent = jnp.exp(scores - top)
            total = jnp.sum(exponent, axis=1, keepdims=True)
            attention = (exponent * (1.0 / total)).astype(bf16)
            halves.append((inside, jnp.dot(attention, values[:, cols], preferred_element_type=f32)))
            logs = jnp.where(lane == pair * (128 // HD) + part, top + jnp.log(total), logs)
        mixed = halves[0][1]
        for inside, other in halves[1:]:
            mixed = jnp.where(inside, other, mixed)
        mixes.append(mixed.astype(bf16))
    mixture = jnp.concatenate(mixes, axis=1)
    mix_out[...] = mixture
    log_out[...] = jnp.transpose(logs)[0:8, :]
    total = jnp.dot(
        mixture, flat_matrix(stage, n_qkv, width // tile, model // tile), preferred_element_type=f32
    )
    store_sums(total, send_out, keep_out)
    for copy in copies:
        copy.wait()


def block_rows(array, start, count):
    return pl.BlockSpec((count,) + tuple(array.shape[1:]), lambda i: (start // count, 0, 0, 0))


def attend_step(pieces, weights, counts, vec, seg_col, seg_row):
    quarter, model = pieces[0].shape
    tokens, width = 4 * quarter, vec.shape[1]
    n_qkv, n_out, n_up = counts
    arrays, spots, table = weights
    side = arrays[0].shape[-1]
    total = n_qkv + n_out + 2 * n_up
    outs = [
        shape((tokens, width), bf16),
        shape((tokens, width), bf16),
        shape((tokens, width), bf16),
        shape((tokens, width), bf16),
        shape((8, tokens), f32),
        shape((tokens // 2, model), bf16),
        shape((tokens // 2, model), f32),
        shape((n_qkv + n_out, side, side), bf16),
        shape((2 * n_up, side, side), bf16),
    ]
    operands = list(pieces) + [vec, seg_col, seg_row]
    return pl.pallas_call(
        functools.partial(attend_kernel, len(arrays), spots, n_qkv, n_out),
        grid_spec=pltpu.PrefetchScalarGridSpec(
            num_scalar_prefetch=1,
            grid=(),
            in_specs=[pl.BlockSpec(memory_space=pl.ANY)] * len(arrays) + vmem_spec(len(operands)),
            out_specs=vmem_spec(7) + [pl.BlockSpec(memory_space=pl.ANY)] * 2,
            scratch_shapes=[
                pltpu.VMEM((tokens, tokens), f32),
                pltpu.VMEM((total, side, side), bf16),
                pltpu.SemaphoreType.DMA((3,)),
            ],
        ),
        out_shape=outs,
        compiler_params=params(60),
        cost_estimate=cost(11),
        name="attend",
    )(table, *arrays, *operands)


def attend_back_kernel(
    p0, p1, p2, p3, w_out, w_qkv, query_in, key_in, value_in, log_in, seg_col, seg_row,
    grad_out, sums_out, send_out, keep_out, bias,
):
    wide = cat_rows((p0, p1, p2, p3))
    tokens, model = wide.shape
    width = query_in.shape[1]
    tile = w_qkv.shape[-1]
    grad_mix = lax.dot_general(
        wide, matrix(w_out, width // tile, model // tile), LAST, preferred_element_type=f32
    ).astype(bf16)
    bias[...] = jnp.where(seg_col[...] == seg_row[...], 0.0, -1e30)
    lane = lax.broadcasted_iota(jnp.int32, (tokens, 128), 1)
    grads = ([], [], [])
    for pair in range(width // 128):
        cols = slice(pair * 128, pair * 128 + 128)
        query, keys, values, mix = query_in[:, cols], key_in[:, cols], value_in[:, cols], grad_mix[:, cols]
        picked = [None, None, None]
        for part in range(128 // HD):
            head = pair * (128 // HD) + part
            inside = (lane >= part * HD) & (lane < part * HD + HD)
            zero = jnp.zeros((), bf16)
            scores = (
                lax.dot_general(jnp.where(inside, keys, zero), query, LAST, preferred_element_type=f32)
                + bias[...]
            )
            attention = jnp.exp(scores - log_in[head : head + 1, :])
            pulled = lax.dot_general(jnp.where(inside, values, zero), mix, LAST, preferred_element_type=f32)
            inner = jnp.sum(attention * pulled, axis=0, keepdims=True)
            grad_scores = (attention * (pulled - inner)).astype(bf16)
            three = (
                lax.dot_general(grad_scores, keys, FIRST, preferred_element_type=f32) * (HD**-0.5),
                jnp.dot(grad_scores, query, preferred_element_type=f32),
                jnp.dot(attention.astype(bf16), mix, preferred_element_type=f32),
            )
            for which in range(3):
                if part == 0:
                    picked[which] = three[which]
                else:
                    picked[which] = jnp.where(inside, three[which], picked[which])
        for which in range(3):
            grads[which].append(picked[which].astype(bf16))
    joined = [jnp.concatenate(g, axis=1) for g in grads]
    every = jnp.concatenate(joined, axis=1)
    grad_out[...] = every
    sums_out[0:1, :] = jnp.sum(joined[0].astype(f32), axis=0, keepdims=True)
    sums_out[1:2, :] = jnp.sum(joined[2].astype(f32), axis=0, keepdims=True)
    total = lax.dot_general(
        every, matrix(w_qkv, model // tile, 3 * width // tile), LAST, preferred_element_type=f32
    )
    store_sums(total, send_out, keep_out)


def attend_back_step(pieces, blocks, counts, query, keys, values, logs, seg_col, seg_row):
    quarter, model = pieces[0].shape
    tokens, width = query.shape
    n_qkv, n_out, n_up = counts
    per = blocks.shape[1]
    outs = [
        shape((tokens, 3 * width), bf16),
        shape((2, width), f32),
        shape((tokens // 2, model), bf16),
        shape((tokens // 2, model), f32),
    ]
    return pl.pallas_call(
        attend_back_kernel,
        grid=(1,),
        in_specs=[whole_spec(p) for p in pieces]
        + [block_rows(blocks, n_qkv // per, n_out // per), block_rows(blocks, 0, n_qkv // per)]
        + [whole_spec(a) for a in (query, keys, values, logs, seg_col, seg_row)],
        out_specs=[whole_spec(o) for o in outs],
        out_shape=outs,
        scratch_shapes=[pltpu.VMEM((tokens, tokens), f32)],
        compiler_params=params(),
        cost_estimate=cost(6.5),
        name="attend_back",
    )(*pieces, blocks, blocks, query, keys, values, logs, seg_col, seg_row)


def ffn_kernel(p0, p1, p2, p3, w_up, w_down, bias, act_out, slope_out, send_out, keep_out, total):
    step = pl.program_id(0)
    wide = cat_rows((p0, p1, p2, p3))
    model = wide.shape[1]
    tile = w_up.shape[-1]
    cols = act_out.shape[1] // tile
    pre = jnp.dot(wide, matrix(w_up, model // tile, cols), preferred_element_type=f32) + bias[...]
    cdf = 0.5 + 0.5 * lax.erf(pre * (0.5**0.5))
    slope_out[...] = cdf + pre * (jnp.exp(-0.5 * pre * pre) * (1.0 / math.sqrt(2.0 * math.pi)))
    activated = (pre * cdf).astype(bf16)
    act_out[...] = activated
    part = jnp.dot(activated, matrix(w_down, cols, model // tile), preferred_element_type=f32)

    @pl.when(step == 0)
    def _():
        total[...] = part

    @pl.when(step > 0)
    def _():
        total[...] += part

    @pl.when(step == pl.num_programs(0) - 1)
    def _():
        store_sums(total[...], send_out, keep_out)


def fixed(array):
    nd = len(array.shape)
    return pl.BlockSpec(tuple(array.shape), lambda i, nd=nd: (0,) * nd)


def ffn_specs(blocks, counts, chunk_blocks):
    n_qkv, n_out, n_up = counts
    per = blocks.shape[1]
    side = blocks.shape[2]
    up_row = 0
    up_rows = n_up // per
    down_row = n_up // per
    up_spec = pl.BlockSpec((up_rows, chunk_blocks, side, side), lambda i: (up_row // up_rows, i, 0, 0))
    down_spec = pl.BlockSpec((chunk_blocks, per, side, side), lambda i: (down_row // chunk_blocks + i, 0, 0, 0))
    return up_spec, down_spec


def ffn_step(pieces, blocks, counts, up_bias, steps=4):
    quarter, model = pieces[0].shape
    tokens, hidden = 4 * quarter, up_bias.shape[1]
    chunk = hidden // steps
    up_spec, down_spec = ffn_specs(blocks, counts, chunk // blocks.shape[2])
    outs = [
        shape((tokens, hidden), bf16),
        shape((tokens, hidden), f32),
        shape((tokens // 2, model), bf16),
        shape((tokens // 2, model), f32),
    ]
    by_cols = pl.BlockSpec((tokens, chunk), lambda i: (0, i))
    return pl.pallas_call(
        ffn_kernel,
        grid=(steps,),
        in_specs=[fixed(p) for p in pieces]
        + [up_spec, down_spec, pl.BlockSpec((1, chunk), lambda i: (0, i))],
        out_specs=[by_cols, by_cols, fixed(outs[2]), fixed(outs[3])],
        out_shape=outs,
        scratch_shapes=[pltpu.VMEM((tokens, model), f32)],
        compiler_params=params(),
        cost_estimate=cost(7.5),
        name="ffn",
    )(*pieces, blocks, blocks, up_bias)


def ffn_back_kernel(p0, p1, p2, p3, w_up, w_down, slope, grad_out, bias_out, send_out, keep_out, total):
    step = pl.program_id(0)
    wide = cat_rows((p0, p1, p2, p3))
    model = wide.shape[1]
    tile = w_up.shape[-1]
    cols = grad_out.shape[1] // tile
    pulled = lax.dot_general(wide, matrix(w_down, cols, model // tile), LAST, preferred_element_type=f32)
    grad = (pulled * slope[...]).astype(bf16)
    grad_out[...] = grad
    bias_out[...] = jnp.sum(grad.astype(f32), axis=0, keepdims=True)
    part = lax.dot_general(grad, matrix(w_up, model // tile, cols), LAST, preferred_element_type=f32)

    @pl.when(step == 0)
    def _():
        total[...] = part

    @pl.when(step > 0)
    def _():
        total[...] += part

    @pl.when(step == pl.num_programs(0) - 1)
    def _():
        store_sums(total[...], send_out, keep_out)


def ffn_back_step(pieces, blocks, counts, slope, steps=4):
    quarter, model = pieces[0].shape
    tokens, hidden = slope.shape
    chunk = hidden // steps
    up_spec, down_spec = ffn_specs(blocks, counts, chunk // blocks.shape[2])
    outs = [
        shape((tokens, hidden), bf16),
        shape((1, hidden), f32),
        shape((tokens // 2, model), bf16),
        shape((tokens // 2, model), f32),
    ]
    by_cols = pl.BlockSpec((tokens, chunk), lambda i: (0, i))
    return pl.pallas_call(
        ffn_back_kernel,
        grid=(steps,),
        in_specs=[fixed(p) for p in pieces] + [up_spec, down_spec, by_cols],
        out_specs=[by_cols, pl.BlockSpec((1, chunk), lambda i: (0, i)), fixed(outs[2]), fixed(outs[3])],
        out_shape=outs,
        scratch_shapes=[pltpu.VMEM((tokens, model), f32)],
        compiler_params=params(),
        cost_estimate=cost(7),
        name="ffn_back",
    )(*pieces, blocks, blocks, slope)


def weight_grad_jobs(jobs, operands, side, store):
    at = 0
    for left_count, right_count, base in jobs:
        left = operands[at : at + left_count]
        right = operands[at + left_count : at + left_count + right_count]
        at += left_count + right_count
        columns = cat_rows(right)
        per = columns.shape[1] // side
        width = left[0].shape[1]
        chunk = min(width, 2 * side)
        for start in range(0, width, chunk):
            rows = jnp.concatenate([ref[:, start : start + chunk] for ref in left], axis=0)
            result = lax.dot_general(rows, columns, FIRST, preferred_element_type=f32).astype(bf16)
            for i in range(chunk // side):
                for j in range(per):
                    store(
                        base + (start // side + i) * per + j,
                        result[i * side : (i + 1) * side, j * side : (j + 1) * side],
                    )


def job_parts(jobs, side):
    operands = [a for left, right, base in jobs for a in left + right]
    layout = tuple((len(left), len(right), base) for left, right, base in jobs)
    blocks = sum(left[0].shape[1] // side * (right[0].shape[1] // side) for left, right, base in jobs)
    tokens = sum(a.shape[0] for a in jobs[0][0])
    return operands, layout, blocks, tokens


def block_grad_kernel(jobs, used, chained, place, *refs):
    out, stage, sem = refs[used + chained :]
    slots = []

    def store(block, value):
        slot = len(slots)
        slots.append(block)
        stage[slot] = value
        pltpu.make_async_copy(stage.at[slot], out.at[place[block]], sem).start()

    weight_grad_jobs(jobs, refs[:used], stage.shape[-1], store)
    pltpu.make_async_copy(stage, out.at[pl.ds(0, stage.shape[0])], sem).wait()


def block_grad_step(jobs, place, total, side, target=None):
    operands, layout, blocks, tokens = job_parts(jobs, side)
    chained = [] if target is None else [target]
    return pl.pallas_call(
        functools.partial(block_grad_kernel, layout, len(operands), len(chained)),
        grid_spec=pltpu.PrefetchScalarGridSpec(
            num_scalar_prefetch=1,
            grid=(),
            in_specs=vmem_spec(len(operands)) + [pl.BlockSpec(memory_space=pl.ANY)] * len(chained),
            out_specs=pl.BlockSpec(memory_space=pl.ANY),
            scratch_shapes=[pltpu.VMEM((blocks, side, side), bf16), pltpu.SemaphoreType.DMA],
        ),
        out_shape=shape((total, side, side), bf16),
        input_output_aliases={1 + len(operands): 0} if chained else {},
        compiler_params=params(60),
        cost_estimate=cost(4 if chained else 6),
        name="block_grad",
    )(place, *operands, *chained)


def update_kernel(part_count, chained, *refs):
    parts = refs[:part_count]
    masters, left, right, left_root, right_root = refs[part_count : part_count + 5]
    grad_out, left_out, right_out, weight_out = refs[part_count + 5 + chained :]
    grad = parts[0][...].astype(f32)
    for part in parts[1:]:
        grad = grad + part[...].astype(f32)
    grad_out[0] = grad
    for b in range(grad.shape[0]):
        low = grad[b].astype(bf16)
        left_out[0, b] = stat_decay * left[0, b] + (1.0 - stat_decay) * lax.dot_general(
            low, low, LAST, preferred_element_type=f32
        )
        right_out[0, b] = stat_decay * right[0, b] + (1.0 - stat_decay) * lax.dot_general(
            low, low, FIRST, preferred_element_type=f32
        )
        inner = jnp.dot(low, right_root[0, b].astype(bf16), preferred_element_type=f32)
        outer = jnp.dot(left_root[0, b].astype(bf16), inner.astype(bf16), preferred_element_type=f32)
        weight_out[0, b] = masters[0, b] - update_rate * outer


def update_step(parts, layer, state, previous):
    layers, slots, side, _ = state[0].shape
    group = 4 if slots % 4 == 0 else slots
    one = pl.BlockSpec((1, group, side, side), lambda i: (layer, i, 0, 0))
    chained = [] if previous is None else list(previous)
    aliases = {len(parts) + 5 + k: k for k in range(len(chained))}
    return pl.pallas_call(
        functools.partial(update_kernel, len(parts), len(chained)),
        grid=(slots // group,),
        in_specs=[pl.BlockSpec((group, side, side), lambda i: (i, 0, 0))] * len(parts)
        + [one] * 5
        + [pl.BlockSpec(memory_space=pl.ANY)] * len(chained),
        out_specs=[one] * 4,
        out_shape=[shape(state[0].shape, f32)] * 4,
        input_output_aliases=aliases,
        compiler_params=params(60),
        cost_estimate=cost(10),
        name="update",
    )(*parts, *state, *chained)


def body(
    layer_in,
    cotangent,
    segment_ids,
    owner_map,
    masters,
    left_stats,
    right_stats,
    left_roots,
    right_roots,
    vectors,
    up_bias,
):
    layers, slots, side = masters.shape[0], masters.shape[1], masters.shape[-1]
    tokens, width = layer_in.shape
    model = width * lax.axis_size("tensor")
    hidden = up_bias.shape[1]
    tile_rows = model // side
    n_qkv = tile_rows * (3 * width // side)
    n_out = width // side * tile_rows
    n_up = tile_rows * (hidden // side)
    counts = (n_qkv, n_out, n_up)
    total = owner_map.shape[1]
    index = lax.axis_index("tensor")
    quarter = tokens // 4

    segments = jnp.concatenate(
        by_index([segment_ids[:, g * quarter : (g + 1) * quarter] for g in range(4)]), axis=1
    )
    segments = jnp.concatenate(
        [segments[:, g * quarter : (g + 1) * quarter] for g in (0, 2, 1, 3)], axis=1
    )
    seg_col, seg_row = segments.reshape(tokens, 1), segments

    made = {}

    def meanwhile(stage, mark):
        def hold(values):
            return values if mark is None else after(values, mark)

        if stage == 0:
            near = swap(vectors, "tensor", 1)
            far = swap(jnp.stack([vectors, near]), "tensor", 2)
            made["vectors"] = jnp.concatenate(by_index([vectors, near, far[0], far[1]]), axis=2)
            made["stream"] = to_tokens(layer_in)
            made["places"] = tuple(send_positions(owner_map, slots))
            part = (made["vectors"], made["stream"]) + made["places"]
        elif stage == 1:
            made["wide"] = gather_tokens(hold(made["stream"]).astype(bf16))
            part = made["wide"] + (seg_col,)
        else:
            made["grad"] = to_tokens(hold(cotangent))
            part = (made["grad"],)
        return (part,)

    own = [masters[layer] for layer in range(layers)]
    sources, points = weight_sources(own, owner_map, meanwhile)
    paired = points is not None
    wide_vectors, stream, wide_in, grad, places = (
        made[name] for name in ("vectors", "stream", "wide", "grad", "places")
    )
    weights = []

    kept = []
    for layer in range(layers):
        vec = wide_vectors[layer]
        if layer > 0:
            wide_in = gather_tokens(stream_low)
            if paired:
                wide_in = wide_in[:1] + (after(wide_in[1], *points[12:14]),) + wide_in[2:]
        query, keys, values, mixture, logs, send, keep, attend_blocks, ffn_blocks = attend_step(
            wide_in, sources[layer], counts, vectors[layer], seg_col, seg_row
        )
        attend_blocks = attend_blocks.reshape(-1, tile_rows, side, side)
        ffn_blocks = ffn_blocks.reshape(-1, tile_rows, side, side)
        weights.append((attend_blocks, ffn_blocks))
        sums, message = scatter_sum(send, keep)
        if layer == 0 and paired:
            sums = (after(sums[0], *points[8:10]),) + sums[1:]
        mid_low, middle, normed_one, scale_one = norm_step(stream, sums, vec, (2, 3, 4))
        wide_mid = gather_tokens(mid_low)
        activated, slope, send, keep = ffn_step(wide_mid, ffn_blocks, counts, up_bias[layer : layer + 1])
        if layer == 0 and paired:
            send = after(send, *points[10:12])
        sums, message = scatter_sum(send, keep)
        stream_low, stream, normed_two, scale_two = norm_step(middle, sums, vec, (5, 6, 7))
        kept.append(
            (wide_in, query, keys, values, mixture, logs, normed_one, scale_one, wide_mid, activated, slope, normed_two, scale_two)
        )

    vector_sums = [None] * layers
    bias_sums = [None] * layers
    sums = None
    above, came = None, ()
    for layer in reversed(range(layers)):
        vec, (attend_blocks, ffn_blocks) = wide_vectors[layer], weights[layer]
        (wide_in, query, keys, values, mixture, logs, normed_one, scale_one, wide_mid, activated, slope, normed_two, scale_two) = kept[layer]
        first = layer == 0 and paired
        grad_low, grad_two, sums_two = norm_back_step(grad, sums, normed_two, scale_two, vec, 6)
        wide_grad = gather_tokens(grad_low)
        if first:
            wide_grad = wide_grad[:1] + (after(wide_grad[1], *came),) + wide_grad[2:]
            came = reduce_next(above, slots, 2, came)
        grad_pre, bias_sum, send, keep = ffn_back_step(wide_grad, ffn_blocks, counts, slope)
        sums, message = scatter_sum(send, keep)
        ffn_jobs = [(wide_mid, (grad_pre,), n_qkv + n_out), ((activated,), wide_grad, n_qkv + n_out + n_up)]
        if first:
            sums = (after(sums[0], *came),) + sums[1:]
            came = reduce_next(above, slots, 3, came)
        else:
            ffn_grads = block_grad_step(ffn_jobs, after(places[layer], message), total, side)
            sums = (after(sums[0], ffn_grads),) + sums[1:]
        grad_low, grad_one, sums_one = norm_back_step(grad_two, sums, normed_one, scale_one, vec, 3)
        wide_first = gather_tokens(grad_low)
        if first:
            ffn_grads = block_grad_step(ffn_jobs, after(places[layer], grad_low), total, side)
            wide_first = wide_first[:1] + (after(wide_first[1], ffn_grads, *came),) + wide_first[2:]
            came = reduce_next(above, slots, 4, came)
        grad_qkv, qv_sums, send, keep = attend_back_step(
            wide_first, attend_blocks, counts, query, keys, values, logs, seg_col, seg_row
        )
        sums, message = scatter_sum(send, keep)
        block_grads = block_grad_step(
            [(wide_in, (grad_qkv,), 0), ((mixture,), wide_first, n_qkv)],
            places[layer] if first else after(places[layer], message), total, side, ffn_grads,
        )
        grad = grad_one
        spread = jnp.concatenate([jnp.zeros_like(sums_one[:2]), sums_one, sums_two], axis=0)
        vector_sums[layer] = lax.dynamic_update_slice(spread, qv_sums, (0, index * width))
        bias_sums[layer] = lax.dynamic_update_slice(
            jnp.zeros((1, 4 * hidden), f32), bias_sum, (0, index * hidden)
        ).reshape(4 * hidden // model, model)
        if layer > 0:
            sums = (after(sums[0], block_grads),) + sums[1:]
            above = block_grads
            if paired:
                came = reduce_start(above, slots)

    small = jnp.stack([jnp.concatenate(pair, axis=0) for pair in zip(vector_sums, bias_sums)])
    small = small + swap(small, "tensor", 1)
    small = small + swap(small, "tensor", 2)
    state = (masters, left_stats, right_stats, left_roots, right_roots)
    if paired:
        before = (above[:slots], *came)
        came = reduce_start(after(block_grads, *came), slots)
        marks = [came]
        small = small + swap(small, "dp", 2)
        marks.append(reduce_next(block_grads, slots, 2, marks[0]))
        marks.append(reduce_next(block_grads, slots, 3, marks[1], small))
        small = small + swap(after(small, *marks[0]), "dp", 4)
        came = reduce_next(block_grads, slots, 4, marks[2], small)
        small = small + swap(after(small, *marks[1]), "dp", 1)
        parts = (after(block_grads[:slots], small), *came)
        input_grad, layer_out = (
            from_tokens(values, (marks[0][0], marks[1][0]))
            for values in (grad + sums[0][:quarter] + sums[1][:quarter].astype(f32) + sums[2].astype(f32), stream)
        )
        updated = update_step(before, 1, (after(masters, *marks[1]),) + state[1:], None)
        updated = update_step(parts, 0, state, updated)
    else:
        small = lax.psum(small, "dp")
        input_grad, layer_out = (
            from_tokens(values)
            for values in (grad + sums[0][:quarter] + sums[1][:quarter].astype(f32) + sums[2].astype(f32), stream)
        )
        updated = None
        for layer, grads in ((1, above), (0, block_grads)):
            mine = lax.psum_scatter(grads, "dp", scatter_dimension=0, tiled=True)
            updated = update_step((mine,), layer, state, updated)
    vector_grads = lax.dynamic_slice(small[:, :8], (0, 0, index * width), (layers, 8, width))
    up_bias_grads = lax.dynamic_slice(
        small[:, 8:].reshape(layers, 4 * hidden), (0, index * hidden), (layers, hidden)
    )
    reduced, left_new, right_new, new_weights = updated
    vector_rate = 0.5 / math.sqrt(tokens * lax.axis_size("dp"))
    return (
        layer_out,
        input_grad,
        reduced,
        left_new,
        right_new,
        new_weights,
        vector_grads,
        vectors - vector_rate * vector_grads,
        up_bias_grads,
        up_bias - vector_rate * up_bias_grads,
    )


def solution(mesh):
    owned = P(None, ("dp", "tensor"), None, None)
    return jax.shard_map(
        body,
        mesh=mesh,
        in_specs=(
            P("dp", "tensor"),
            P("dp", "tensor"),
            P("dp", None),
            P(),
            owned,
            owned,
            owned,
            owned,
            owned,
            P(None, None, "tensor"),
            P(None, "tensor"),
        ),
        out_specs=(
            P("dp", "tensor"),
            P("dp", "tensor"),
            owned,
            owned,
            owned,
            owned,
            P(None, None, "tensor"),
            P(None, None, "tensor"),
            P(None, "tensor"),
            P(None, "tensor"),
        ),
        check_vma=False,
    )
```

```python
import functools
import math

import jax
import jax.numpy as jnp
from jax import lax
from jax.experimental import pallas as pl
from jax.experimental.pallas import tpu as pltpu
from jax.sharding import PartitionSpec as P

HD = 64
eps_norm = 1e-12
stat_decay = 0.5
update_rate = 0.5
f32 = jnp.float32
bf16 = jnp.bfloat16

LAST = (((1,), (1,)), ((), ()))
FIRST = (((0,), (0,)), ((), ()))


def vmem_spec(count):
    return [pl.BlockSpec(memory_space=pltpu.VMEM)] * count


def params(mib=40):
    return pltpu.CompilerParams(vmem_limit_bytes=mib * 1024 * 1024)


def cost(microseconds):
    return pl.CostEstimate(flops=0, bytes_accessed=int(microseconds * 3.4e6), transcendentals=0)


def shape(dims, dtype):
    return jax.ShapeDtypeStruct(dims, dtype)


def cat_rows(refs):
    return jnp.concatenate([ref[...] for ref in refs], axis=0)


def matrix(ref, rows, cols):
    width = ref.shape[1]
    return jnp.concatenate(
        [
            jnp.concatenate(
                [ref[(r * cols + c) // width, (r * cols + c) % width] for c in range(cols)], axis=1
            )
            for r in range(rows)
        ],
        axis=0,
    )


def flat_matrix(ref, base, rows, cols):
    return jnp.concatenate(
        [jnp.concatenate([ref[base + r * cols + c] for c in range(cols)], axis=1) for r in range(rows)], axis=0
    )


def swap(values, axis, flip):
    count = lax.axis_size(axis)
    return lax.ppermute(values, axis, [(i, i ^ flip) for i in range(count)])


def gather_tokens(piece):
    far = swap(piece, "tensor", 2)
    near = swap(piece, "tensor", 1)
    both = swap(far, "tensor", 1)
    return (piece, far, near, both)


def scatter_sum(send, keep, *marks):
    rows = send.shape[0] // 2
    first = swap(send, "tensor", 1)
    message = (keep[rows:] + first[rows:].astype(f32)).astype(bf16)
    if marks:
        message = after(message, *marks)
    return (keep, first, swap(message, "tensor", 2)), message


def by_index(relative):
    index = lax.axis_index("tensor")
    core, x_pos = index % 2 == 1, index // 2 == 1
    r0, r1, r2, r3 = relative
    a0, a1 = jnp.where(core, r1, r0), jnp.where(core, r0, r1)
    a2, a3 = jnp.where(core, r3, r2), jnp.where(core, r2, r3)
    return [
        jnp.where(x_pos, a2, a0),
        jnp.where(x_pos, a3, a1),
        jnp.where(x_pos, a0, a2),
        jnp.where(x_pos, a1, a3),
    ]


def to_tokens(values):
    rows, width = values.shape
    quarter = rows // 4
    r0, r1, r2, r3 = by_index([values[g * quarter : (g + 1) * quarter] for g in range(4)])
    got = swap(jnp.stack([r2, r3]), "tensor", 2)
    near = swap(jnp.stack([r1, got[1]]), "tensor", 1)
    return jnp.concatenate(by_index([r0, near[0], got[0], near[1]]), axis=1)


def from_tokens(values, marks=None):
    width = values.shape[1] // 4
    r0, r1, r2, r3 = by_index([values[:, g * width : (g + 1) * width] for g in range(4)])
    near = jnp.stack([r1, r3])
    got = swap(near if marks is None else after(near, marks[0]), "tensor", 1)
    rest = jnp.stack([r2, got[1]])
    far = swap(rest if marks is None else after(rest, marks[1]), "tensor", 2)
    return jnp.concatenate(by_index([r0, got[0], far[0], far[1]]), axis=0)


ring = (0, 2, 4, 6, 7, 5, 3, 1)


def ring_place():
    index = lax.axis_index("dp")
    return jnp.where(index % 2 == 0, index // 2, 7 - index // 2)


def owner_place(owner):
    return jnp.where(owner % 2 == 0, owner // 2, 7 - owner // 2)


def turn(values, way):
    return lax.ppermute(values, "dp", [(ring[p], ring[(p + way) % 8]) for p in range(8)])


def after(values, *others):
    return lax.optimization_barrier((values,) + tuple(others))[0]


def has_ring():
    return lax.axis_size("dp") == 8


def weight_sources(own, owner_map, meanwhile):
    layers, total = owner_map.shape
    slots = own[0].shape[0]
    half = slots // 2
    positions = jnp.arange(total, dtype=jnp.int32)
    hits = owner_map[:, None, :] == positions[None, :, None]
    inverse = jnp.sum(jnp.where(hits, positions[None, None, :], 0), axis=2).astype(jnp.int32)
    if not has_ring():
        wholes = [lax.all_gather(values.astype(bf16), "dp", axis=0, tiled=True) for values in own]
        for stage in range(3):
            meanwhile(stage, None)
        return [((whole,), ((0, 0),), row[None, :]) for whole, row in zip(wholes, inverse)], None
    ways = jnp.array([0, -1, -2, -3, 1, 2, 3, 4], jnp.int32)
    spots = tuple((j, first) for j in range(7) for first in (0, half)) + ((7, 0), (8, 0))
    target = (ring_place() + ways) % 8
    device = jnp.where(target < 4, 2 * target, 15 - 2 * target)
    mask = device[None, :, None, None] == jnp.arange(8, dtype=jnp.int32)[None, None, :, None]
    rows = jnp.sum(jnp.where(mask, inverse.reshape(layers, 1, 8, slots), 0), axis=2)
    tables = [table for table in rows.reshape(layers, 16, half).astype(jnp.int32)]
    result, points, last, beside = [], [], (), ()
    for layer in range(layers):
        mine = own[layer] if layer == 0 else after(own[layer], points[0])
        mine = mine.astype(bf16)
        start = after(mine, *last) if last else mine
        behind, ahead = [turn(start, 1)], [turn(start, -1)]
        for step in range(3):
            if layer == 0:
                beside += meanwhile(step, behind[-2] if step else None)
            done = (behind[-1], ahead[-1]) + (beside[-1] if layer == 0 else ())
            points.append(behind[-1])
            points.append(ahead[-1])
            next_behind, next_ahead = after(behind[-1], *done), after(ahead[-1], *done)
            if step == 2:
                next_behind, next_ahead = next_behind[:half], next_ahead[half:]
            behind.append(turn(next_behind, 1))
            ahead.append(turn(next_ahead, -1))
        last = (behind[3], ahead[3])
        points += last
        result.append(((mine, *behind[:3], *ahead[:3], behind[3], ahead[3]), spots, tables[layer]))
    return result, points


def send_positions(owner_row, slots):
    if not has_ring():
        return owner_row
    way = (owner_place(owner_row // slots) - ring_place()) % 8
    return (way * slots + owner_row % slots).astype(jnp.int32)


def reduce_start(grads, slots):
    half = slots // 2
    return turn(grads[4 * slots : 4 * slots + half], 1), turn(grads[4 * slots + half : 5 * slots], -1)


def reduce_next(grads, slots, step, came, *marks):
    forward = grads[(5 - step) * slots : (6 - step) * slots].astype(f32)
    backward = grads[(3 + step) * slots : (4 + step) * slots].astype(f32)
    ahead, behind = came[0].astype(f32), came[1].astype(f32)
    if step == 2:
        half = slots // 2
        forward = jnp.concatenate([forward[:half] + ahead, forward[half:]])
        backward = jnp.concatenate([backward[:half], backward[half:] + behind])
    else:
        forward, backward = forward + ahead, backward + behind
    forward, backward = lax.optimization_barrier((forward.astype(bf16), backward.astype(bf16), *marks))[:2]
    return turn(forward, 1), turn(backward, -1)


def norm_kernel(base, keep, first, second, vec, low_out, full_out, normed_out, scale_out, *, rows):
    bias, gain, shift = rows
    hidden = (
        base[...]
        + keep[...]
        + first[...].astype(f32)
        + second[...].astype(f32)
        + vec[bias : bias + 1, :]
    )
    center = jnp.mean(hidden, axis=1, keepdims=True)
    centred = hidden - center
    spread = jnp.mean(centred * centred, axis=1, keepdims=True)
    scale = lax.rsqrt(spread + eps_norm)
    normed = centred * scale
    full = normed * vec[gain : gain + 1, :] + vec[shift : shift + 1, :]
    full_out[...] = full
    low_out[...] = full.astype(bf16)
    normed_out[...] = normed
    scale_out[...] = scale


def top_half(array):
    return pl.BlockSpec((array.shape[0] // 2, array.shape[1]), lambda i: (0, 0))


def whole_spec(array):
    nd = len(array.shape)
    return pl.BlockSpec(tuple(array.shape), lambda i, nd=nd: (0,) * nd)


def norm_step(base, sums, vec, rows):
    keep, first, second = sums
    tokens, width = base.shape
    outs = [
        shape((tokens, width), bf16),
        shape((tokens, width), f32),
        shape((tokens, width), f32),
        shape((tokens, 1), f32),
    ]
    return pl.pallas_call(
        functools.partial(norm_kernel, rows=rows),
        grid=(1,),
        in_specs=[whole_spec(base), top_half(keep), top_half(first), whole_spec(second), whole_spec(vec)],
        out_specs=[whole_spec(o) for o in outs],
        out_shape=outs,
        compiler_params=params(12),
        cost_estimate=cost(1.2),
        name="norm",
    )(base, keep, first, second, vec)


def norm_back_kernel(*refs, gain, summed):
    if summed:
        base, keep, first, second, normed, scale, vec, low_out, full_out, sums_out = refs
        grad = base[...] + keep[...] + first[...].astype(f32) + second[...].astype(f32)
    else:
        base, normed, scale, vec, low_out, full_out, sums_out = refs
        grad = base[...]
    value = normed[...]
    scaled = grad * vec[gain : gain + 1, :]
    mean_grad = jnp.mean(scaled, axis=1, keepdims=True)
    mean_cross = jnp.mean(scaled * value, axis=1, keepdims=True)
    result = scale[...] * (scaled - mean_grad - value * mean_cross)
    full_out[...] = result
    low_out[...] = result.astype(bf16)
    sums_out[0:1, :] = jnp.sum(result, axis=0, keepdims=True)
    sums_out[1:2, :] = jnp.sum(grad * value, axis=0, keepdims=True)
    sums_out[2:3, :] = jnp.sum(grad, axis=0, keepdims=True)


def norm_back_step(base, sums, normed, scale, vec, gain):
    tokens, width = base.shape
    outs = [shape((tokens, width), bf16), shape((tokens, width), f32), shape((3, width), f32)]
    operands = [base]
    specs = [whole_spec(base)]
    if sums is not None:
        keep, first, second = sums
        operands += [keep, first, second]
        specs += [top_half(keep), top_half(first), whole_spec(second)]
    operands += [normed, scale, vec]
    specs += [whole_spec(normed), whole_spec(scale), whole_spec(vec)]
    return pl.pallas_call(
        functools.partial(norm_back_kernel, gain=gain, summed=sums is not None),
        grid=(1,),
        in_specs=specs,
        out_specs=[whole_spec(o) for o in outs],
        out_shape=outs,
        compiler_params=params(12),
        cost_estimate=cost(1.5),
        name="norm_back",
    )(*operands)


def store_sums(total, send_out, keep_out):
    half = total.shape[0] // 2
    send_out[...] = total[half:].astype(bf16)
    keep_out[...] = total[:half]


def start_blocks(sources, spots, table, stage, sem):
    slots = table.shape[1]
    for row, (which, first) in enumerate(spots):

        @pl.loop(0, slots, unroll=min(slots, 24))
        def _(s, row=row, which=which, first=first):
            pltpu.make_async_copy(sources[which].at[first + s], stage.at[table[row, s]], sem).start()


def segment_bias(seg):
    row = seg[...]
    column = jnp.transpose(jnp.broadcast_to(row, (128, row.shape[1])))[:, 0:1]
    return jnp.where(column == row, 0.0, -1e30)


def attend_kernel(
    count, spots, n_qkv, n_out, table, *refs
):
    sources = refs[:count]
    (
        p0, p1, p2, p3, vec, seg,
        query_out, key_out, value_out, mix_out, log_out, send_out, keep_out, attend_out, ffn_out,
        bias, stage, sems,
    ) = refs[count:]
    start_blocks(sources, spots, table, stage, sems.at[0])
    wide = cat_rows((p0, p1, p2, p3))
    bias[...] = segment_bias(seg)
    pltpu.make_async_copy(stage, stage, sems.at[0]).wait()
    cut = n_qkv + n_out
    copies = (
        pltpu.make_async_copy(stage.at[pl.ds(0, cut)], attend_out, sems.at[1]),
        pltpu.make_async_copy(stage.at[pl.ds(cut, ffn_out.shape[0])], ffn_out, sems.at[2]),
    )
    for copy in copies:
        copy.start()
    tokens, model = wide.shape
    width = query_out.shape[1]
    tile = stage.shape[-1]
    projected = jnp.dot(
        wide, flat_matrix(stage, 0, model // tile, 3 * width // tile), preferred_element_type=f32
    )
    query = (projected[:, :width] + vec[0:1, :]).astype(bf16) * jnp.asarray(HD**-0.5, bf16)
    keys = projected[:, width : 2 * width].astype(bf16)
    values = (projected[:, 2 * width :] + vec[1:2, :]).astype(bf16)
    query_out[...] = query
    key_out[...] = keys
    value_out[...] = values
    lane = lax.broadcasted_iota(jnp.int32, (tokens, 128), 1)
    logs = jnp.zeros((tokens, 128), f32)
    mixes = []
    for pair in range(width // 128):
        cols = slice(pair * 128, pair * 128 + 128)
        halves = []
        for part in range(128 // HD):
            inside = (lane >= part * HD) & (lane < part * HD + HD)
            one = jnp.where(inside, query[:, cols], jnp.zeros((), bf16))
            scores = lax.dot_general(one, keys[:, cols], LAST, preferred_element_type=f32) + bias[...]
            top = jnp.max(scores, axis=1, keepdims=True)
            exponent = jnp.exp(scores - top)
            total = jnp.sum(exponent, axis=1, keepdims=True)
            attention = (exponent * (1.0 / total)).astype(bf16)
            halves.append((inside, jnp.dot(attention, values[:, cols], preferred_element_type=f32)))
            logs = jnp.where(lane == pair * (128 // HD) + part, top + jnp.log(total), logs)
        mixed = halves[0][1]
        for inside, other in halves[1:]:
            mixed = jnp.where(inside, other, mixed)
        mixes.append(mixed.astype(bf16))
    mixture = jnp.concatenate(mixes, axis=1)
    mix_out[...] = mixture
    log_out[...] = jnp.transpose(logs)[0:8, :]
    total = jnp.dot(
        mixture, flat_matrix(stage, n_qkv, width // tile, model // tile), preferred_element_type=f32
    )
    store_sums(total, send_out, keep_out)
    for copy in copies:
        copy.wait()


def block_rows(array, start, count):
    return pl.BlockSpec((count,) + tuple(array.shape[1:]), lambda i: (start // count, 0, 0, 0))


def attend_step(pieces, weights, counts, vec, seg):
    quarter, model = pieces[0].shape
    tokens, width = 4 * quarter, vec.shape[1]
    n_qkv, n_out, n_up = counts
    arrays, spots, table = weights
    side = arrays[0].shape[-1]
    total = n_qkv + n_out + 2 * n_up
    outs = [
        shape((tokens, width), bf16),
        shape((tokens, width), bf16),
        shape((tokens, width), bf16),
        shape((tokens, width), bf16),
        shape((8, tokens), f32),
        shape((tokens // 2, model), bf16),
        shape((tokens // 2, model), f32),
        shape((n_qkv + n_out, side, side), bf16),
        shape((2 * n_up, side, side), bf16),
    ]
    operands = list(pieces) + [vec, seg]
    return pl.pallas_call(
        functools.partial(attend_kernel, len(arrays), spots, n_qkv, n_out),
        grid_spec=pltpu.PrefetchScalarGridSpec(
            num_scalar_prefetch=1,
            grid=(),
            in_specs=[pl.BlockSpec(memory_space=pl.ANY)] * len(arrays) + vmem_spec(len(operands)),
            out_specs=vmem_spec(7) + [pl.BlockSpec(memory_space=pl.ANY)] * 2,
            scratch_shapes=[
                pltpu.VMEM((tokens, tokens), f32),
                pltpu.VMEM((total, side, side), bf16),
                pltpu.SemaphoreType.DMA((3,)),
            ],
        ),
        out_shape=outs,
        compiler_params=params(60),
        cost_estimate=cost(11),
        name="attend",
    )(table, *arrays, *operands)


def attend_back_kernel(
    p0, p1, p2, p3, w_out, w_qkv, query_in, key_in, value_in, log_in, seg,
    grad_out, sums_out, send_out, keep_out, bias,
):
    wide = cat_rows((p0, p1, p2, p3))
    tokens, model = wide.shape
    width = query_in.shape[1]
    tile = w_qkv.shape[-1]
    grad_mix = lax.dot_general(
        wide, matrix(w_out, width // tile, model // tile), LAST, preferred_element_type=f32
    ).astype(bf16)
    bias[...] = segment_bias(seg)
    lane = lax.broadcasted_iota(jnp.int32, (tokens, 128), 1)
    grads = ([], [], [])
    for pair in range(width // 128):
        cols = slice(pair * 128, pair * 128 + 128)
        query, keys, values, mix = query_in[:, cols], key_in[:, cols], value_in[:, cols], grad_mix[:, cols]
        picked = [None, None, None]
        for part in range(128 // HD):
            head = pair * (128 // HD) + part
            inside = (lane >= part * HD) & (lane < part * HD + HD)
            zero = jnp.zeros((), bf16)
            scores = (
                lax.dot_general(jnp.where(inside, keys, zero), query, LAST, preferred_element_type=f32)
                + bias[...]
            )
            attention = jnp.exp(scores - log_in[head : head + 1, :])
            pulled = lax.dot_general(jnp.where(inside, values, zero), mix, LAST, preferred_element_type=f32)
            inner = jnp.sum(attention * pulled, axis=0, keepdims=True)
            grad_scores = (attention * (pulled - inner)).astype(bf16)
            three = (
                lax.dot_general(grad_scores, keys, FIRST, preferred_element_type=f32) * (HD**-0.5),
                jnp.dot(grad_scores, query, preferred_element_type=f32),
                jnp.dot(attention.astype(bf16), mix, preferred_element_type=f32),
            )
            for which in range(3):
                if part == 0:
                    picked[which] = three[which]
                else:
                    picked[which] = jnp.where(inside, three[which], picked[which])
        for which in range(3):
            grads[which].append(picked[which].astype(bf16))
    joined = [jnp.concatenate(g, axis=1) for g in grads]
    every = jnp.concatenate(joined, axis=1)
    grad_out[...] = every
    sums_out[0:1, :] = jnp.sum(joined[0].astype(f32), axis=0, keepdims=True)
    sums_out[1:2, :] = jnp.sum(joined[2].astype(f32), axis=0, keepdims=True)
    total = lax.dot_general(
        every, matrix(w_qkv, model // tile, 3 * width // tile), LAST, preferred_element_type=f32
    )
    store_sums(total, send_out, keep_out)


def attend_back_step(pieces, blocks, counts, query, keys, values, logs, seg):
    quarter, model = pieces[0].shape
    tokens, width = query.shape
    n_qkv, n_out, n_up = counts
    per = blocks.shape[1]
    outs = [
        shape((tokens, 3 * width), bf16),
        shape((2, width), f32),
        shape((tokens // 2, model), bf16),
        shape((tokens // 2, model), f32),
    ]
    return pl.pallas_call(
        attend_back_kernel,
        grid=(1,),
        in_specs=[whole_spec(p) for p in pieces]
        + [block_rows(blocks, n_qkv // per, n_out // per), block_rows(blocks, 0, n_qkv // per)]
        + [whole_spec(a) for a in (query, keys, values, logs, seg)],
        out_specs=[whole_spec(o) for o in outs],
        out_shape=outs,
        scratch_shapes=[pltpu.VMEM((tokens, tokens), f32)],
        compiler_params=params(),
        cost_estimate=cost(6.5),
        name="attend_back",
    )(*pieces, blocks, blocks, query, keys, values, logs, seg)


def ffn_kernel(p0, p1, p2, p3, w_up, w_down, bias, act_out, slope_out, send_out, keep_out, total):
    step = pl.program_id(0)
    wide = cat_rows((p0, p1, p2, p3))
    model = wide.shape[1]
    tile = w_up.shape[-1]
    cols = act_out.shape[1] // tile
    pre = jnp.dot(wide, matrix(w_up, model // tile, cols), preferred_element_type=f32) + bias[...]
    cdf = 0.5 + 0.5 * lax.erf(pre * (0.5**0.5))
    slope_out[...] = cdf + pre * (jnp.exp(-0.5 * pre * pre) * (1.0 / math.sqrt(2.0 * math.pi)))
    activated = (pre * cdf).astype(bf16)
    act_out[...] = activated
    part = jnp.dot(activated, matrix(w_down, cols, model // tile), preferred_element_type=f32)

    @pl.when(step == 0)
    def _():
        total[...] = part

    @pl.when(step > 0)
    def _():
        total[...] += part

    @pl.when(step == pl.num_programs(0) - 1)
    def _():
        store_sums(total[...], send_out, keep_out)


def fixed(array):
    nd = len(array.shape)
    return pl.BlockSpec(tuple(array.shape), lambda i, nd=nd: (0,) * nd)


def ffn_specs(blocks, counts, chunk_blocks):
    n_qkv, n_out, n_up = counts
    per = blocks.shape[1]
    side = blocks.shape[2]
    up_row = 0
    up_rows = n_up // per
    down_row = n_up // per
    up_spec = pl.BlockSpec((up_rows, chunk_blocks, side, side), lambda i: (up_row // up_rows, i, 0, 0))
    down_spec = pl.BlockSpec((chunk_blocks, per, side, side), lambda i: (down_row // chunk_blocks + i, 0, 0, 0))
    return up_spec, down_spec


def ffn_step(pieces, blocks, counts, up_bias, steps=4):
    quarter, model = pieces[0].shape
    tokens, hidden = 4 * quarter, up_bias.shape[1]
    chunk = hidden // steps
    up_spec, down_spec = ffn_specs(blocks, counts, chunk // blocks.shape[2])
    outs = [
        shape((tokens, hidden), bf16),
        shape((tokens, hidden), f32),
        shape((tokens // 2, model), bf16),
        shape((tokens // 2, model), f32),
    ]
    by_cols = pl.BlockSpec((tokens, chunk), lambda i: (0, i))
    return pl.pallas_call(
        ffn_kernel,
        grid=(steps,),
        in_specs=[fixed(p) for p in pieces]
        + [up_spec, down_spec, pl.BlockSpec((1, chunk), lambda i: (0, i))],
        out_specs=[by_cols, by_cols, fixed(outs[2]), fixed(outs[3])],
        out_shape=outs,
        scratch_shapes=[pltpu.VMEM((tokens, model), f32)],
        compiler_params=params(),
        cost_estimate=cost(5),
        name="ffn",
    )(*pieces, blocks, blocks, up_bias)


def ffn_back_kernel(p0, p1, p2, p3, w_up, w_down, slope, grad_out, bias_out, send_out, keep_out, total):
    step = pl.program_id(0)
    wide = cat_rows((p0, p1, p2, p3))
    model = wide.shape[1]
    tile = w_up.shape[-1]
    cols = grad_out.shape[1] // tile
    pulled = lax.dot_general(wide, matrix(w_down, cols, model // tile), LAST, preferred_element_type=f32)
    grad = (pulled * slope[...]).astype(bf16)
    grad_out[...] = grad
    bias_out[...] = jnp.sum(grad.astype(f32), axis=0, keepdims=True)
    part = lax.dot_general(grad, matrix(w_up, model // tile, cols), LAST, preferred_element_type=f32)

    @pl.when(step == 0)
    def _():
        total[...] = part

    @pl.when(step > 0)
    def _():
        total[...] += part

    @pl.when(step == pl.num_programs(0) - 1)
    def _():
        store_sums(total[...], send_out, keep_out)


def ffn_back_step(pieces, blocks, counts, slope, steps=4):
    quarter, model = pieces[0].shape
    tokens, hidden = slope.shape
    chunk = hidden // steps
    up_spec, down_spec = ffn_specs(blocks, counts, chunk // blocks.shape[2])
    outs = [
        shape((tokens, hidden), bf16),
        shape((1, hidden), f32),
        shape((tokens // 2, model), bf16),
        shape((tokens // 2, model), f32),
    ]
    by_cols = pl.BlockSpec((tokens, chunk), lambda i: (0, i))
    return pl.pallas_call(
        ffn_back_kernel,
        grid=(steps,),
        in_specs=[fixed(p) for p in pieces] + [up_spec, down_spec, by_cols],
        out_specs=[by_cols, pl.BlockSpec((1, chunk), lambda i: (0, i)), fixed(outs[2]), fixed(outs[3])],
        out_shape=outs,
        scratch_shapes=[pltpu.VMEM((tokens, model), f32)],
        compiler_params=params(),
        cost_estimate=cost(7),
        name="ffn_back",
    )(*pieces, blocks, blocks, slope)


def weight_grad_jobs(jobs, operands, side, store):
    at = 0
    for left_count, right_count, base in jobs:
        left = operands[at : at + left_count]
        right = operands[at + left_count : at + left_count + right_count]
        at += left_count + right_count
        columns = cat_rows(right)
        per = columns.shape[1] // side
        width = left[0].shape[1]
        chunk = min(width, 2 * side)
        for start in range(0, width, chunk):
            rows = jnp.concatenate([ref[:, start : start + chunk] for ref in left], axis=0)
            result = lax.dot_general(rows, columns, FIRST, preferred_element_type=f32).astype(bf16)
            for i in range(chunk // side):
                for j in range(per):
                    store(
                        base + (start // side + i) * per + j,
                        result[i * side : (i + 1) * side, j * side : (j + 1) * side],
                    )


def job_parts(jobs, side):
    operands = [a for left, right, base in jobs for a in left + right]
    layout = tuple((len(left), len(right), base) for left, right, base in jobs)
    blocks = sum(left[0].shape[1] // side * (right[0].shape[1] // side) for left, right, base in jobs)
    tokens = sum(a.shape[0] for a in jobs[0][0])
    return operands, layout, blocks, tokens


def block_grad_kernel(jobs, used, chained, place, *refs):
    out, stage, sem = refs[used + chained :]
    slots = []

    def store(block, value):
        slot = len(slots)
        slots.append(block)
        stage[slot] = value
        pltpu.make_async_copy(stage.at[slot], out.at[place[block]], sem).start()

    weight_grad_jobs(jobs, refs[:used], stage.shape[-1], store)
    pltpu.make_async_copy(stage, out.at[pl.ds(0, stage.shape[0])], sem).wait()


def block_grad_step(jobs, place, total, side, target=None):
    operands, layout, blocks, tokens = job_parts(jobs, side)
    chained = [] if target is None else [target]
    return pl.pallas_call(
        functools.partial(block_grad_kernel, layout, len(operands), len(chained)),
        grid_spec=pltpu.PrefetchScalarGridSpec(
            num_scalar_prefetch=1,
            grid=(),
            in_specs=vmem_spec(len(operands)) + [pl.BlockSpec(memory_space=pl.ANY)] * len(chained),
            out_specs=pl.BlockSpec(memory_space=pl.ANY),
            scratch_shapes=[pltpu.VMEM((blocks, side, side), bf16), pltpu.SemaphoreType.DMA],
        ),
        out_shape=shape((total, side, side), bf16),
        input_output_aliases={1 + len(operands): 0} if chained else {},
        compiler_params=params(60),
        cost_estimate=cost(4 if chained else 6),
        name="block_grad",
    )(place, *operands, *chained)


def update_kernel(part_count, chained, *refs):
    parts = refs[:part_count]
    masters, left, right, left_root, right_root = refs[part_count : part_count + 5]
    grad_out, left_out, right_out, weight_out = refs[part_count + 5 + chained :]
    grad = parts[0][...].astype(f32)
    for part in parts[1:]:
        grad = grad + part[...].astype(f32)
    grad_out[0] = grad
    for b in range(grad.shape[0]):
        low = grad[b].astype(bf16)
        left_out[0, b] = stat_decay * left[0, b] + (1.0 - stat_decay) * lax.dot_general(
            low, low, LAST, preferred_element_type=f32
        )
        right_out[0, b] = stat_decay * right[0, b] + (1.0 - stat_decay) * lax.dot_general(
            low, low, FIRST, preferred_element_type=f32
        )
        inner = jnp.dot(low, right_root[0, b].astype(bf16), preferred_element_type=f32)
        outer = jnp.dot(left_root[0, b].astype(bf16), inner.astype(bf16), preferred_element_type=f32)
        weight_out[0, b] = masters[0, b] - update_rate * outer


def update_step(parts, layer, state, previous):
    layers, slots, side, _ = state[0].shape
    group = 4 if slots % 4 == 0 else slots
    one = pl.BlockSpec((1, group, side, side), lambda i: (layer, i, 0, 0))
    chained = [] if previous is None else list(previous)
    aliases = {len(parts) + 5 + k: k for k in range(len(chained))}
    return pl.pallas_call(
        functools.partial(update_kernel, len(parts), len(chained)),
        grid=(slots // group,),
        in_specs=[pl.BlockSpec((group, side, side), lambda i: (i, 0, 0))] * len(parts)
        + [one] * 5
        + [pl.BlockSpec(memory_space=pl.ANY)] * len(chained),
        out_specs=[one] * 4,
        out_shape=[shape(state[0].shape, f32)] * 4,
        input_output_aliases=aliases,
        compiler_params=params(60),
        cost_estimate=cost(10),
        name="update",
    )(*parts, *state, *chained)


def body(
    layer_in,
    cotangent,
    segment_ids,
    owner_map,
    masters,
    left_stats,
    right_stats,
    left_roots,
    right_roots,
    vectors,
    up_bias,
):
    layers, slots, side = masters.shape[0], masters.shape[1], masters.shape[-1]
    tokens, width = layer_in.shape
    model = width * lax.axis_size("tensor")
    hidden = up_bias.shape[1]
    tile_rows = model // side
    n_qkv = tile_rows * (3 * width // side)
    n_out = width // side * tile_rows
    n_up = tile_rows * (hidden // side)
    counts = (n_qkv, n_out, n_up)
    total = owner_map.shape[1]
    index = lax.axis_index("tensor")
    quarter = tokens // 4

    segments = jnp.concatenate(
        by_index([segment_ids[:, g * quarter : (g + 1) * quarter] for g in range(4)]), axis=1
    )
    segments = jnp.concatenate(
        [segments[:, g * quarter : (g + 1) * quarter] for g in (0, 2, 1, 3)], axis=1
    )
    seg = segments.astype(f32)

    made = {}

    def meanwhile(stage, mark):
        def hold(values):
            return values if mark is None else after(values, mark)

        if stage == 0:
            near = swap(vectors, "tensor", 1)
            far = swap(jnp.stack([vectors, near]), "tensor", 2)
            made["vectors"] = jnp.concatenate(by_index([vectors, near, far[0], far[1]]), axis=2)
            made["stream"] = to_tokens(layer_in)
            made["places"] = tuple(send_positions(owner_map, slots))
            part = (made["vectors"], made["stream"]) + made["places"]
        elif stage == 1:
            made["wide"] = gather_tokens(hold(made["stream"]).astype(bf16))
            part = made["wide"] + (seg,)
        else:
            made["grad"] = to_tokens(hold(cotangent))
            part = (made["grad"],)
        return (part,)

    own = [masters[layer] for layer in range(layers)]
    sources, points = weight_sources(own, owner_map, meanwhile)
    paired = points is not None
    wide_vectors, stream, wide_in, grad, places = (
        made[name] for name in ("vectors", "stream", "wide", "grad", "places")
    )
    weights = []

    kept = []
    for layer in range(layers):
        vec = wide_vectors[layer]
        if layer > 0:
            wide_in = gather_tokens(stream_low)
        query, keys, values, mixture, logs, send, keep, attend_blocks, ffn_blocks = attend_step(
            wide_in, sources[layer], counts, vectors[layer], seg
        )
        attend_blocks = attend_blocks.reshape(-1, tile_rows, side, side)
        ffn_blocks = ffn_blocks.reshape(-1, tile_rows, side, side)
        weights.append((attend_blocks, ffn_blocks))
        sums, message = scatter_sum(send, keep)
        if layer == 0 and paired:
            sums = (after(sums[0], *points[8:10]),) + sums[1:]
        mid_low, middle, normed_one, scale_one = norm_step(stream, sums, vec, (2, 3, 4))
        wide_mid = gather_tokens(mid_low)
        if layer == 0 and paired:
            wide_mid = wide_mid[:1] + (after(wide_mid[1], *points[10:12]),) + wide_mid[2:]
        activated, slope, send, keep = ffn_step(wide_mid, ffn_blocks, counts, up_bias[layer : layer + 1])
        sums, message = scatter_sum(send, keep, *(points[12:14] if layer == 0 and paired else ()))
        stream_low, stream, normed_two, scale_two = norm_step(middle, sums, vec, (5, 6, 7))
        kept.append(
            (wide_in, query, keys, values, mixture, logs, normed_one, scale_one, wide_mid, activated, slope, normed_two, scale_two)
        )

    vector_sums = [None] * layers
    bias_sums = [None] * layers
    sums = None
    above, came = None, ()
    for layer in reversed(range(layers)):
        vec, (attend_blocks, ffn_blocks) = wide_vectors[layer], weights[layer]
        (wide_in, query, keys, values, mixture, logs, normed_one, scale_one, wide_mid, activated, slope, normed_two, scale_two) = kept[layer]
        first = layer == 0 and paired
        grad_low, grad_two, sums_two = norm_back_step(grad, sums, normed_two, scale_two, vec, 6)
        wide_grad = gather_tokens(grad_low)
        if first:
            wide_grad = wide_grad[:1] + (after(wide_grad[1], *came),) + wide_grad[2:]
            came = reduce_next(above, slots, 2, came)
        grad_pre, bias_sum, send, keep = ffn_back_step(wide_grad, ffn_blocks, counts, slope)
        sums, message = scatter_sum(send, keep)
        ffn_jobs = [(wide_mid, (grad_pre,), n_qkv + n_out), ((activated,), wide_grad, n_qkv + n_out + n_up)]
        if first:
            sums = (after(sums[0], *came),) + sums[1:]
            came = reduce_next(above, slots, 3, came)
        else:
            ffn_grads = block_grad_step(ffn_jobs, after(places[layer], message), total, side)
            sums = (after(sums[0], ffn_grads),) + sums[1:]
        grad_low, grad_one, sums_one = norm_back_step(grad_two, sums, normed_one, scale_one, vec, 3)
        wide_first = gather_tokens(grad_low)
        if first:
            ffn_grads = block_grad_step(ffn_jobs, after(places[layer], grad_low), total, side)
            wide_first = wide_first[:1] + (after(wide_first[1], ffn_grads, *came),) + wide_first[2:]
            came = reduce_next(above, slots, 4, came)
        grad_qkv, qv_sums, send, keep = attend_back_step(
            wide_first, attend_blocks, counts, query, keys, values, logs, seg
        )
        sums, message = scatter_sum(send, keep)
        block_grads = block_grad_step(
            [(wide_in, (grad_qkv,), 0), ((mixture,), wide_first, n_qkv)],
            places[layer] if first else after(places[layer], message), total, side, ffn_grads,
        )
        grad = grad_one
        spread = jnp.concatenate([jnp.zeros_like(sums_one[:2]), sums_one, sums_two], axis=0)
        vector_sums[layer] = lax.dynamic_update_slice(spread, qv_sums, (0, index * width))
        bias_sums[layer] = lax.dynamic_update_slice(
            jnp.zeros((1, 4 * hidden), f32), bias_sum, (0, index * hidden)
        ).reshape(4 * hidden // model, model)
        if layer > 0:
            sums = (after(sums[0], block_grads),) + sums[1:]
            above = block_grads
            if paired:
                came = reduce_start(above, slots)

    small = jnp.stack([jnp.concatenate(pair, axis=0) for pair in zip(vector_sums, bias_sums)])
    small = small + swap(small, "tensor", 1)
    small = small + swap(small, "tensor", 2)
    state = (masters, left_stats, right_stats, left_roots, right_roots)
    if paired:
        before = (above[:slots], *came)
        marks = [reduce_start(after(block_grads, small, *came), slots)]
        small = small + swap(small, "dp", 2)
        marks.append(reduce_next(block_grads, slots, 2, marks[0], small))
        small = small + swap(after(small, *marks[0]), "dp", 4)
        marks.append(reduce_next(block_grads, slots, 3, marks[1], small))
        small = small + swap(after(small, *marks[1]), "dp", 1)
        came = reduce_next(block_grads, slots, 4, marks[2], small)
        parts = (block_grads[:slots], *came)
        input_grad, layer_out = (
            from_tokens(values, (marks[0][0], marks[1][0]))
            for values in (grad + sums[0][:quarter] + sums[1][:quarter].astype(f32) + sums[2].astype(f32), stream)
        )
        updated = update_step(before, 1, (after(masters, *marks[1]),) + state[1:], None)
        updated = update_step(parts, 0, state, updated)
    else:
        small = lax.psum(small, "dp")
        input_grad, layer_out = (
            from_tokens(values)
            for values in (grad + sums[0][:quarter] + sums[1][:quarter].astype(f32) + sums[2].astype(f32), stream)
        )
        updated = None
        for layer, grads in ((1, above), (0, block_grads)):
            mine = lax.psum_scatter(grads, "dp", scatter_dimension=0, tiled=True)
            updated = update_step((mine,), layer, state, updated)
    vector_grads = lax.dynamic_slice(small[:, :8], (0, 0, index * width), (layers, 8, width))
    up_bias_grads = lax.dynamic_slice(
        small[:, 8:].reshape(layers, 4 * hidden), (0, index * hidden), (layers, hidden)
    )
    reduced, left_new, right_new, new_weights = updated
    vector_rate = 0.5 / math.sqrt(tokens * lax.axis_size("dp"))
    return (
        layer_out,
        input_grad,
        reduced,
        left_new,
        right_new,
        new_weights,
        vector_grads,
        vectors - vector_rate * vector_grads,
        up_bias_grads,
        up_bias - vector_rate * up_bias_grads,
    )


def solution(mesh):
    owned = P(None, ("dp", "tensor"), None, None)
    return jax.shard_map(
        body,
        mesh=mesh,
        in_specs=(
            P("dp", "tensor"),
            P("dp", "tensor"),
            P("dp", None),
            P(),
            owned,
            owned,
            owned,
            owned,
            owned,
            P(None, None, "tensor"),
            P(None, "tensor"),
        ),
        out_specs=(
            P("dp", "tensor"),
            P("dp", "tensor"),
            owned,
            owned,
            owned,
            owned,
            P(None, None, "tensor"),
            P(None, None, "tensor"),
            P(None, "tensor"),
            P(None, "tensor"),
        ),
        check_vma=False,
    )
```

```python
import functools
import math

import jax
import jax.numpy as jnp
from jax import lax
from jax.experimental import pallas as pl
from jax.experimental.pallas import tpu as pltpu
from jax.sharding import PartitionSpec as P

HD = 64
eps_norm = 1e-12
stat_decay = 0.5
update_rate = 0.5
f32 = jnp.float32
bf16 = jnp.bfloat16

LAST = (((1,), (1,)), ((), ()))
FIRST = (((0,), (0,)), ((), ()))


def vmem_spec(count):
    return [pl.BlockSpec(memory_space=pltpu.VMEM)] * count


def params(mib=40):
    return pltpu.CompilerParams(vmem_limit_bytes=mib * 1024 * 1024)


def cost(microseconds):
    return pl.CostEstimate(flops=0, bytes_accessed=int(microseconds * 3.4e6), transcendentals=0)


def shape(dims, dtype):
    return jax.ShapeDtypeStruct(dims, dtype)


def cat_rows(refs):
    return jnp.concatenate([ref[...] for ref in refs], axis=0)


def matrix(ref, rows, cols):
    width = ref.shape[1]
    return jnp.concatenate(
        [
            jnp.concatenate(
                [ref[(r * cols + c) // width, (r * cols + c) % width] for c in range(cols)], axis=1
            )
            for r in range(rows)
        ],
        axis=0,
    )


def flat_matrix(ref, base, rows, cols):
    return jnp.concatenate(
        [jnp.concatenate([ref[base + r * cols + c] for c in range(cols)], axis=1) for r in range(rows)], axis=0
    )


def swap(values, axis, flip):
    count = lax.axis_size(axis)
    return lax.ppermute(values, axis, [(i, i ^ flip) for i in range(count)])


def gather_tokens(piece):
    far = swap(piece, "tensor", 2)
    near = swap(piece, "tensor", 1)
    both = swap(far, "tensor", 1)
    return (piece, far, near, both)


def scatter_sum(send, keep, *marks):
    rows = send.shape[0] // 2
    first = swap(send, "tensor", 1)
    message = (keep[rows:] + first[rows:].astype(f32)).astype(bf16)
    if marks:
        message = after(message, *marks)
    return (keep, first, swap(message, "tensor", 2)), message


def by_index(relative):
    index = lax.axis_index("tensor")
    core, x_pos = index % 2 == 1, index // 2 == 1
    r0, r1, r2, r3 = relative
    a0, a1 = jnp.where(core, r1, r0), jnp.where(core, r0, r1)
    a2, a3 = jnp.where(core, r3, r2), jnp.where(core, r2, r3)
    return [
        jnp.where(x_pos, a2, a0),
        jnp.where(x_pos, a3, a1),
        jnp.where(x_pos, a0, a2),
        jnp.where(x_pos, a1, a3),
    ]


def to_tokens(values):
    rows, width = values.shape
    quarter = rows // 4
    r0, r1, r2, r3 = by_index([values[g * quarter : (g + 1) * quarter] for g in range(4)])
    got = swap(jnp.stack([r2, r3]), "tensor", 2)
    near = swap(jnp.stack([r1, got[1]]), "tensor", 1)
    return jnp.concatenate(by_index([r0, near[0], got[0], near[1]]), axis=1)


def from_tokens(values, marks=None):
    width = values.shape[1] // 4
    r0, r1, r2, r3 = by_index([values[:, g * width : (g + 1) * width] for g in range(4)])
    near = jnp.stack([r1, r3])
    got = swap(near if marks is None else after(near, marks[0]), "tensor", 1)
    rest = jnp.stack([r2, got[1]])
    far = swap(rest if marks is None else after(rest, marks[1]), "tensor", 2)
    return jnp.concatenate(by_index([r0, got[0], far[0], far[1]]), axis=0)


ring = (0, 2, 4, 6, 7, 5, 3, 1)


def ring_place():
    index = lax.axis_index("dp")
    return jnp.where(index % 2 == 0, index // 2, 7 - index // 2)


def owner_place(owner):
    return jnp.where(owner % 2 == 0, owner // 2, 7 - owner // 2)


def turn(values, way):
    return lax.ppermute(values, "dp", [(ring[p], ring[(p + way) % 8]) for p in range(8)])


def after(values, *others):
    return lax.optimization_barrier((values,) + tuple(others))[0]


def has_ring():
    return lax.axis_size("dp") == 8


def weight_sources(own, owner_map, meanwhile):
    layers, total = owner_map.shape
    slots = own[0].shape[0]
    half = slots // 2
    positions = jnp.arange(total, dtype=jnp.int32)
    hits = owner_map[:, None, :] == positions[None, :, None]
    inverse = jnp.sum(jnp.where(hits, positions[None, None, :], 0), axis=2).astype(jnp.int32)
    if not has_ring():
        wholes = [lax.all_gather(values.astype(bf16), "dp", axis=0, tiled=True) for values in own]
        for stage in range(3):
            meanwhile(stage, None)
        return [((whole,), ((0, 0),), row[None, :]) for whole, row in zip(wholes, inverse)], None
    ways = jnp.array([0, -1, -2, -3, 1, 2, 3, 4], jnp.int32)
    spots = tuple((j, first) for j in range(7) for first in (0, half)) + ((7, 0), (8, 0))
    target = (ring_place() + ways) % 8
    device = jnp.where(target < 4, 2 * target, 15 - 2 * target)
    mask = device[None, :, None, None] == jnp.arange(8, dtype=jnp.int32)[None, None, :, None]
    rows = jnp.sum(jnp.where(mask, inverse.reshape(layers, 1, 8, slots), 0), axis=2)
    tables = [table for table in rows.reshape(layers, 16, half).astype(jnp.int32)]
    result, points, last, beside = [], [], (), ()
    for layer in range(layers):
        mine = own[layer] if layer == 0 else after(own[layer], points[0])
        mine = mine.astype(bf16)
        start = after(mine, *last) if last else mine
        behind, ahead = [turn(start, 1)], [turn(start, -1)]
        for step in range(3):
            if layer == 0:
                beside += meanwhile(step, behind[-2] if step else None)
            done = (behind[-1], ahead[-1]) + (beside[-1] if layer == 0 else ())
            points.append(behind[-1])
            points.append(ahead[-1])
            next_behind, next_ahead = after(behind[-1], *done), after(ahead[-1], *done)
            if step == 2:
                next_behind, next_ahead = next_behind[:half], next_ahead[half:]
            behind.append(turn(next_behind, 1))
            ahead.append(turn(next_ahead, -1))
        last = (behind[3], ahead[3])
        points += last
        result.append(((mine, *behind[:3], *ahead[:3], behind[3], ahead[3]), spots, tables[layer]))
    return result, points


def send_positions(owner_row, slots):
    if not has_ring():
        return owner_row
    way = (owner_place(owner_row // slots) - ring_place()) % 8
    return (way * slots + owner_row % slots).astype(jnp.int32)


def reduce_start(grads, slots):
    half = slots // 2
    return turn(grads[4 * slots : 4 * slots + half], 1), turn(grads[4 * slots + half : 5 * slots], -1)


def reduce_next(grads, slots, step, came, *marks):
    forward = grads[(5 - step) * slots : (6 - step) * slots].astype(f32)
    backward = grads[(3 + step) * slots : (4 + step) * slots].astype(f32)
    ahead, behind = came[0].astype(f32), came[1].astype(f32)
    if step == 2:
        half = slots // 2
        forward = jnp.concatenate([forward[:half] + ahead, forward[half:]])
        backward = jnp.concatenate([backward[:half], backward[half:] + behind])
    else:
        forward, backward = forward + ahead, backward + behind
    forward, backward = lax.optimization_barrier((forward.astype(bf16), backward.astype(bf16), *marks))[:2]
    return turn(forward, 1), turn(backward, -1)


def norm_kernel(base, keep, first, second, vec, low_out, full_out, normed_out, scale_out, *, rows):
    bias, gain, shift = rows
    hidden = (
        base[...]
        + keep[...]
        + first[...].astype(f32)
        + second[...].astype(f32)
        + vec[bias : bias + 1, :]
    )
    center = jnp.mean(hidden, axis=1, keepdims=True)
    centred = hidden - center
    spread = jnp.mean(centred * centred, axis=1, keepdims=True)
    scale = lax.rsqrt(spread + eps_norm)
    normed = centred * scale
    full = normed * vec[gain : gain + 1, :] + vec[shift : shift + 1, :]
    full_out[...] = full
    low_out[...] = full.astype(bf16)
    normed_out[...] = normed
    scale_out[...] = scale


def top_half(array):
    return pl.BlockSpec((array.shape[0] // 2, array.shape[1]), lambda i: (0, 0))


def whole_spec(array):
    nd = len(array.shape)
    return pl.BlockSpec(tuple(array.shape), lambda i, nd=nd: (0,) * nd)


def norm_step(base, sums, vec, rows):
    keep, first, second = sums
    tokens, width = base.shape
    outs = [
        shape((tokens, width), bf16),
        shape((tokens, width), f32),
        shape((tokens, width), f32),
        shape((tokens, 1), f32),
    ]
    return pl.pallas_call(
        functools.partial(norm_kernel, rows=rows),
        grid=(1,),
        in_specs=[whole_spec(base), top_half(keep), top_half(first), whole_spec(second), whole_spec(vec)],
        out_specs=[whole_spec(o) for o in outs],
        out_shape=outs,
        compiler_params=params(12),
        cost_estimate=cost(1.2),
        name="norm",
    )(base, keep, first, second, vec)


def norm_back_kernel(*refs, gain, summed):
    if summed:
        base, keep, first, second, normed, scale, vec, low_out, full_out, sums_out = refs
        grad = base[...] + keep[...] + first[...].astype(f32) + second[...].astype(f32)
    else:
        base, normed, scale, vec, low_out, full_out, sums_out = refs
        grad = base[...]
    value = normed[...]
    scaled = grad * vec[gain : gain + 1, :]
    mean_grad = jnp.mean(scaled, axis=1, keepdims=True)
    mean_cross = jnp.mean(scaled * value, axis=1, keepdims=True)
    result = scale[...] * (scaled - mean_grad - value * mean_cross)
    full_out[...] = result
    low_out[...] = result.astype(bf16)
    sums_out[0:1, :] = jnp.sum(result, axis=0, keepdims=True)
    sums_out[1:2, :] = jnp.sum(grad * value, axis=0, keepdims=True)
    sums_out[2:3, :] = jnp.sum(grad, axis=0, keepdims=True)


def norm_back_step(base, sums, normed, scale, vec, gain):
    tokens, width = base.shape
    outs = [shape((tokens, width), bf16), shape((tokens, width), f32), shape((3, width), f32)]
    operands = [base]
    specs = [whole_spec(base)]
    if sums is not None:
        keep, first, second = sums
        operands += [keep, first, second]
        specs += [top_half(keep), top_half(first), whole_spec(second)]
    operands += [normed, scale, vec]
    specs += [whole_spec(normed), whole_spec(scale), whole_spec(vec)]
    return pl.pallas_call(
        functools.partial(norm_back_kernel, gain=gain, summed=sums is not None),
        grid=(1,),
        in_specs=specs,
        out_specs=[whole_spec(o) for o in outs],
        out_shape=outs,
        compiler_params=params(12),
        cost_estimate=cost(1.5),
        name="norm_back",
    )(*operands)


def store_sums(total, send_out, keep_out):
    half = total.shape[0] // 2
    send_out[...] = total[half:].astype(bf16)
    keep_out[...] = total[:half]


def start_blocks(sources, spots, table, stage, sem):
    slots = table.shape[1]
    for row, (which, first) in enumerate(spots):

        @pl.loop(0, slots, unroll=min(slots, 24))
        def _(s, row=row, which=which, first=first):
            pltpu.make_async_copy(sources[which].at[first + s], stage.at[table[row, s]], sem).start()


def segment_bias(seg):
    row = seg[...]
    column = jnp.transpose(jnp.broadcast_to(row, (128, row.shape[1])))[:, 0:1]
    return jnp.where(column == row, 0.0, -1e30)


def attend_kernel(
    count, spots, n_qkv, n_out, table, *refs
):
    sources = refs[:count]
    (
        p0, p1, p2, p3, vec, seg,
        query_out, key_out, value_out, mix_out, log_out, send_out, keep_out, attend_out, ffn_out,
        bias, stage, sems,
    ) = refs[count:]
    start_blocks(sources, spots, table, stage, sems.at[0])
    wide = cat_rows((p0, p1, p2, p3))
    bias[...] = segment_bias(seg)
    pltpu.make_async_copy(stage, stage, sems.at[0]).wait()
    cut = n_qkv + n_out
    copies = (
        pltpu.make_async_copy(stage.at[pl.ds(0, cut)], attend_out, sems.at[1]),
        pltpu.make_async_copy(stage.at[pl.ds(cut, ffn_out.shape[0])], ffn_out, sems.at[2]),
    )
    for copy in copies:
        copy.start()
    tokens, model = wide.shape
    width = query_out.shape[1]
    tile = stage.shape[-1]
    projected = jnp.dot(
        wide, flat_matrix(stage, 0, model // tile, 3 * width // tile), preferred_element_type=f32
    )
    query = (projected[:, :width] + vec[0:1, :]).astype(bf16) * jnp.asarray(HD**-0.5, bf16)
    keys = projected[:, width : 2 * width].astype(bf16)
    values = (projected[:, 2 * width :] + vec[1:2, :]).astype(bf16)
    query_out[...] = query
    key_out[...] = keys
    value_out[...] = values
    lane = lax.broadcasted_iota(jnp.int32, (tokens, 128), 1)
    logs = jnp.zeros((tokens, 128), f32)
    mixes = []
    for pair in range(width // 128):
        cols = slice(pair * 128, pair * 128 + 128)
        halves = []
        for part in range(128 // HD):
            inside = (lane >= part * HD) & (lane < part * HD + HD)
            one = jnp.where(inside, query[:, cols], jnp.zeros((), bf16))
            scores = lax.dot_general(one, keys[:, cols], LAST, preferred_element_type=f32) + bias[...]
            top = jnp.max(scores, axis=1, keepdims=True)
            exponent = jnp.exp(scores - top)
            total = jnp.sum(exponent, axis=1, keepdims=True)
            attention = (exponent * (1.0 / total)).astype(bf16)
            halves.append((inside, jnp.dot(attention, values[:, cols], preferred_element_type=f32)))
            logs = jnp.where(lane == pair * (128 // HD) + part, top + jnp.log(total), logs)
        mixed = halves[0][1]
        for inside, other in halves[1:]:
            mixed = jnp.where(inside, other, mixed)
        mixes.append(mixed.astype(bf16))
    mixture = jnp.concatenate(mixes, axis=1)
    mix_out[...] = mixture
    log_out[...] = jnp.transpose(logs)[0:8, :]
    total = jnp.dot(
        mixture, flat_matrix(stage, n_qkv, width // tile, model // tile), preferred_element_type=f32
    )
    store_sums(total, send_out, keep_out)
    for copy in copies:
        copy.wait()


def block_rows(array, start, count):
    return pl.BlockSpec((count,) + tuple(array.shape[1:]), lambda i: (start // count, 0, 0, 0))


def attend_step(pieces, weights, counts, vec, seg):
    quarter, model = pieces[0].shape
    tokens, width = 4 * quarter, vec.shape[1]
    n_qkv, n_out, n_up = counts
    arrays, spots, table = weights
    side = arrays[0].shape[-1]
    total = n_qkv + n_out + 2 * n_up
    outs = [
        shape((tokens, width), bf16),
        shape((tokens, width), bf16),
        shape((tokens, width), bf16),
        shape((tokens, width), bf16),
        shape((8, tokens), f32),
        shape((tokens // 2, model), bf16),
        shape((tokens // 2, model), f32),
        shape((n_qkv + n_out, side, side), bf16),
        shape((2 * n_up, side, side), bf16),
    ]
    operands = list(pieces) + [vec, seg]
    return pl.pallas_call(
        functools.partial(attend_kernel, len(arrays), spots, n_qkv, n_out),
        grid_spec=pltpu.PrefetchScalarGridSpec(
            num_scalar_prefetch=1,
            grid=(),
            in_specs=[pl.BlockSpec(memory_space=pl.ANY)] * len(arrays) + vmem_spec(len(operands)),
            out_specs=vmem_spec(7) + [pl.BlockSpec(memory_space=pl.ANY)] * 2,
            scratch_shapes=[
                pltpu.VMEM((tokens, tokens), f32),
                pltpu.VMEM((total, side, side), bf16),
                pltpu.SemaphoreType.DMA((3,)),
            ],
        ),
        out_shape=outs,
        compiler_params=params(60),
        cost_estimate=cost(11),
        name="attend",
    )(table, *arrays, *operands)


def attend_back_kernel(
    p0, p1, p2, p3, w_out, w_qkv, query_in, key_in, value_in, log_in, seg,
    grad_out, sums_out, send_out, keep_out, bias,
):
    wide = cat_rows((p0, p1, p2, p3))
    tokens, model = wide.shape
    width = query_in.shape[1]
    tile = w_qkv.shape[-1]
    grad_mix = lax.dot_general(
        wide, matrix(w_out, width // tile, model // tile), LAST, preferred_element_type=f32
    ).astype(bf16)
    bias[...] = segment_bias(seg)
    lane = lax.broadcasted_iota(jnp.int32, (tokens, 128), 1)
    grads = ([], [], [])
    for pair in range(width // 128):
        cols = slice(pair * 128, pair * 128 + 128)
        query, keys, values, mix = query_in[:, cols], key_in[:, cols], value_in[:, cols], grad_mix[:, cols]
        picked = [None, None, None]
        for part in range(128 // HD):
            head = pair * (128 // HD) + part
            inside = (lane >= part * HD) & (lane < part * HD + HD)
            zero = jnp.zeros((), bf16)
            scores = (
                lax.dot_general(jnp.where(inside, keys, zero), query, LAST, preferred_element_type=f32)
                + bias[...]
            )
            attention = jnp.exp(scores - log_in[head : head + 1, :])
            pulled = lax.dot_general(jnp.where(inside, values, zero), mix, LAST, preferred_element_type=f32)
            inner = jnp.sum(attention * pulled, axis=0, keepdims=True)
            grad_scores = (attention * (pulled - inner)).astype(bf16)
            three = (
                lax.dot_general(grad_scores, keys, FIRST, preferred_element_type=f32) * (HD**-0.5),
                jnp.dot(grad_scores, query, preferred_element_type=f32),
                jnp.dot(attention.astype(bf16), mix, preferred_element_type=f32),
            )
            for which in range(3):
                if part == 0:
                    picked[which] = three[which]
                else:
                    picked[which] = jnp.where(inside, three[which], picked[which])
        for which in range(3):
            grads[which].append(picked[which].astype(bf16))
    joined = [jnp.concatenate(g, axis=1) for g in grads]
    every = jnp.concatenate(joined, axis=1)
    grad_out[...] = every
    sums_out[0:1, :] = jnp.sum(joined[0].astype(f32), axis=0, keepdims=True)
    sums_out[1:2, :] = jnp.sum(joined[2].astype(f32), axis=0, keepdims=True)
    total = lax.dot_general(
        every, matrix(w_qkv, model // tile, 3 * width // tile), LAST, preferred_element_type=f32
    )
    store_sums(total, send_out, keep_out)


def attend_back_step(pieces, blocks, counts, query, keys, values, logs, seg):
    quarter, model = pieces[0].shape
    tokens, width = query.shape
    n_qkv, n_out, n_up = counts
    per = blocks.shape[1]
    outs = [
        shape((tokens, 3 * width), bf16),
        shape((2, width), f32),
        shape((tokens // 2, model), bf16),
        shape((tokens // 2, model), f32),
    ]
    return pl.pallas_call(
        attend_back_kernel,
        grid=(1,),
        in_specs=[whole_spec(p) for p in pieces]
        + [block_rows(blocks, n_qkv // per, n_out // per), block_rows(blocks, 0, n_qkv // per)]
        + [whole_spec(a) for a in (query, keys, values, logs, seg)],
        out_specs=[whole_spec(o) for o in outs],
        out_shape=outs,
        scratch_shapes=[pltpu.VMEM((tokens, tokens), f32)],
        compiler_params=params(),
        cost_estimate=cost(6.5),
        name="attend_back",
    )(*pieces, blocks, blocks, query, keys, values, logs, seg)


def ffn_kernel(p0, p1, p2, p3, w_up, w_down, bias, act_out, slope_out, send_out, keep_out):
    wide = cat_rows((p0, p1, p2, p3))
    model = wide.shape[1]
    tile = w_up.shape[-1]
    cols = act_out.shape[1] // tile
    pre = jnp.dot(wide, matrix(w_up, model // tile, cols), preferred_element_type=f32) + bias[...]
    cdf = 0.5 + 0.5 * lax.erf(pre * (0.5**0.5))
    slope_out[...] = cdf + pre * (jnp.exp(-0.5 * pre * pre) * (1.0 / math.sqrt(2.0 * math.pi)))
    activated = (pre * cdf).astype(bf16)
    act_out[...] = activated
    total = jnp.dot(activated, matrix(w_down, cols, model // tile), preferred_element_type=f32)
    store_sums(total, send_out, keep_out)


def fixed(array):
    nd = len(array.shape)
    return pl.BlockSpec(tuple(array.shape), lambda i, nd=nd: (0,) * nd)


def ffn_specs(blocks, counts, chunk_blocks):
    n_qkv, n_out, n_up = counts
    per = blocks.shape[1]
    side = blocks.shape[2]
    up_row = 0
    up_rows = n_up // per
    down_row = n_up // per
    up_spec = pl.BlockSpec((up_rows, chunk_blocks, side, side), lambda i: (up_row // up_rows, i, 0, 0))
    down_spec = pl.BlockSpec((chunk_blocks, per, side, side), lambda i: (down_row // chunk_blocks + i, 0, 0, 0))
    return up_spec, down_spec


def ffn_step(pieces, blocks, counts, up_bias):
    quarter, model = pieces[0].shape
    tokens, hidden = 4 * quarter, up_bias.shape[1]
    up_spec, down_spec = ffn_specs(blocks, counts, hidden // blocks.shape[2])
    outs = [
        shape((tokens, hidden), bf16),
        shape((tokens, hidden), f32),
        shape((tokens // 2, model), bf16),
        shape((tokens // 2, model), f32),
    ]
    return pl.pallas_call(
        ffn_kernel,
        grid=(1,),
        in_specs=[fixed(p) for p in pieces]
        + [up_spec, down_spec, fixed(up_bias)],
        out_specs=[fixed(o) for o in outs],
        out_shape=outs,
        compiler_params=params(),
        cost_estimate=cost(5),
        name="ffn",
    )(*pieces, blocks, blocks, up_bias)


def ffn_back_kernel(p0, p1, p2, p3, w_up, w_down, slope, grad_out, bias_out, send_out, keep_out):
    wide = cat_rows((p0, p1, p2, p3))
    model = wide.shape[1]
    tile = w_up.shape[-1]
    cols = grad_out.shape[1] // tile
    pulled = lax.dot_general(wide, matrix(w_down, cols, model // tile), LAST, preferred_element_type=f32)
    grad = (pulled * slope[...]).astype(bf16)
    grad_out[...] = grad
    bias_out[...] = jnp.sum(grad.astype(f32), axis=0, keepdims=True)
    total = lax.dot_general(grad, matrix(w_up, model // tile, cols), LAST, preferred_element_type=f32)
    store_sums(total, send_out, keep_out)


def ffn_back_step(pieces, blocks, counts, slope):
    quarter, model = pieces[0].shape
    tokens, hidden = slope.shape
    up_spec, down_spec = ffn_specs(blocks, counts, hidden // blocks.shape[2])
    outs = [
        shape((tokens, hidden), bf16),
        shape((1, hidden), f32),
        shape((tokens // 2, model), bf16),
        shape((tokens // 2, model), f32),
    ]
    return pl.pallas_call(
        ffn_back_kernel,
        grid=(1,),
        in_specs=[fixed(p) for p in pieces] + [up_spec, down_spec, fixed(slope)],
        out_specs=[fixed(o) for o in outs],
        out_shape=outs,
        compiler_params=params(),
        cost_estimate=cost(7),
        name="ffn_back",
    )(*pieces, blocks, blocks, slope)


def weight_grad_jobs(jobs, operands, side, store):
    at = 0
    for left_count, right_count, base in jobs:
        left = operands[at : at + left_count]
        right = operands[at + left_count : at + left_count + right_count]
        at += left_count + right_count
        columns = cat_rows(right)
        per = columns.shape[1] // side
        width = left[0].shape[1]
        chunk = min(width, 2 * side)
        for start in range(0, width, chunk):
            rows = jnp.concatenate([ref[:, start : start + chunk] for ref in left], axis=0)
            result = lax.dot_general(rows, columns, FIRST, preferred_element_type=f32).astype(bf16)
            for i in range(chunk // side):
                for j in range(per):
                    store(
                        base + (start // side + i) * per + j,
                        result[i * side : (i + 1) * side, j * side : (j + 1) * side],
                    )


def job_parts(jobs, side):
    operands = [a for left, right, base in jobs for a in left + right]
    layout = tuple((len(left), len(right), base) for left, right, base in jobs)
    blocks = sum(left[0].shape[1] // side * (right[0].shape[1] // side) for left, right, base in jobs)
    tokens = sum(a.shape[0] for a in jobs[0][0])
    return operands, layout, blocks, tokens


def block_grad_kernel(jobs, used, chained, place, *refs):
    out, stage, sem = refs[used + chained :]
    slots = []

    def store(block, value):
        slot = len(slots)
        slots.append(block)
        stage[slot] = value
        pltpu.make_async_copy(stage.at[slot], out.at[place[block]], sem).start()

    weight_grad_jobs(jobs, refs[:used], stage.shape[-1], store)
    pltpu.make_async_copy(stage, out.at[pl.ds(0, stage.shape[0])], sem).wait()


def block_grad_step(jobs, place, total, side, target=None):
    operands, layout, blocks, tokens = job_parts(jobs, side)
    chained = [] if target is None else [target]
    return pl.pallas_call(
        functools.partial(block_grad_kernel, layout, len(operands), len(chained)),
        grid_spec=pltpu.PrefetchScalarGridSpec(
            num_scalar_prefetch=1,
            grid=(),
            in_specs=vmem_spec(len(operands)) + [pl.BlockSpec(memory_space=pl.ANY)] * len(chained),
            out_specs=pl.BlockSpec(memory_space=pl.ANY),
            scratch_shapes=[pltpu.VMEM((blocks, side, side), bf16), pltpu.SemaphoreType.DMA],
        ),
        out_shape=shape((total, side, side), bf16),
        input_output_aliases={1 + len(operands): 0} if chained else {},
        compiler_params=params(60),
        cost_estimate=cost(4 if chained else 6),
        name="block_grad",
    )(place, *operands, *chained)


def update_kernel(part_count, chained, *refs):
    parts = refs[:part_count]
    masters, left, right, left_root, right_root = refs[part_count : part_count + 5]
    grad_out, left_out, right_out, weight_out = refs[part_count + 5 + chained :]
    grad = parts[0][...].astype(f32)
    for part in parts[1:]:
        grad = grad + part[...].astype(f32)
    grad_out[0] = grad
    for b in range(grad.shape[0]):
        low = grad[b].astype(bf16)
        left_out[0, b] = stat_decay * left[0, b] + (1.0 - stat_decay) * lax.dot_general(
            low, low, LAST, preferred_element_type=f32
        )
        right_out[0, b] = stat_decay * right[0, b] + (1.0 - stat_decay) * lax.dot_general(
            low, low, FIRST, preferred_element_type=f32
        )
        inner = jnp.dot(low, right_root[0, b].astype(bf16), preferred_element_type=f32)
        outer = jnp.dot(left_root[0, b].astype(bf16), inner.astype(bf16), preferred_element_type=f32)
        weight_out[0, b] = masters[0, b] - update_rate * outer


def update_step(parts, layer, state, previous):
    layers, slots, side, _ = state[0].shape
    group = 4 if slots % 4 == 0 else slots
    one = pl.BlockSpec((1, group, side, side), lambda i: (layer, i, 0, 0))
    chained = [] if previous is None else list(previous)
    aliases = {len(parts) + 5 + k: k for k in range(len(chained))}
    return pl.pallas_call(
        functools.partial(update_kernel, len(parts), len(chained)),
        grid=(slots // group,),
        in_specs=[pl.BlockSpec((group, side, side), lambda i: (i, 0, 0))] * len(parts)
        + [one] * 5
        + [pl.BlockSpec(memory_space=pl.ANY)] * len(chained),
        out_specs=[one] * 4,
        out_shape=[shape(state[0].shape, f32)] * 4,
        input_output_aliases=aliases,
        compiler_params=params(60),
        cost_estimate=cost(10),
        name="update",
    )(*parts, *state, *chained)


def body(
    layer_in,
    cotangent,
    segment_ids,
    owner_map,
    masters,
    left_stats,
    right_stats,
    left_roots,
    right_roots,
    vectors,
    up_bias,
):
    layers, slots, side = masters.shape[0], masters.shape[1], masters.shape[-1]
    tokens, width = layer_in.shape
    model = width * lax.axis_size("tensor")
    hidden = up_bias.shape[1]
    tile_rows = model // side
    n_qkv = tile_rows * (3 * width // side)
    n_out = width // side * tile_rows
    n_up = tile_rows * (hidden // side)
    counts = (n_qkv, n_out, n_up)
    total = owner_map.shape[1]
    index = lax.axis_index("tensor")
    quarter = tokens // 4

    segments = jnp.concatenate(
        by_index([segment_ids[:, g * quarter : (g + 1) * quarter] for g in range(4)]), axis=1
    )
    segments = jnp.concatenate(
        [segments[:, g * quarter : (g + 1) * quarter] for g in (0, 2, 1, 3)], axis=1
    )
    seg = segments.astype(f32)

    made = {}

    def meanwhile(stage, mark):
        def hold(values):
            return values if mark is None else after(values, mark)

        if stage == 0:
            near = swap(vectors, "tensor", 1)
            far = swap(jnp.stack([vectors, near]), "tensor", 2)
            made["vectors"] = jnp.concatenate(by_index([vectors, near, far[0], far[1]]), axis=2)
            made["stream"] = to_tokens(layer_in)
            made["places"] = tuple(send_positions(owner_map, slots))
            part = (made["vectors"], made["stream"]) + made["places"]
        elif stage == 1:
            made["wide"] = gather_tokens(hold(made["stream"]).astype(bf16))
            part = made["wide"] + (seg,)
        else:
            made["grad"] = to_tokens(hold(cotangent))
            part = (made["grad"],)
        return (part,)

    own = [masters[layer] for layer in range(layers)]
    sources, points = weight_sources(own, owner_map, meanwhile)
    paired = points is not None
    wide_vectors, stream, wide_in, grad, places = (
        made[name] for name in ("vectors", "stream", "wide", "grad", "places")
    )
    weights = []

    kept = []
    for layer in range(layers):
        vec = wide_vectors[layer]
        if layer > 0:
            wide_in = gather_tokens(stream_low)
        query, keys, values, mixture, logs, send, keep, attend_blocks, ffn_blocks = attend_step(
            wide_in, sources[layer], counts, vectors[layer], seg
        )
        attend_blocks = attend_blocks.reshape(-1, tile_rows, side, side)
        ffn_blocks = ffn_blocks.reshape(-1, tile_rows, side, side)
        weights.append((attend_blocks, ffn_blocks))
        sums, message = scatter_sum(send, keep)
        if layer == 0 and paired:
            sums = (after(sums[0], *points[8:10]),) + sums[1:]
        mid_low, middle, normed_one, scale_one = norm_step(stream, sums, vec, (2, 3, 4))
        wide_mid = gather_tokens(mid_low)
        if layer == 0 and paired:
            wide_mid = wide_mid[:1] + (after(wide_mid[1], *points[10:12]),) + wide_mid[2:]
        activated, slope, send, keep = ffn_step(wide_mid, ffn_blocks, counts, up_bias[layer : layer + 1])
        sums, message = scatter_sum(send, keep, *(points[12:14] if layer == 0 and paired else ()))
        stream_low, stream, normed_two, scale_two = norm_step(middle, sums, vec, (5, 6, 7))
        kept.append(
            (wide_in, query, keys, values, mixture, logs, normed_one, scale_one, wide_mid, activated, slope, normed_two, scale_two)
        )

    vector_sums = [None] * layers
    bias_sums = [None] * layers
    sums = None
    above, came = None, ()
    for layer in reversed(range(layers)):
        vec, (attend_blocks, ffn_blocks) = wide_vectors[layer], weights[layer]
        (wide_in, query, keys, values, mixture, logs, normed_one, scale_one, wide_mid, activated, slope, normed_two, scale_two) = kept[layer]
        first = layer == 0 and paired
        grad_low, grad_two, sums_two = norm_back_step(grad, sums, normed_two, scale_two, vec, 6)
        wide_grad = gather_tokens(grad_low)
        if first:
            wide_grad = wide_grad[:1] + (after(wide_grad[1], *came),) + wide_grad[2:]
            came = reduce_next(above, slots, 2, came)
        grad_pre, bias_sum, send, keep = ffn_back_step(wide_grad, ffn_blocks, counts, slope)
        sums, message = scatter_sum(send, keep)
        ffn_jobs = [(wide_mid, (grad_pre,), n_qkv + n_out), ((activated,), wide_grad, n_qkv + n_out + n_up)]
        if first:
            sums = (after(sums[0], *came),) + sums[1:]
            came = reduce_next(above, slots, 3, came)
        else:
            ffn_grads = block_grad_step(ffn_jobs, after(places[layer], message), total, side)
            sums = (after(sums[0], ffn_grads),) + sums[1:]
        grad_low, grad_one, sums_one = norm_back_step(grad_two, sums, normed_one, scale_one, vec, 3)
        wide_first = gather_tokens(grad_low)
        if first:
            ffn_grads = block_grad_step(ffn_jobs, after(places[layer], grad_low), total, side)
            wide_first = wide_first[:1] + (after(wide_first[1], ffn_grads, *came),) + wide_first[2:]
            came = reduce_next(above, slots, 4, came)
        grad_qkv, qv_sums, send, keep = attend_back_step(
            wide_first, attend_blocks, counts, query, keys, values, logs, seg
        )
        sums, message = scatter_sum(send, keep)
        block_grads = block_grad_step(
            [(wide_in, (grad_qkv,), 0), ((mixture,), wide_first, n_qkv)],
            places[layer] if first else after(places[layer], message), total, side, ffn_grads,
        )
        grad = grad_one
        spread = jnp.concatenate([jnp.zeros_like(sums_one[:2]), sums_one, sums_two], axis=0)
        vector_sums[layer] = lax.dynamic_update_slice(spread, qv_sums, (0, index * width))
        bias_sums[layer] = lax.dynamic_update_slice(
            jnp.zeros((1, 4 * hidden), f32), bias_sum, (0, index * hidden)
        ).reshape(4 * hidden // model, model)
        if layer > 0:
            sums = (after(sums[0], block_grads),) + sums[1:]
            above = block_grads
            if paired:
                came = reduce_start(above, slots)

    small = jnp.stack([jnp.concatenate(pair, axis=0) for pair in zip(vector_sums, bias_sums)])
    small = small + swap(small, "tensor", 1)
    small = small + swap(small, "tensor", 2)
    state = (masters, left_stats, right_stats, left_roots, right_roots)
    if paired:
        before = (above[:slots], *came)
        marks = [reduce_start(after(block_grads, small, *came), slots)]
        small = small + swap(small, "dp", 2)
        marks.append(reduce_next(block_grads, slots, 2, marks[0], small))
        small = small + swap(after(small, *marks[0]), "dp", 4)
        marks.append(reduce_next(block_grads, slots, 3, marks[1], small))
        small = small + swap(after(small, *marks[1]), "dp", 1)
        came = reduce_next(block_grads, slots, 4, marks[2], small)
        parts = (block_grads[:slots], *came)
        input_grad, layer_out = (
            from_tokens(values, (marks[0][0], marks[1][0]))
            for values in (grad + sums[0][:quarter] + sums[1][:quarter].astype(f32) + sums[2].astype(f32), stream)
        )
        updated = update_step(before, 1, (after(masters, *marks[1]),) + state[1:], None)
        updated = update_step(parts, 0, state, updated)
    else:
        small = lax.psum(small, "dp")
        input_grad, layer_out = (
            from_tokens(values)
            for values in (grad + sums[0][:quarter] + sums[1][:quarter].astype(f32) + sums[2].astype(f32), stream)
        )
        updated = None
        for layer, grads in ((1, above), (0, block_grads)):
            mine = lax.psum_scatter(grads, "dp", scatter_dimension=0, tiled=True)
            updated = update_step((mine,), layer, state, updated)
    vector_grads = lax.dynamic_slice(small[:, :8], (0, 0, index * width), (layers, 8, width))
    up_bias_grads = lax.dynamic_slice(
        small[:, 8:].reshape(layers, 4 * hidden), (0, index * hidden), (layers, hidden)
    )
    reduced, left_new, right_new, new_weights = updated
    vector_rate = 0.5 / math.sqrt(tokens * lax.axis_size("dp"))
    return (
        layer_out,
        input_grad,
        reduced,
        left_new,
        right_new,
        new_weights,
        vector_grads,
        vectors - vector_rate * vector_grads,
        up_bias_grads,
        up_bias - vector_rate * up_bias_grads,
    )


def solution(mesh):
    owned = P(None, ("dp", "tensor"), None, None)
    return jax.shard_map(
        body,
        mesh=mesh,
        in_specs=(
            P("dp", "tensor"),
            P("dp", "tensor"),
            P("dp", None),
            P(),
            owned,
            owned,
            owned,
            owned,
            owned,
            P(None, None, "tensor"),
            P(None, "tensor"),
        ),
        out_specs=(
            P("dp", "tensor"),
            P("dp", "tensor"),
            owned,
            owned,
            owned,
            owned,
            P(None, None, "tensor"),
            P(None, None, "tensor"),
            P(None, "tensor"),
            P(None, "tensor"),
        ),
        check_vma=False,
    )
```

```python
import functools
import math

import jax
import jax.numpy as jnp
from jax import lax
from jax.experimental import pallas as pl
from jax.experimental.pallas import tpu as pltpu
from jax.sharding import PartitionSpec as P

HD = 64
eps_norm = 1e-12
stat_decay = 0.5
update_rate = 0.5
f32 = jnp.float32
bf16 = jnp.bfloat16

LAST = (((1,), (1,)), ((), ()))
FIRST = (((0,), (0,)), ((), ()))


def vmem_spec(count):
    return [pl.BlockSpec(memory_space=pltpu.VMEM)] * count


def params(mib=40):
    return pltpu.CompilerParams(vmem_limit_bytes=mib * 1024 * 1024)


def cost(microseconds):
    return pl.CostEstimate(flops=0, bytes_accessed=int(microseconds * 3.4e6), transcendentals=0)


def shape(dims, dtype):
    return jax.ShapeDtypeStruct(dims, dtype)


def cat_rows(refs):
    return jnp.concatenate([ref[...] for ref in refs], axis=0)


def matrix(ref, rows, cols):
    width = ref.shape[1]
    return jnp.concatenate(
        [
            jnp.concatenate(
                [ref[(r * cols + c) // width, (r * cols + c) % width] for c in range(cols)], axis=1
            )
            for r in range(rows)
        ],
        axis=0,
    )


def flat_matrix(ref, base, rows, cols):
    return jnp.concatenate(
        [jnp.concatenate([ref[base + r * cols + c] for c in range(cols)], axis=1) for r in range(rows)], axis=0
    )


def swap(values, axis, flip):
    count = lax.axis_size(axis)
    return lax.ppermute(values, axis, [(i, i ^ flip) for i in range(count)])


def gather_tokens(piece):
    far = swap(piece, "tensor", 2)
    near = swap(piece, "tensor", 1)
    both = swap(far, "tensor", 1)
    return (piece, far, near, both)


def scatter_sum(send, keep, *marks):
    rows = send.shape[0] // 2
    first = swap(send, "tensor", 1)
    message = (keep[rows:] + first[rows:].astype(f32)).astype(bf16)
    if marks:
        message = after(message, *marks)
    return (keep, first, swap(message, "tensor", 2)), message


def by_index(relative):
    index = lax.axis_index("tensor")
    core, x_pos = index % 2 == 1, index // 2 == 1
    r0, r1, r2, r3 = relative
    a0, a1 = jnp.where(core, r1, r0), jnp.where(core, r0, r1)
    a2, a3 = jnp.where(core, r3, r2), jnp.where(core, r2, r3)
    return [
        jnp.where(x_pos, a2, a0),
        jnp.where(x_pos, a3, a1),
        jnp.where(x_pos, a0, a2),
        jnp.where(x_pos, a1, a3),
    ]


def to_tokens(values):
    rows, width = values.shape
    quarter = rows // 4
    r0, r1, r2, r3 = by_index([values[g * quarter : (g + 1) * quarter] for g in range(4)])
    got = swap(jnp.stack([r2, r3]), "tensor", 2)
    near = swap(jnp.stack([r1, got[1]]), "tensor", 1)
    return jnp.concatenate(by_index([r0, near[0], got[0], near[1]]), axis=1)


def from_tokens(values, marks=None):
    width = values.shape[1] // 4
    r0, r1, r2, r3 = by_index([values[:, g * width : (g + 1) * width] for g in range(4)])
    near = jnp.stack([r1, r3])
    got = swap(near if marks is None else after(near, marks[0]), "tensor", 1)
    rest = jnp.stack([r2, got[1]])
    far = swap(rest if marks is None else after(rest, marks[1]), "tensor", 2)
    return jnp.concatenate(by_index([r0, got[0], far[0], far[1]]), axis=0)


ring = (0, 2, 4, 6, 7, 5, 3, 1)


def ring_place():
    index = lax.axis_index("dp")
    return jnp.where(index % 2 == 0, index // 2, 7 - index // 2)


def owner_place(owner):
    return jnp.where(owner % 2 == 0, owner // 2, 7 - owner // 2)


def turn(values, way):
    return lax.ppermute(values, "dp", [(ring[p], ring[(p + way) % 8]) for p in range(8)])


def after(values, *others):
    return lax.optimization_barrier((values,) + tuple(others))[0]


def has_ring():
    return lax.axis_size("dp") == 8


def weight_sources(own, owner_map, meanwhile):
    layers, total = owner_map.shape
    slots = own[0].shape[0]
    half = slots // 2
    positions = jnp.arange(total, dtype=jnp.int32)
    hits = owner_map[:, None, :] == positions[None, :, None]
    inverse = jnp.sum(jnp.where(hits, positions[None, None, :], 0), axis=2).astype(jnp.int32)
    if not has_ring():
        wholes = [lax.all_gather(values.astype(bf16), "dp", axis=0, tiled=True) for values in own]
        for stage in range(3):
            meanwhile(stage, None)
        return [((whole,), ((0, 0),), row[None, :]) for whole, row in zip(wholes, inverse)], None
    ways = jnp.array([0, -1, -2, -3, 1, 2, 3, 4], jnp.int32)
    spots = tuple((j, first) for j in range(7) for first in (0, half)) + ((7, 0), (8, 0))
    target = (ring_place() + ways) % 8
    device = jnp.where(target < 4, 2 * target, 15 - 2 * target)
    mask = device[None, :, None, None] == jnp.arange(8, dtype=jnp.int32)[None, None, :, None]
    rows = jnp.sum(jnp.where(mask, inverse.reshape(layers, 1, 8, slots), 0), axis=2)
    tables = [table for table in rows.reshape(layers, 16, half).astype(jnp.int32)]
    result, points, last, beside = [], [], (), ()
    for layer in range(layers):
        mine = own[layer] if layer == 0 else after(own[layer], points[0])
        mine = mine.astype(bf16)
        start = after(mine, *last) if last else mine
        behind, ahead = [turn(start, 1)], [turn(start, -1)]
        for step in range(3):
            if layer == 0:
                beside += meanwhile(step, behind[-2] if step else None)
            done = (behind[-1], ahead[-1]) + (beside[-1] if layer == 0 else ())
            points.append(behind[-1])
            points.append(ahead[-1])
            next_behind, next_ahead = after(behind[-1], *done), after(ahead[-1], *done)
            if step == 2:
                next_behind, next_ahead = next_behind[:half], next_ahead[half:]
            behind.append(turn(next_behind, 1))
            ahead.append(turn(next_ahead, -1))
        last = (behind[3], ahead[3])
        points += last
        result.append(((mine, *behind[:3], *ahead[:3], behind[3], ahead[3]), spots, tables[layer]))
    return result, points


def send_positions(owner_row, slots):
    if not has_ring():
        return owner_row
    way = (owner_place(owner_row // slots) - ring_place()) % 8
    return (way * slots + owner_row % slots).astype(jnp.int32)


def reduce_start(grads, slots):
    half = slots // 2
    return turn(grads[4 * slots : 4 * slots + half], 1), turn(grads[4 * slots + half : 5 * slots], -1)


def reduce_next(grads, slots, step, came, *marks):
    forward = grads[(5 - step) * slots : (6 - step) * slots].astype(f32)
    backward = grads[(3 + step) * slots : (4 + step) * slots].astype(f32)
    ahead, behind = came[0].astype(f32), came[1].astype(f32)
    if step == 2:
        half = slots // 2
        forward = jnp.concatenate([forward[:half] + ahead, forward[half:]])
        backward = jnp.concatenate([backward[:half], backward[half:] + behind])
    else:
        forward, backward = forward + ahead, backward + behind
    forward, backward = lax.optimization_barrier((forward.astype(bf16), backward.astype(bf16), *marks))[:2]
    return turn(forward, 1), turn(backward, -1)


def norm_kernel(base, keep, first, second, vec, low_out, full_out, normed_out, scale_out, *, rows):
    bias, gain, shift = rows
    hidden = (
        base[...]
        + keep[...]
        + first[...].astype(f32)
        + second[...].astype(f32)
        + vec[bias : bias + 1, :]
    )
    center = jnp.mean(hidden, axis=1, keepdims=True)
    centred = hidden - center
    spread = jnp.mean(centred * centred, axis=1, keepdims=True)
    scale = lax.rsqrt(spread + eps_norm)
    normed = centred * scale
    full = normed * vec[gain : gain + 1, :] + vec[shift : shift + 1, :]
    full_out[...] = full
    low_out[...] = full.astype(bf16)
    normed_out[...] = normed
    scale_out[...] = scale


def top_half(array):
    return pl.BlockSpec((array.shape[0] // 2, array.shape[1]), lambda i: (0, 0))


def whole_spec(array):
    nd = len(array.shape)
    return pl.BlockSpec(tuple(array.shape), lambda i, nd=nd: (0,) * nd)


def norm_step(base, sums, vec, rows):
    keep, first, second = sums
    tokens, width = base.shape
    outs = [
        shape((tokens, width), bf16),
        shape((tokens, width), f32),
        shape((tokens, width), f32),
        shape((tokens, 1), f32),
    ]
    return pl.pallas_call(
        functools.partial(norm_kernel, rows=rows),
        grid=(1,),
        in_specs=[whole_spec(base), top_half(keep), top_half(first), whole_spec(second), whole_spec(vec)],
        out_specs=[whole_spec(o) for o in outs],
        out_shape=outs,
        compiler_params=params(12),
        cost_estimate=cost(1.2),
        name="norm",
    )(base, keep, first, second, vec)


def norm_back_kernel(*refs, gain, summed):
    if summed:
        base, keep, first, second, normed, scale, vec, low_out, full_out, sums_out = refs
        grad = base[...] + keep[...] + first[...].astype(f32) + second[...].astype(f32)
    else:
        base, normed, scale, vec, low_out, full_out, sums_out = refs
        grad = base[...]
    value = normed[...]
    scaled = grad * vec[gain : gain + 1, :]
    mean_grad = jnp.mean(scaled, axis=1, keepdims=True)
    mean_cross = jnp.mean(scaled * value, axis=1, keepdims=True)
    result = scale[...] * (scaled - mean_grad - value * mean_cross)
    full_out[...] = result
    low_out[...] = result.astype(bf16)
    sums_out[0:1, :] = jnp.sum(result, axis=0, keepdims=True)
    sums_out[1:2, :] = jnp.sum(grad * value, axis=0, keepdims=True)
    sums_out[2:3, :] = jnp.sum(grad, axis=0, keepdims=True)


def norm_back_step(base, sums, normed, scale, vec, gain):
    tokens, width = base.shape
    outs = [shape((tokens, width), bf16), shape((tokens, width), f32), shape((3, width), f32)]
    operands = [base]
    specs = [whole_spec(base)]
    if sums is not None:
        keep, first, second = sums
        operands += [keep, first, second]
        specs += [top_half(keep), top_half(first), whole_spec(second)]
    operands += [normed, scale, vec]
    specs += [whole_spec(normed), whole_spec(scale), whole_spec(vec)]
    return pl.pallas_call(
        functools.partial(norm_back_kernel, gain=gain, summed=sums is not None),
        grid=(1,),
        in_specs=specs,
        out_specs=[whole_spec(o) for o in outs],
        out_shape=outs,
        compiler_params=params(12),
        cost_estimate=cost(1.5),
        name="norm_back",
    )(*operands)


def store_sums(total, send_out, keep_out):
    half = total.shape[0] // 2
    send_out[...] = total[half:].astype(bf16)
    keep_out[...] = total[:half]


def start_blocks(sources, spots, table, stage, sem):
    slots = table.shape[1]
    for row, (which, first) in enumerate(spots):

        @pl.loop(0, slots, unroll=min(slots, 24))
        def _(s, row=row, which=which, first=first):
            pltpu.make_async_copy(sources[which].at[first + s], stage.at[table[row, s]], sem).start()


def segment_bias(seg):
    row = seg[...]
    column = jnp.transpose(jnp.broadcast_to(row, (128, row.shape[1])))[:, 0:1]
    return jnp.where(column == row, 0.0, -1e30)


def attend_kernel(
    count, spots, n_qkv, n_out, table, *refs
):
    sources = refs[:count]
    (
        p0, p1, p2, p3, vec, seg,
        query_out, key_out, value_out, mix_out, log_out, send_out, keep_out, attend_out, ffn_out,
        bias, stage, sems,
    ) = refs[count:]
    start_blocks(sources, spots, table, stage, sems.at[0])
    wide = cat_rows((p0, p1, p2, p3))
    bias[...] = segment_bias(seg)
    pltpu.make_async_copy(stage, stage, sems.at[0]).wait()
    cut = n_qkv + n_out
    copies = (
        pltpu.make_async_copy(stage.at[pl.ds(0, cut)], attend_out, sems.at[1]),
        pltpu.make_async_copy(stage.at[pl.ds(cut, ffn_out.shape[0])], ffn_out, sems.at[2]),
    )
    for copy in copies:
        copy.start()
    tokens, model = wide.shape
    width = query_out.shape[1]
    tile = stage.shape[-1]
    projected = jnp.dot(
        wide, flat_matrix(stage, 0, model // tile, 3 * width // tile), preferred_element_type=f32
    )
    query = (projected[:, :width] + vec[0:1, :]).astype(bf16) * jnp.asarray(HD**-0.5, bf16)
    keys = projected[:, width : 2 * width].astype(bf16)
    values = (projected[:, 2 * width :] + vec[1:2, :]).astype(bf16)
    query_out[...] = query
    key_out[...] = keys
    value_out[...] = values
    lane = lax.broadcasted_iota(jnp.int32, (tokens, 128), 1)
    logs = jnp.zeros((tokens, 128), f32)
    mixes = []
    for pair in range(width // 128):
        cols = slice(pair * 128, pair * 128 + 128)
        halves = []
        for part in range(128 // HD):
            inside = (lane >= part * HD) & (lane < part * HD + HD)
            one = jnp.where(inside, query[:, cols], jnp.zeros((), bf16))
            scores = lax.dot_general(one, keys[:, cols], LAST, preferred_element_type=f32) + bias[...]
            top = jnp.max(scores, axis=1, keepdims=True)
            exponent = jnp.exp(scores - top)
            total = jnp.sum(exponent, axis=1, keepdims=True)
            attention = (exponent * (1.0 / total)).astype(bf16)
            halves.append((inside, jnp.dot(attention, values[:, cols], preferred_element_type=f32)))
            logs = jnp.where(lane == pair * (128 // HD) + part, top + jnp.log(total), logs)
        mixed = halves[0][1]
        for inside, other in halves[1:]:
            mixed = jnp.where(inside, other, mixed)
        mixes.append(mixed.astype(bf16))
    mixture = jnp.concatenate(mixes, axis=1)
    mix_out[...] = mixture
    log_out[...] = jnp.transpose(logs)[0:8, :]
    total = jnp.dot(
        mixture, flat_matrix(stage, n_qkv, width // tile, model // tile), preferred_element_type=f32
    )
    store_sums(total, send_out, keep_out)
    for copy in copies:
        copy.wait()


def block_rows(array, start, count):
    return pl.BlockSpec((count,) + tuple(array.shape[1:]), lambda i: (start // count, 0, 0, 0))


def attend_step(pieces, weights, counts, vec, seg):
    quarter, model = pieces[0].shape
    tokens, width = 4 * quarter, vec.shape[1]
    n_qkv, n_out, n_up = counts
    arrays, spots, table = weights
    side = arrays[0].shape[-1]
    total = n_qkv + n_out + 2 * n_up
    outs = [
        shape((tokens, width), bf16),
        shape((tokens, width), bf16),
        shape((tokens, width), bf16),
        shape((tokens, width), bf16),
        shape((8, tokens), f32),
        shape((tokens // 2, model), bf16),
        shape((tokens // 2, model), f32),
        shape((n_qkv + n_out, side, side), bf16),
        shape((2 * n_up, side, side), bf16),
    ]
    operands = list(pieces) + [vec, seg]
    return pl.pallas_call(
        functools.partial(attend_kernel, len(arrays), spots, n_qkv, n_out),
        grid_spec=pltpu.PrefetchScalarGridSpec(
            num_scalar_prefetch=1,
            grid=(),
            in_specs=[pl.BlockSpec(memory_space=pl.ANY)] * len(arrays) + vmem_spec(len(operands)),
            out_specs=vmem_spec(7) + [pl.BlockSpec(memory_space=pl.ANY)] * 2,
            scratch_shapes=[
                pltpu.VMEM((tokens, tokens), f32),
                pltpu.VMEM((total, side, side), bf16),
                pltpu.SemaphoreType.DMA((3,)),
            ],
        ),
        out_shape=outs,
        compiler_params=params(60),
        cost_estimate=cost(11),
        name="attend",
    )(table, *arrays, *operands)


def attend_back_kernel(
    p0, p1, p2, p3, w_out, w_qkv, query_in, key_in, value_in, log_in, seg,
    grad_out, sums_out, send_out, keep_out, bias,
):
    wide = cat_rows((p0, p1, p2, p3))
    tokens, model = wide.shape
    width = query_in.shape[1]
    tile = w_qkv.shape[-1]
    grad_mix = lax.dot_general(
        wide, matrix(w_out, width // tile, model // tile), LAST, preferred_element_type=f32
    ).astype(bf16)
    bias[...] = segment_bias(seg)
    lane = lax.broadcasted_iota(jnp.int32, (tokens, 128), 1)
    grads = ([], [], [])
    for pair in range(width // 128):
        cols = slice(pair * 128, pair * 128 + 128)
        query, keys, values, mix = query_in[:, cols], key_in[:, cols], value_in[:, cols], grad_mix[:, cols]
        picked = [None, None, None]
        for part in range(128 // HD):
            head = pair * (128 // HD) + part
            inside = (lane >= part * HD) & (lane < part * HD + HD)
            zero = jnp.zeros((), bf16)
            scores = (
                lax.dot_general(jnp.where(inside, keys, zero), query, LAST, preferred_element_type=f32)
                + bias[...]
            )
            attention = jnp.exp(scores - log_in[head : head + 1, :])
            pulled = lax.dot_general(jnp.where(inside, values, zero), mix, LAST, preferred_element_type=f32)
            inner = jnp.sum(attention * pulled, axis=0, keepdims=True)
            grad_scores = (attention * (pulled - inner)).astype(bf16)
            three = (
                lax.dot_general(grad_scores, keys, FIRST, preferred_element_type=f32) * (HD**-0.5),
                jnp.dot(grad_scores, query, preferred_element_type=f32),
                jnp.dot(attention.astype(bf16), mix, preferred_element_type=f32),
            )
            for which in range(3):
                if part == 0:
                    picked[which] = three[which]
                else:
                    picked[which] = jnp.where(inside, three[which], picked[which])
        for which in range(3):
            grads[which].append(picked[which].astype(bf16))
    joined = [jnp.concatenate(g, axis=1) for g in grads]
    every = jnp.concatenate(joined, axis=1)
    grad_out[...] = every
    sums_out[0:1, :] = jnp.sum(joined[0].astype(f32), axis=0, keepdims=True)
    sums_out[1:2, :] = jnp.sum(joined[2].astype(f32), axis=0, keepdims=True)
    total = lax.dot_general(
        every, matrix(w_qkv, model // tile, 3 * width // tile), LAST, preferred_element_type=f32
    )
    store_sums(total, send_out, keep_out)


def attend_back_step(pieces, blocks, counts, query, keys, values, logs, seg):
    quarter, model = pieces[0].shape
    tokens, width = query.shape
    n_qkv, n_out, n_up = counts
    per = blocks.shape[1]
    outs = [
        shape((tokens, 3 * width), bf16),
        shape((2, width), f32),
        shape((tokens // 2, model), bf16),
        shape((tokens // 2, model), f32),
    ]
    return pl.pallas_call(
        attend_back_kernel,
        grid=(1,),
        in_specs=[whole_spec(p) for p in pieces]
        + [block_rows(blocks, n_qkv // per, n_out // per), block_rows(blocks, 0, n_qkv // per)]
        + [whole_spec(a) for a in (query, keys, values, logs, seg)],
        out_specs=[whole_spec(o) for o in outs],
        out_shape=outs,
        scratch_shapes=[pltpu.VMEM((tokens, tokens), f32)],
        compiler_params=params(32),
        cost_estimate=cost(6.5),
        name="attend_back",
    )(*pieces, blocks, blocks, query, keys, values, logs, seg)


def ffn_kernel(p0, p1, p2, p3, w_up, w_down, bias, act_out, slope_out, send_out, keep_out):
    wide = cat_rows((p0, p1, p2, p3))
    model = wide.shape[1]
    tile = w_up.shape[-1]
    cols = act_out.shape[1] // tile
    pre = jnp.dot(wide, matrix(w_up, model // tile, cols), preferred_element_type=f32) + bias[...]
    cdf = 0.5 + 0.5 * lax.erf(pre * (0.5**0.5))
    slope_out[...] = cdf + pre * (jnp.exp(-0.5 * pre * pre) * (1.0 / math.sqrt(2.0 * math.pi)))
    activated = (pre * cdf).astype(bf16)
    act_out[...] = activated
    total = jnp.dot(activated, matrix(w_down, cols, model // tile), preferred_element_type=f32)
    store_sums(total, send_out, keep_out)


def fixed(array):
    nd = len(array.shape)
    return pl.BlockSpec(tuple(array.shape), lambda i, nd=nd: (0,) * nd)


def ffn_specs(blocks, counts, chunk_blocks):
    n_qkv, n_out, n_up = counts
    per = blocks.shape[1]
    side = blocks.shape[2]
    up_row = 0
    up_rows = n_up // per
    down_row = n_up // per
    up_spec = pl.BlockSpec((up_rows, chunk_blocks, side, side), lambda i: (up_row // up_rows, i, 0, 0))
    down_spec = pl.BlockSpec((chunk_blocks, per, side, side), lambda i: (down_row // chunk_blocks + i, 0, 0, 0))
    return up_spec, down_spec


def ffn_step(pieces, blocks, counts, up_bias):
    quarter, model = pieces[0].shape
    tokens, hidden = 4 * quarter, up_bias.shape[1]
    up_spec, down_spec = ffn_specs(blocks, counts, hidden // blocks.shape[2])
    outs = [
        shape((tokens, hidden), bf16),
        shape((tokens, hidden), f32),
        shape((tokens // 2, model), bf16),
        shape((tokens // 2, model), f32),
    ]
    return pl.pallas_call(
        ffn_kernel,
        grid=(1,),
        in_specs=[fixed(p) for p in pieces]
        + [up_spec, down_spec, fixed(up_bias)],
        out_specs=[fixed(o) for o in outs],
        out_shape=outs,
        compiler_params=params(24),
        cost_estimate=cost(5),
        name="ffn",
    )(*pieces, blocks, blocks, up_bias)


def ffn_back_kernel(p0, p1, p2, p3, w_up, w_down, slope, grad_out, bias_out, send_out, keep_out):
    wide = cat_rows((p0, p1, p2, p3))
    model = wide.shape[1]
    tile = w_up.shape[-1]
    cols = grad_out.shape[1] // tile
    pulled = lax.dot_general(wide, matrix(w_down, cols, model // tile), LAST, preferred_element_type=f32)
    grad = (pulled * slope[...]).astype(bf16)
    grad_out[...] = grad
    bias_out[...] = jnp.sum(grad.astype(f32), axis=0, keepdims=True)
    total = lax.dot_general(grad, matrix(w_up, model // tile, cols), LAST, preferred_element_type=f32)
    store_sums(total, send_out, keep_out)


def ffn_back_step(pieces, blocks, counts, slope):
    quarter, model = pieces[0].shape
    tokens, hidden = slope.shape
    up_spec, down_spec = ffn_specs(blocks, counts, hidden // blocks.shape[2])
    outs = [
        shape((tokens, hidden), bf16),
        shape((1, hidden), f32),
        shape((tokens // 2, model), bf16),
        shape((tokens // 2, model), f32),
    ]
    return pl.pallas_call(
        ffn_back_kernel,
        grid=(1,),
        in_specs=[fixed(p) for p in pieces] + [up_spec, down_spec, fixed(slope)],
        out_specs=[fixed(o) for o in outs],
        out_shape=outs,
        compiler_params=params(24),
        cost_estimate=cost(7),
        name="ffn_back",
    )(*pieces, blocks, blocks, slope)


def weight_grad_jobs(jobs, operands, side, store):
    at = 0
    for left_count, right_count, base in jobs:
        left = operands[at : at + left_count]
        right = operands[at + left_count : at + left_count + right_count]
        at += left_count + right_count
        columns = cat_rows(right)
        per = columns.shape[1] // side
        width = left[0].shape[1]
        chunk = min(width, 2 * side)
        for start in range(0, width, chunk):
            rows = jnp.concatenate([ref[:, start : start + chunk] for ref in left], axis=0)
            result = lax.dot_general(rows, columns, FIRST, preferred_element_type=f32).astype(bf16)
            for i in range(chunk // side):
                for j in range(per):
                    store(
                        base + (start // side + i) * per + j,
                        result[i * side : (i + 1) * side, j * side : (j + 1) * side],
                    )


def job_parts(jobs, side):
    operands = [a for left, right, base in jobs for a in left + right]
    layout = tuple((len(left), len(right), base) for left, right, base in jobs)
    blocks = sum(left[0].shape[1] // side * (right[0].shape[1] // side) for left, right, base in jobs)
    tokens = sum(a.shape[0] for a in jobs[0][0])
    return operands, layout, blocks, tokens


def block_grad_kernel(jobs, used, chained, place, *refs):
    out, stage, sem = refs[used + chained :]
    slots = []

    def store(block, value):
        slot = len(slots)
        slots.append(block)
        stage[slot] = value
        pltpu.make_async_copy(stage.at[slot], out.at[place[block]], sem).start()

    weight_grad_jobs(jobs, refs[:used], stage.shape[-1], store)
    pltpu.make_async_copy(stage, out.at[pl.ds(0, stage.shape[0])], sem).wait()


def block_grad_step(jobs, place, total, side, target=None):
    operands, layout, blocks, tokens = job_parts(jobs, side)
    chained = [] if target is None else [target]
    return pl.pallas_call(
        functools.partial(block_grad_kernel, layout, len(operands), len(chained)),
        grid_spec=pltpu.PrefetchScalarGridSpec(
            num_scalar_prefetch=1,
            grid=(),
            in_specs=vmem_spec(len(operands)) + [pl.BlockSpec(memory_space=pl.ANY)] * len(chained),
            out_specs=pl.BlockSpec(memory_space=pl.ANY),
            scratch_shapes=[pltpu.VMEM((blocks, side, side), bf16), pltpu.SemaphoreType.DMA],
        ),
        out_shape=shape((total, side, side), bf16),
        input_output_aliases={1 + len(operands): 0} if chained else {},
        compiler_params=params(54),
        cost_estimate=cost(4 if chained else 6),
        name="block_grad",
    )(place, *operands, *chained)


def update_kernel(part_count, chained, *refs):
    parts = refs[:part_count]
    masters, left, right, left_root, right_root = refs[part_count : part_count + 5]
    grad_out, left_out, right_out, weight_out = refs[part_count + 5 + chained :]
    grad = parts[0][...].astype(f32)
    for part in parts[1:]:
        grad = grad + part[...].astype(f32)
    grad_out[0] = grad
    for b in range(grad.shape[0]):
        low = grad[b].astype(bf16)
        left_out[0, b] = stat_decay * left[0, b] + (1.0 - stat_decay) * lax.dot_general(
            low, low, LAST, preferred_element_type=f32
        )
        right_out[0, b] = stat_decay * right[0, b] + (1.0 - stat_decay) * lax.dot_general(
            low, low, FIRST, preferred_element_type=f32
        )
        inner = jnp.dot(low, right_root[0, b].astype(bf16), preferred_element_type=f32)
        outer = jnp.dot(left_root[0, b].astype(bf16), inner.astype(bf16), preferred_element_type=f32)
        weight_out[0, b] = masters[0, b] - update_rate * outer


def update_step(parts, layer, state, previous):
    layers, slots, side, _ = state[0].shape
    group = 6 if slots % 6 == 0 else slots
    one = pl.BlockSpec((1, group, side, side), lambda i: (layer, i, 0, 0))
    chained = [] if previous is None else list(previous)
    aliases = {len(parts) + 5 + k: k for k in range(len(chained))}
    return pl.pallas_call(
        functools.partial(update_kernel, len(parts), len(chained)),
        grid=(slots // group,),
        in_specs=[pl.BlockSpec((group, side, side), lambda i: (i, 0, 0))] * len(parts)
        + [one] * 5
        + [pl.BlockSpec(memory_space=pl.ANY)] * len(chained),
        out_specs=[one] * 4,
        out_shape=[shape(state[0].shape, f32)] * 4,
        input_output_aliases=aliases,
        compiler_params=params(60),
        cost_estimate=cost(10),
        name="update",
    )(*parts, *state, *chained)


def body(
    layer_in,
    cotangent,
    segment_ids,
    owner_map,
    masters,
    left_stats,
    right_stats,
    left_roots,
    right_roots,
    vectors,
    up_bias,
):
    layers, slots, side = masters.shape[0], masters.shape[1], masters.shape[-1]
    tokens, width = layer_in.shape
    model = width * lax.axis_size("tensor")
    hidden = up_bias.shape[1]
    tile_rows = model // side
    n_qkv = tile_rows * (3 * width // side)
    n_out = width // side * tile_rows
    n_up = tile_rows * (hidden // side)
    counts = (n_qkv, n_out, n_up)
    total = owner_map.shape[1]
    index = lax.axis_index("tensor")
    quarter = tokens // 4

    segments = jnp.concatenate(
        by_index([segment_ids[:, g * quarter : (g + 1) * quarter] for g in range(4)]), axis=1
    )
    segments = jnp.concatenate(
        [segments[:, g * quarter : (g + 1) * quarter] for g in (0, 2, 1, 3)], axis=1
    )
    seg = segments.astype(f32)

    made = {}

    def meanwhile(stage, mark):
        def hold(values):
            return values if mark is None else after(values, mark)

        if stage == 0:
            near = swap(vectors, "tensor", 1)
            far = swap(jnp.stack([vectors, near]), "tensor", 2)
            made["vectors"] = jnp.concatenate(by_index([vectors, near, far[0], far[1]]), axis=2)
            made["stream"] = to_tokens(layer_in)
            made["places"] = tuple(send_positions(owner_map, slots))
            part = (made["vectors"], made["stream"]) + made["places"]
        elif stage == 1:
            made["wide"] = gather_tokens(hold(made["stream"]).astype(bf16))
            part = made["wide"] + (seg,)
        else:
            made["grad"] = to_tokens(hold(cotangent))
            part = (made["grad"],)
        return (part,)

    own = [masters[layer] for layer in range(layers)]
    sources, points = weight_sources(own, owner_map, meanwhile)
    paired = points is not None
    wide_vectors, stream, wide_in, grad, places = (
        made[name] for name in ("vectors", "stream", "wide", "grad", "places")
    )
    weights = []

    kept = []
    for layer in range(layers):
        vec = wide_vectors[layer]
        if layer > 0:
            wide_in = gather_tokens(stream_low)
        query, keys, values, mixture, logs, send, keep, attend_blocks, ffn_blocks = attend_step(
            wide_in, sources[layer], counts, vectors[layer], seg
        )
        attend_blocks = attend_blocks.reshape(-1, tile_rows, side, side)
        ffn_blocks = ffn_blocks.reshape(-1, tile_rows, side, side)
        weights.append((attend_blocks, ffn_blocks))
        sums, message = scatter_sum(send, keep)
        if layer == 0 and paired:
            sums = (after(sums[0], *points[8:10]),) + sums[1:]
        mid_low, middle, normed_one, scale_one = norm_step(stream, sums, vec, (2, 3, 4))
        wide_mid = gather_tokens(mid_low)
        if layer == 0 and paired:
            wide_mid = wide_mid[:1] + (after(wide_mid[1], *points[10:12]),) + wide_mid[2:]
        activated, slope, send, keep = ffn_step(wide_mid, ffn_blocks, counts, up_bias[layer : layer + 1])
        sums, message = scatter_sum(send, keep, *(points[12:14] if layer == 0 and paired else ()))
        stream_low, stream, normed_two, scale_two = norm_step(middle, sums, vec, (5, 6, 7))
        kept.append(
            (wide_in, query, keys, values, mixture, logs, normed_one, scale_one, wide_mid, activated, slope, normed_two, scale_two)
        )

    vector_sums = [None] * layers
    bias_sums = [None] * layers
    sums = None
    above, came = None, ()
    for layer in reversed(range(layers)):
        vec, (attend_blocks, ffn_blocks) = wide_vectors[layer], weights[layer]
        (wide_in, query, keys, values, mixture, logs, normed_one, scale_one, wide_mid, activated, slope, normed_two, scale_two) = kept[layer]
        first = layer == 0 and paired
        grad_low, grad_two, sums_two = norm_back_step(grad, sums, normed_two, scale_two, vec, 6)
        wide_grad = gather_tokens(grad_low)
        if first:
            wide_grad = wide_grad[:1] + (after(wide_grad[1], *came),) + wide_grad[2:]
            came = reduce_next(above, slots, 2, came)
        grad_pre, bias_sum, send, keep = ffn_back_step(wide_grad, ffn_blocks, counts, slope)
        sums, message = scatter_sum(send, keep)
        ffn_jobs = [(wide_mid, (grad_pre,), n_qkv + n_out), ((activated,), wide_grad, n_qkv + n_out + n_up)]
        if first:
            sums = (after(sums[0], *came),) + sums[1:]
            came = reduce_next(above, slots, 3, came)
        else:
            ffn_grads = block_grad_step(ffn_jobs, after(places[layer], message), total, side)
            sums = (after(sums[0], ffn_grads),) + sums[1:]
        grad_low, grad_one, sums_one = norm_back_step(grad_two, sums, normed_one, scale_one, vec, 3)
        wide_first = gather_tokens(grad_low)
        if first:
            ffn_grads = block_grad_step(ffn_jobs, after(places[layer], grad_low), total, side)
            wide_first = wide_first[:1] + (after(wide_first[1], ffn_grads, *came),) + wide_first[2:]
            came = reduce_next(above, slots, 4, came)
        grad_qkv, qv_sums, send, keep = attend_back_step(
            wide_first, attend_blocks, counts, query, keys, values, logs, seg
        )
        sums, message = scatter_sum(send, keep)
        block_grads = block_grad_step(
            [(wide_in, (grad_qkv,), 0), ((mixture,), wide_first, n_qkv)],
            places[layer] if first else after(places[layer], message), total, side, ffn_grads,
        )
        grad = grad_one
        spread = jnp.concatenate([jnp.zeros_like(sums_one[:2]), sums_one, sums_two], axis=0)
        vector_sums[layer] = lax.dynamic_update_slice(spread, qv_sums, (0, index * width))
        bias_sums[layer] = lax.dynamic_update_slice(
            jnp.zeros((1, 4 * hidden), f32), bias_sum, (0, index * hidden)
        ).reshape(4 * hidden // model, model)
        if layer > 0:
            sums = (after(sums[0], block_grads),) + sums[1:]
            above = block_grads
            if paired:
                came = reduce_start(above, slots)

    small = jnp.stack([jnp.concatenate(pair, axis=0) for pair in zip(vector_sums, bias_sums)])
    small = small + swap(small, "tensor", 1)
    small = small + swap(small, "tensor", 2)
    state = (masters, left_stats, right_stats, left_roots, right_roots)
    if paired:
        before = (above[:slots], *came)
        marks = [reduce_start(after(block_grads, *came), slots)]
        small = small + swap(small, "dp", 2)
        marks.append(reduce_next(block_grads, slots, 2, marks[0], small))
        marks.append(reduce_next(block_grads, slots, 3, marks[1]))
        small = small + swap(after(small, *marks[0]), "dp", 4)
        came = reduce_next(block_grads, slots, 4, marks[2], small)
        small = small + swap(after(small, *marks[1]), "dp", 1)
        parts = (after(block_grads[:slots], small), *came)
        input_grad, layer_out = (
            from_tokens(values, (marks[0][0], marks[1][0]))
            for values in (grad + sums[0][:quarter] + sums[1][:quarter].astype(f32) + sums[2].astype(f32), stream)
        )
        updated = update_step(before, 1, (after(masters, *marks[1]),) + state[1:], None)
        updated = update_step(parts, 0, state, updated)
    else:
        small = lax.psum(small, "dp")
        input_grad, layer_out = (
            from_tokens(values)
            for values in (grad + sums[0][:quarter] + sums[1][:quarter].astype(f32) + sums[2].astype(f32), stream)
        )
        updated = None
        for layer, grads in ((1, above), (0, block_grads)):
            mine = lax.psum_scatter(grads, "dp", scatter_dimension=0, tiled=True)
            updated = update_step((mine,), layer, state, updated)
    vector_grads = lax.dynamic_slice(small[:, :8], (0, 0, index * width), (layers, 8, width))
    up_bias_grads = lax.dynamic_slice(
        small[:, 8:].reshape(layers, 4 * hidden), (0, index * hidden), (layers, hidden)
    )
    reduced, left_new, right_new, new_weights = updated
    vector_rate = 0.5 / math.sqrt(tokens * lax.axis_size("dp"))
    return (
        layer_out,
        input_grad,
        reduced,
        left_new,
        right_new,
        new_weights,
        vector_grads,
        vectors - vector_rate * vector_grads,
        up_bias_grads,
        up_bias - vector_rate * up_bias_grads,
    )


def solution(mesh):
    owned = P(None, ("dp", "tensor"), None, None)
    return jax.shard_map(
        body,
        mesh=mesh,
        in_specs=(
            P("dp", "tensor"),
            P("dp", "tensor"),
            P("dp", None),
            P(),
            owned,
            owned,
            owned,
            owned,
            owned,
            P(None, None, "tensor"),
            P(None, "tensor"),
        ),
        out_specs=(
            P("dp", "tensor"),
            P("dp", "tensor"),
            owned,
            owned,
            owned,
            owned,
            P(None, None, "tensor"),
            P(None, None, "tensor"),
            P(None, "tensor"),
            P(None, "tensor"),
        ),
        check_vma=False,
    )
```

```python
import functools
import math

import jax
import jax.numpy as jnp
from jax import lax
from jax.experimental import pallas as pl
from jax.experimental.pallas import tpu as pltpu
from jax.sharding import PartitionSpec as P

HD = 64
eps_norm = 1e-12
stat_decay = 0.5
update_rate = 0.5
f32 = jnp.float32
bf16 = jnp.bfloat16

LAST = (((1,), (1,)), ((), ()))
FIRST = (((0,), (0,)), ((), ()))


def vmem_spec(count):
    return [pl.BlockSpec(memory_space=pltpu.VMEM)] * count


def params(mib=40):
    return pltpu.CompilerParams(vmem_limit_bytes=mib * 1024 * 1024)


def cost(microseconds):
    return pl.CostEstimate(flops=0, bytes_accessed=int(microseconds * 3.4e6), transcendentals=0)


def shape(dims, dtype):
    return jax.ShapeDtypeStruct(dims, dtype)


def cat_rows(refs):
    return jnp.concatenate([ref[...] for ref in refs], axis=0)


def matrix(ref, rows, cols):
    width = ref.shape[1]
    return jnp.concatenate(
        [
            jnp.concatenate(
                [ref[(r * cols + c) // width, (r * cols + c) % width] for c in range(cols)], axis=1
            )
            for r in range(rows)
        ],
        axis=0,
    )


def flat_matrix(ref, base, rows, cols):
    return jnp.concatenate(
        [jnp.concatenate([ref[base + r * cols + c] for c in range(cols)], axis=1) for r in range(rows)], axis=0
    )


def swap(values, axis, flip):
    count = lax.axis_size(axis)
    return lax.ppermute(values, axis, [(i, i ^ flip) for i in range(count)])


def gather_tokens(piece):
    far = swap(piece, "tensor", 2)
    near = swap(piece, "tensor", 1)
    both = swap(far, "tensor", 1)
    return (piece, far, near, both)


def scatter_sum(send, keep, *marks):
    rows = send.shape[0] // 2
    first = swap(send, "tensor", 1)
    message = (keep[rows:] + first[rows:].astype(f32)).astype(bf16)
    if marks:
        message = after(message, *marks)
    return (keep, first, swap(message, "tensor", 2)), message


def by_index(relative):
    index = lax.axis_index("tensor")
    core, x_pos = index % 2 == 1, index // 2 == 1
    r0, r1, r2, r3 = relative
    a0, a1 = jnp.where(core, r1, r0), jnp.where(core, r0, r1)
    a2, a3 = jnp.where(core, r3, r2), jnp.where(core, r2, r3)
    return [
        jnp.where(x_pos, a2, a0),
        jnp.where(x_pos, a3, a1),
        jnp.where(x_pos, a0, a2),
        jnp.where(x_pos, a1, a3),
    ]


def to_tokens(values):
    rows, width = values.shape
    quarter = rows // 4
    r0, r1, r2, r3 = by_index([values[g * quarter : (g + 1) * quarter] for g in range(4)])
    got = swap(jnp.stack([r2, r3]), "tensor", 2)
    near = swap(jnp.stack([r1, got[1]]), "tensor", 1)
    return jnp.concatenate(by_index([r0, near[0], got[0], near[1]]), axis=1)


def from_tokens(values, marks=None):
    width = values.shape[1] // 4
    r0, r1, r2, r3 = by_index([values[:, g * width : (g + 1) * width] for g in range(4)])
    near = jnp.stack([r1, r3])
    got = swap(near if marks is None else after(near, marks[0]), "tensor", 1)
    rest = jnp.stack([r2, got[1]])
    far = swap(rest if marks is None else after(rest, marks[1]), "tensor", 2)
    return jnp.concatenate(by_index([r0, got[0], far[0], far[1]]), axis=0)


ring = (0, 2, 4, 6, 7, 5, 3, 1)


def ring_place():
    index = lax.axis_index("dp")
    return jnp.where(index % 2 == 0, index // 2, 7 - index // 2)


def owner_place(owner):
    return jnp.where(owner % 2 == 0, owner // 2, 7 - owner // 2)


def turn(values, way):
    return lax.ppermute(values, "dp", [(ring[p], ring[(p + way) % 8]) for p in range(8)])


def after(values, *others):
    return lax.optimization_barrier((values,) + tuple(others))[0]


def has_ring():
    return lax.axis_size("dp") == 8


def weight_sources(own, owner_map, meanwhile):
    layers, total = owner_map.shape
    slots = own[0].shape[0]
    half = slots // 2
    positions = jnp.arange(total, dtype=jnp.int32)
    hits = owner_map[:, None, :] == positions[None, :, None]
    inverse = jnp.sum(jnp.where(hits, positions[None, None, :], 0), axis=2).astype(jnp.int32)
    if not has_ring():
        wholes = [lax.all_gather(values.astype(bf16), "dp", axis=0, tiled=True) for values in own]
        for stage in range(3):
            meanwhile(stage, None)
        return [((whole,), ((0, 0),), row[None, :]) for whole, row in zip(wholes, inverse)], None
    ways = jnp.array([0, -1, -2, -3, 1, 2, 3, 4], jnp.int32)
    spots = tuple((j, first) for j in range(7) for first in (0, half)) + ((7, 0), (8, 0))
    target = (ring_place() + ways) % 8
    device = jnp.where(target < 4, 2 * target, 15 - 2 * target)
    mask = device[None, :, None, None] == jnp.arange(8, dtype=jnp.int32)[None, None, :, None]
    rows = jnp.sum(jnp.where(mask, inverse.reshape(layers, 1, 8, slots), 0), axis=2)
    tables = [table for table in rows.reshape(layers, 16, half).astype(jnp.int32)]
    result, points, last, beside = [], [], (), ()
    for layer in range(layers):
        mine = own[layer] if layer == 0 else after(own[layer], points[0])
        mine = mine.astype(bf16)
        start = after(mine, *last) if last else mine
        behind, ahead = [turn(start, 1)], [turn(start, -1)]
        for step in range(3):
            if layer == 0:
                beside += meanwhile(step, behind[-2] if step else None)
            done = (behind[-1], ahead[-1]) + (beside[-1] if layer == 0 else ())
            points.append(behind[-1])
            points.append(ahead[-1])
            next_behind, next_ahead = after(behind[-1], *done), after(ahead[-1], *done)
            if step == 2:
                next_behind, next_ahead = next_behind[:half], next_ahead[half:]
            behind.append(turn(next_behind, 1))
            ahead.append(turn(next_ahead, -1))
        last = (behind[3], ahead[3])
        points += last
        result.append(((mine, *behind[:3], *ahead[:3], behind[3], ahead[3]), spots, tables[layer]))
    return result, points


def send_positions(owner_row, slots):
    if not has_ring():
        return owner_row
    way = (owner_place(owner_row // slots) - ring_place()) % 8
    return (way * slots + owner_row % slots).astype(jnp.int32)


def reduce_start(grads, slots):
    half = slots // 2
    return turn(grads[4 * slots : 4 * slots + half], 1), turn(grads[4 * slots + half : 5 * slots], -1)


def reduce_next(grads, slots, step, came, *marks):
    forward = grads[(5 - step) * slots : (6 - step) * slots].astype(f32)
    backward = grads[(3 + step) * slots : (4 + step) * slots].astype(f32)
    ahead, behind = came[0].astype(f32), came[1].astype(f32)
    if step == 2:
        half = slots // 2
        forward = jnp.concatenate([forward[:half] + ahead, forward[half:]])
        backward = jnp.concatenate([backward[:half], backward[half:] + behind])
    else:
        forward, backward = forward + ahead, backward + behind
    forward, backward = lax.optimization_barrier((forward.astype(bf16), backward.astype(bf16), *marks))[:2]
    return turn(forward, 1), turn(backward, -1)


def norm_kernel(base, keep, first, second, vec, low_out, full_out, normed_out, scale_out, *, rows):
    bias, gain, shift = rows
    hidden = (
        base[...]
        + keep[...]
        + first[...].astype(f32)
        + second[...].astype(f32)
        + vec[bias : bias + 1, :]
    )
    center = jnp.mean(hidden, axis=1, keepdims=True)
    centred = hidden - center
    spread = jnp.mean(centred * centred, axis=1, keepdims=True)
    scale = lax.rsqrt(spread + eps_norm)
    normed = centred * scale
    full = normed * vec[gain : gain + 1, :] + vec[shift : shift + 1, :]
    full_out[...] = full
    low_out[...] = full.astype(bf16)
    normed_out[...] = normed
    scale_out[...] = scale


def top_half(array):
    return pl.BlockSpec((array.shape[0] // 2, array.shape[1]), lambda i: (0, 0))


def whole_spec(array):
    nd = len(array.shape)
    return pl.BlockSpec(tuple(array.shape), lambda i, nd=nd: (0,) * nd)


def norm_step(base, sums, vec, rows):
    keep, first, second = sums
    tokens, width = base.shape
    outs = [
        shape((tokens, width), bf16),
        shape((tokens, width), f32),
        shape((tokens, width), f32),
        shape((tokens, 1), f32),
    ]
    return pl.pallas_call(
        functools.partial(norm_kernel, rows=rows),
        grid=(1,),
        in_specs=[whole_spec(base), top_half(keep), top_half(first), whole_spec(second), whole_spec(vec)],
        out_specs=[whole_spec(o) for o in outs],
        out_shape=outs,
        compiler_params=params(12),
        cost_estimate=cost(1.2),
        name="norm",
    )(base, keep, first, second, vec)


def norm_back_kernel(*refs, gain, summed):
    if summed:
        base, keep, first, second, normed, scale, vec, low_out, full_out, sums_out = refs
        grad = base[...] + keep[...] + first[...].astype(f32) + second[...].astype(f32)
    else:
        base, normed, scale, vec, low_out, full_out, sums_out = refs
        grad = base[...]
    value = normed[...]
    scaled = grad * vec[gain : gain + 1, :]
    mean_grad = jnp.mean(scaled, axis=1, keepdims=True)
    mean_cross = jnp.mean(scaled * value, axis=1, keepdims=True)
    result = scale[...] * (scaled - mean_grad - value * mean_cross)
    full_out[...] = result
    low_out[...] = result.astype(bf16)
    sums_out[0:1, :] = jnp.sum(result, axis=0, keepdims=True)
    sums_out[1:2, :] = jnp.sum(grad * value, axis=0, keepdims=True)
    sums_out[2:3, :] = jnp.sum(grad, axis=0, keepdims=True)


def norm_back_step(base, sums, normed, scale, vec, gain):
    tokens, width = base.shape
    outs = [shape((tokens, width), bf16), shape((tokens, width), f32), shape((3, width), f32)]
    operands = [base]
    specs = [whole_spec(base)]
    if sums is not None:
        keep, first, second = sums
        operands += [keep, first, second]
        specs += [top_half(keep), top_half(first), whole_spec(second)]
    operands += [normed, scale, vec]
    specs += [whole_spec(normed), whole_spec(scale), whole_spec(vec)]
    return pl.pallas_call(
        functools.partial(norm_back_kernel, gain=gain, summed=sums is not None),
        grid=(1,),
        in_specs=specs,
        out_specs=[whole_spec(o) for o in outs],
        out_shape=outs,
        compiler_params=params(12),
        cost_estimate=cost(1.5),
        name="norm_back",
    )(*operands)


def store_sums(total, send_out, keep_out):
    half = total.shape[0] // 2
    send_out[...] = total[half:].astype(bf16)
    keep_out[...] = total[:half]


def start_blocks(sources, spots, table, stage, sem):
    slots = table.shape[1]
    for row, (which, first) in enumerate(spots):

        @pl.loop(0, slots, unroll=min(slots, 24))
        def _(s, row=row, which=which, first=first):
            pltpu.make_async_copy(sources[which].at[first + s], stage.at[table[row, s]], sem).start()


def segment_bias(seg):
    row = seg[...]
    column = jnp.transpose(jnp.broadcast_to(row, (128, row.shape[1])))[:, 0:1]
    return jnp.where(column == row, 0.0, -1e30)


def attend_kernel(
    count, spots, n_qkv, n_out, table, *refs
):
    sources = refs[:count]
    (
        p0, p1, p2, p3, vec, seg,
        query_out, key_out, value_out, mix_out, log_out, send_out, keep_out, attend_out, ffn_out,
        bias, stage, sems,
    ) = refs[count:]
    start_blocks(sources, spots, table, stage, sems.at[0])
    wide = cat_rows((p0, p1, p2, p3))
    bias[...] = segment_bias(seg)
    pltpu.make_async_copy(stage, stage, sems.at[0]).wait()
    cut = n_qkv + n_out
    copies = (
        pltpu.make_async_copy(stage.at[pl.ds(0, cut)], attend_out, sems.at[1]),
        pltpu.make_async_copy(stage.at[pl.ds(cut, ffn_out.shape[0])], ffn_out, sems.at[2]),
    )
    for copy in copies:
        copy.start()
    tokens, model = wide.shape
    width = query_out.shape[1]
    tile = stage.shape[-1]
    projected = jnp.dot(
        wide, flat_matrix(stage, 0, model // tile, 3 * width // tile), preferred_element_type=f32
    )
    query = (projected[:, :width] + vec[0:1, :]).astype(bf16) * jnp.asarray(HD**-0.5, bf16)
    keys = projected[:, width : 2 * width].astype(bf16)
    values = (projected[:, 2 * width :] + vec[1:2, :]).astype(bf16)
    query_out[...] = query
    key_out[...] = keys
    value_out[...] = values
    lane = lax.broadcasted_iota(jnp.int32, (tokens, 128), 1)
    logs = jnp.zeros((tokens, 128), f32)
    mixes = []
    for pair in range(width // 128):
        cols = slice(pair * 128, pair * 128 + 128)
        halves = []
        for part in range(128 // HD):
            inside = (lane >= part * HD) & (lane < part * HD + HD)
            one = jnp.where(inside, query[:, cols], jnp.zeros((), bf16))
            scores = lax.dot_general(one, keys[:, cols], LAST, preferred_element_type=f32) + bias[...]
            top = jnp.max(scores, axis=1, keepdims=True)
            exponent = jnp.exp(scores - top)
            total = jnp.sum(exponent, axis=1, keepdims=True)
            attention = (exponent * (1.0 / total)).astype(bf16)
            halves.append((inside, jnp.dot(attention, values[:, cols], preferred_element_type=f32)))
            logs = jnp.where(lane == pair * (128 // HD) + part, top + jnp.log(total), logs)
        mixed = halves[0][1]
        for inside, other in halves[1:]:
            mixed = jnp.where(inside, other, mixed)
        mixes.append(mixed.astype(bf16))
    mixture = jnp.concatenate(mixes, axis=1)
    mix_out[...] = mixture
    log_out[...] = jnp.transpose(logs)[0:8, :]
    total = jnp.dot(
        mixture, flat_matrix(stage, n_qkv, width // tile, model // tile), preferred_element_type=f32
    )
    store_sums(total, send_out, keep_out)
    for copy in copies:
        copy.wait()


def block_rows(array, start, count):
    return pl.BlockSpec((count,) + tuple(array.shape[1:]), lambda i: (start // count, 0, 0, 0))


def attend_step(pieces, weights, counts, vec, seg):
    quarter, model = pieces[0].shape
    tokens, width = 4 * quarter, vec.shape[1]
    n_qkv, n_out, n_up = counts
    arrays, spots, table = weights
    side = arrays[0].shape[-1]
    total = n_qkv + n_out + 2 * n_up
    outs = [
        shape((tokens, width), bf16),
        shape((tokens, width), bf16),
        shape((tokens, width), bf16),
        shape((tokens, width), bf16),
        shape((8, tokens), f32),
        shape((tokens // 2, model), bf16),
        shape((tokens // 2, model), f32),
        shape((n_qkv + n_out, side, side), bf16),
        shape((2 * n_up, side, side), bf16),
    ]
    operands = list(pieces) + [vec, seg]
    return pl.pallas_call(
        functools.partial(attend_kernel, len(arrays), spots, n_qkv, n_out),
        grid_spec=pltpu.PrefetchScalarGridSpec(
            num_scalar_prefetch=1,
            grid=(),
            in_specs=[pl.BlockSpec(memory_space=pl.ANY)] * len(arrays) + vmem_spec(len(operands)),
            out_specs=vmem_spec(7) + [pl.BlockSpec(memory_space=pl.ANY)] * 2,
            scratch_shapes=[
                pltpu.VMEM((tokens, tokens), f32),
                pltpu.VMEM((total, side, side), bf16),
                pltpu.SemaphoreType.DMA((3,)),
            ],
        ),
        out_shape=outs,
        compiler_params=params(60),
        cost_estimate=cost(11),
        name="attend",
    )(table, *arrays, *operands)


def attend_back_kernel(
    p0, p1, p2, p3, w_out, w_qkv, query_in, key_in, value_in, log_in, seg,
    grad_out, sums_out, send_out, keep_out, bias,
):
    wide = cat_rows((p0, p1, p2, p3))
    tokens, model = wide.shape
    width = query_in.shape[1]
    tile = w_qkv.shape[-1]
    grad_mix = lax.dot_general(
        wide, matrix(w_out, width // tile, model // tile), LAST, preferred_element_type=f32
    ).astype(bf16)
    bias[...] = segment_bias(seg)
    lane = lax.broadcasted_iota(jnp.int32, (tokens, 128), 1)
    grads = ([], [], [])
    for pair in range(width // 128):
        cols = slice(pair * 128, pair * 128 + 128)
        query, keys, values, mix = query_in[:, cols], key_in[:, cols], value_in[:, cols], grad_mix[:, cols]
        picked = [None, None, None]
        for part in range(128 // HD):
            head = pair * (128 // HD) + part
            inside = (lane >= part * HD) & (lane < part * HD + HD)
            zero = jnp.zeros((), bf16)
            scores = (
                lax.dot_general(jnp.where(inside, keys, zero), query, LAST, preferred_element_type=f32)
                + bias[...]
            )
            attention = jnp.exp(scores - log_in[head : head + 1, :])
            pulled = lax.dot_general(jnp.where(inside, values, zero), mix, LAST, preferred_element_type=f32)
            inner = jnp.sum(attention * pulled, axis=0, keepdims=True)
            grad_scores = (attention * (pulled - inner)).astype(bf16)
            three = (
                lax.dot_general(grad_scores, keys, FIRST, preferred_element_type=f32) * (HD**-0.5),
                jnp.dot(grad_scores, query, preferred_element_type=f32),
                jnp.dot(attention.astype(bf16), mix, preferred_element_type=f32),
            )
            for which in range(3):
                if part == 0:
                    picked[which] = three[which]
                else:
                    picked[which] = jnp.where(inside, three[which], picked[which])
        for which in range(3):
            grads[which].append(picked[which].astype(bf16))
    joined = [jnp.concatenate(g, axis=1) for g in grads]
    every = jnp.concatenate(joined, axis=1)
    grad_out[...] = every
    sums_out[0:1, :] = jnp.sum(joined[0].astype(f32), axis=0, keepdims=True)
    sums_out[1:2, :] = jnp.sum(joined[2].astype(f32), axis=0, keepdims=True)
    total = lax.dot_general(
        every, matrix(w_qkv, model // tile, 3 * width // tile), LAST, preferred_element_type=f32
    )
    store_sums(total, send_out, keep_out)


def attend_back_step(pieces, blocks, counts, query, keys, values, logs, seg):
    quarter, model = pieces[0].shape
    tokens, width = query.shape
    n_qkv, n_out, n_up = counts
    per = blocks.shape[1]
    outs = [
        shape((tokens, 3 * width), bf16),
        shape((2, width), f32),
        shape((tokens // 2, model), bf16),
        shape((tokens // 2, model), f32),
    ]
    return pl.pallas_call(
        attend_back_kernel,
        grid=(1,),
        in_specs=[whole_spec(p) for p in pieces]
        + [block_rows(blocks, n_qkv // per, n_out // per), block_rows(blocks, 0, n_qkv // per)]
        + [whole_spec(a) for a in (query, keys, values, logs, seg)],
        out_specs=[whole_spec(o) for o in outs],
        out_shape=outs,
        scratch_shapes=[pltpu.VMEM((tokens, tokens), f32)],
        compiler_params=params(32),
        cost_estimate=cost(6.5),
        name="attend_back",
    )(*pieces, blocks, blocks, query, keys, values, logs, seg)


def ffn_kernel(p0, p1, p2, p3, w_up, w_down, bias, act_out, slope_out, send_out, keep_out):
    wide = cat_rows((p0, p1, p2, p3))
    model = wide.shape[1]
    tile = w_up.shape[-1]
    cols = act_out.shape[1] // tile
    pre = jnp.dot(wide, matrix(w_up, model // tile, cols), preferred_element_type=f32) + bias[...]
    cdf = 0.5 + 0.5 * lax.erf(pre * (0.5**0.5))
    slope_out[...] = cdf + pre * (jnp.exp(-0.5 * pre * pre) * (1.0 / math.sqrt(2.0 * math.pi)))
    activated = (pre * cdf).astype(bf16)
    act_out[...] = activated
    total = jnp.dot(activated, matrix(w_down, cols, model // tile), preferred_element_type=f32)
    store_sums(total, send_out, keep_out)


def fixed(array):
    nd = len(array.shape)
    return pl.BlockSpec(tuple(array.shape), lambda i, nd=nd: (0,) * nd)


def ffn_specs(blocks, counts, chunk_blocks):
    n_qkv, n_out, n_up = counts
    per = blocks.shape[1]
    side = blocks.shape[2]
    up_row = 0
    up_rows = n_up // per
    down_row = n_up // per
    up_spec = pl.BlockSpec((up_rows, chunk_blocks, side, side), lambda i: (up_row // up_rows, i, 0, 0))
    down_spec = pl.BlockSpec((chunk_blocks, per, side, side), lambda i: (down_row // chunk_blocks + i, 0, 0, 0))
    return up_spec, down_spec


def ffn_step(pieces, blocks, counts, up_bias):
    quarter, model = pieces[0].shape
    tokens, hidden = 4 * quarter, up_bias.shape[1]
    up_spec, down_spec = ffn_specs(blocks, counts, hidden // blocks.shape[2])
    outs = [
        shape((tokens, hidden), bf16),
        shape((tokens, hidden), f32),
        shape((tokens // 2, model), bf16),
        shape((tokens // 2, model), f32),
    ]
    return pl.pallas_call(
        ffn_kernel,
        grid=(1,),
        in_specs=[fixed(p) for p in pieces]
        + [up_spec, down_spec, fixed(up_bias)],
        out_specs=[fixed(o) for o in outs],
        out_shape=outs,
        compiler_params=params(24),
        cost_estimate=cost(5),
        name="ffn",
    )(*pieces, blocks, blocks, up_bias)


def ffn_back_kernel(p0, p1, p2, p3, w_up, w_down, slope, grad_out, bias_out, send_out, keep_out):
    wide = cat_rows((p0, p1, p2, p3))
    model = wide.shape[1]
    tile = w_up.shape[-1]
    cols = grad_out.shape[1] // tile
    pulled = lax.dot_general(wide, matrix(w_down, cols, model // tile), LAST, preferred_element_type=f32)
    grad = (pulled * slope[...]).astype(bf16)
    grad_out[...] = grad
    bias_out[...] = jnp.sum(grad.astype(f32), axis=0, keepdims=True)
    total = lax.dot_general(grad, matrix(w_up, model // tile, cols), LAST, preferred_element_type=f32)
    store_sums(total, send_out, keep_out)


def ffn_back_step(pieces, blocks, counts, slope):
    quarter, model = pieces[0].shape
    tokens, hidden = slope.shape
    up_spec, down_spec = ffn_specs(blocks, counts, hidden // blocks.shape[2])
    outs = [
        shape((tokens, hidden), bf16),
        shape((1, hidden), f32),
        shape((tokens // 2, model), bf16),
        shape((tokens // 2, model), f32),
    ]
    return pl.pallas_call(
        ffn_back_kernel,
        grid=(1,),
        in_specs=[fixed(p) for p in pieces] + [up_spec, down_spec, fixed(slope)],
        out_specs=[fixed(o) for o in outs],
        out_shape=outs,
        compiler_params=params(24),
        cost_estimate=cost(7),
        name="ffn_back",
    )(*pieces, blocks, blocks, slope)


def weight_grad_jobs(jobs, operands, side, store):
    at = 0
    for left_count, right_count, base in jobs:
        left = operands[at : at + left_count]
        right = operands[at + left_count : at + left_count + right_count]
        at += left_count + right_count
        columns = cat_rows(right)
        per = columns.shape[1] // side
        width = left[0].shape[1]
        chunk = min(width, 2 * side)
        for start in range(0, width, chunk):
            rows = jnp.concatenate([ref[:, start : start + chunk] for ref in left], axis=0)
            result = lax.dot_general(rows, columns, FIRST, preferred_element_type=f32).astype(bf16)
            for i in range(chunk // side):
                for j in range(per):
                    store(
                        base + (start // side + i) * per + j,
                        result[i * side : (i + 1) * side, j * side : (j + 1) * side],
                    )


def job_parts(jobs, side):
    operands = [a for left, right, base in jobs for a in left + right]
    layout = tuple((len(left), len(right), base) for left, right, base in jobs)
    blocks = sum(left[0].shape[1] // side * (right[0].shape[1] // side) for left, right, base in jobs)
    tokens = sum(a.shape[0] for a in jobs[0][0])
    return operands, layout, blocks, tokens


def block_grad_kernel(jobs, used, chained, place, *refs):
    out, stage, sem = refs[used + chained :]
    slots = []

    def store(block, value):
        slot = len(slots)
        slots.append(block)
        stage[slot] = value
        pltpu.make_async_copy(stage.at[slot], out.at[place[block]], sem).start()

    weight_grad_jobs(jobs, refs[:used], stage.shape[-1], store)
    pltpu.make_async_copy(stage, out.at[pl.ds(0, stage.shape[0])], sem).wait()


def block_grad_step(jobs, place, total, side, target=None):
    operands, layout, blocks, tokens = job_parts(jobs, side)
    chained = [] if target is None else [target]
    return pl.pallas_call(
        functools.partial(block_grad_kernel, layout, len(operands), len(chained)),
        grid_spec=pltpu.PrefetchScalarGridSpec(
            num_scalar_prefetch=1,
            grid=(),
            in_specs=vmem_spec(len(operands)) + [pl.BlockSpec(memory_space=pl.ANY)] * len(chained),
            out_specs=pl.BlockSpec(memory_space=pl.ANY),
            scratch_shapes=[pltpu.VMEM((blocks, side, side), bf16), pltpu.SemaphoreType.DMA],
        ),
        out_shape=shape((total, side, side), bf16),
        input_output_aliases={1 + len(operands): 0} if chained else {},
        compiler_params=params(54),
        cost_estimate=cost(4 if chained else 6),
        name="block_grad",
    )(place, *operands, *chained)


def update_kernel(part_count, chained, *refs):
    parts = refs[:part_count]
    masters, left, right, left_root, right_root = refs[part_count : part_count + 5]
    grad_out, left_out, right_out, weight_out = refs[part_count + 5 + chained :]
    grad = parts[0][...].astype(f32)
    for part in parts[1:]:
        grad = grad + part[...].astype(f32)
    grad_out[0] = grad
    for b in range(grad.shape[0]):
        low = grad[b].astype(bf16)
        left_out[0, b] = stat_decay * left[0, b] + (1.0 - stat_decay) * lax.dot_general(
            low, low, LAST, preferred_element_type=f32
        )
        right_out[0, b] = stat_decay * right[0, b] + (1.0 - stat_decay) * lax.dot_general(
            low, low, FIRST, preferred_element_type=f32
        )
        inner = jnp.dot(low, right_root[0, b].astype(bf16), preferred_element_type=f32)
        outer = jnp.dot(left_root[0, b].astype(bf16), inner.astype(bf16), preferred_element_type=f32)
        weight_out[0, b] = masters[0, b] - update_rate * outer


def update_step(parts, layer, state, previous):
    layers, slots, side, _ = state[0].shape
    group = 6 if slots % 6 == 0 else slots
    one = pl.BlockSpec((1, group, side, side), lambda i: (layer, i, 0, 0))
    chained = [] if previous is None else list(previous)
    aliases = {len(parts) + 5 + k: k for k in range(len(chained))}
    return pl.pallas_call(
        functools.partial(update_kernel, len(parts), len(chained)),
        grid=(slots // group,),
        in_specs=[pl.BlockSpec((group, side, side), lambda i: (i, 0, 0))] * len(parts)
        + [one] * 5
        + [pl.BlockSpec(memory_space=pl.ANY)] * len(chained),
        out_specs=[one] * 4,
        out_shape=[shape(state[0].shape, f32)] * 4,
        input_output_aliases=aliases,
        compiler_params=params(32),
        cost_estimate=cost(10),
        name="update",
    )(*parts, *state, *chained)


def body(
    layer_in,
    cotangent,
    segment_ids,
    owner_map,
    masters,
    left_stats,
    right_stats,
    left_roots,
    right_roots,
    vectors,
    up_bias,
):
    layers, slots, side = masters.shape[0], masters.shape[1], masters.shape[-1]
    tokens, width = layer_in.shape
    model = width * lax.axis_size("tensor")
    hidden = up_bias.shape[1]
    tile_rows = model // side
    n_qkv = tile_rows * (3 * width // side)
    n_out = width // side * tile_rows
    n_up = tile_rows * (hidden // side)
    counts = (n_qkv, n_out, n_up)
    total = owner_map.shape[1]
    index = lax.axis_index("tensor")
    quarter = tokens // 4

    segments = jnp.concatenate(
        by_index([segment_ids[:, g * quarter : (g + 1) * quarter] for g in range(4)]), axis=1
    )
    segments = jnp.concatenate(
        [segments[:, g * quarter : (g + 1) * quarter] for g in (0, 2, 1, 3)], axis=1
    )
    seg = segments.astype(f32)

    made = {}

    def meanwhile(stage, mark):
        def hold(values):
            return values if mark is None else after(values, mark)

        if stage == 0:
            near = swap(vectors, "tensor", 1)
            far = swap(jnp.stack([vectors, near]), "tensor", 2)
            made["vectors"] = jnp.concatenate(by_index([vectors, near, far[0], far[1]]), axis=2)
            made["stream"] = to_tokens(layer_in)
            made["places"] = tuple(send_positions(owner_map, slots))
            part = (made["vectors"], made["stream"]) + made["places"]
        elif stage == 1:
            made["wide"] = gather_tokens(hold(made["stream"]).astype(bf16))
            part = made["wide"] + (seg,)
        else:
            made["grad"] = to_tokens(hold(cotangent))
            part = (made["grad"],)
        return (part,)

    own = [masters[layer] for layer in range(layers)]
    sources, points = weight_sources(own, owner_map, meanwhile)
    paired = points is not None
    wide_vectors, stream, wide_in, grad, places = (
        made[name] for name in ("vectors", "stream", "wide", "grad", "places")
    )
    weights = []

    kept = []
    for layer in range(layers):
        vec = wide_vectors[layer]
        if layer > 0:
            wide_in = gather_tokens(stream_low)
        query, keys, values, mixture, logs, send, keep, attend_blocks, ffn_blocks = attend_step(
            wide_in, sources[layer], counts, vectors[layer], seg
        )
        attend_blocks = attend_blocks.reshape(-1, tile_rows, side, side)
        ffn_blocks = ffn_blocks.reshape(-1, tile_rows, side, side)
        weights.append((attend_blocks, ffn_blocks))
        sums, message = scatter_sum(send, keep)
        if layer == 0 and paired:
            sums = (after(sums[0], *points[8:10]),) + sums[1:]
        mid_low, middle, normed_one, scale_one = norm_step(stream, sums, vec, (2, 3, 4))
        wide_mid = gather_tokens(mid_low)
        if layer == 0 and paired:
            wide_mid = wide_mid[:1] + (after(wide_mid[1], *points[10:12]),) + wide_mid[2:]
        activated, slope, send, keep = ffn_step(wide_mid, ffn_blocks, counts, up_bias[layer : layer + 1])
        sums, message = scatter_sum(send, keep, *(points[12:14] if layer == 0 and paired else ()))
        stream_low, stream, normed_two, scale_two = norm_step(middle, sums, vec, (5, 6, 7))
        kept.append(
            (wide_in, query, keys, values, mixture, logs, normed_one, scale_one, wide_mid, activated, slope, normed_two, scale_two)
        )

    vector_sums = [None] * layers
    bias_sums = [None] * layers
    sums = None
    above, came = None, ()
    for layer in reversed(range(layers)):
        vec, (attend_blocks, ffn_blocks) = wide_vectors[layer], weights[layer]
        (wide_in, query, keys, values, mixture, logs, normed_one, scale_one, wide_mid, activated, slope, normed_two, scale_two) = kept[layer]
        first = layer == 0 and paired
        grad_low, grad_two, sums_two = norm_back_step(grad, sums, normed_two, scale_two, vec, 6)
        wide_grad = gather_tokens(grad_low)
        if first:
            wide_grad = wide_grad[:1] + (after(wide_grad[1], *came),) + wide_grad[2:]
            came = reduce_next(above, slots, 2, came)
        grad_pre, bias_sum, send, keep = ffn_back_step(wide_grad, ffn_blocks, counts, slope)
        sums, message = scatter_sum(send, keep)
        ffn_jobs = [(wide_mid, (grad_pre,), n_qkv + n_out), ((activated,), wide_grad, n_qkv + n_out + n_up)]
        if first:
            sums = (after(sums[0], *came),) + sums[1:]
            came = reduce_next(above, slots, 3, came)
        else:
            ffn_grads = block_grad_step(ffn_jobs, after(places[layer], message), total, side)
            sums = (after(sums[0], ffn_grads),) + sums[1:]
        grad_low, grad_one, sums_one = norm_back_step(grad_two, sums, normed_one, scale_one, vec, 3)
        wide_first = gather_tokens(grad_low)
        if first:
            ffn_grads = block_grad_step(ffn_jobs, after(places[layer], grad_low), total, side)
            wide_first = wide_first[:1] + (after(wide_first[1], ffn_grads, *came),) + wide_first[2:]
            came = reduce_next(above, slots, 4, came)
        grad_qkv, qv_sums, send, keep = attend_back_step(
            wide_first, attend_blocks, counts, query, keys, values, logs, seg
        )
        sums, message = scatter_sum(send, keep)
        block_grads = block_grad_step(
            [(wide_in, (grad_qkv,), 0), ((mixture,), wide_first, n_qkv)],
            places[layer] if first else after(places[layer], message), total, side, ffn_grads,
        )
        grad = grad_one
        spread = jnp.concatenate([jnp.zeros_like(sums_one[:2]), sums_one, sums_two], axis=0)
        vector_sums[layer] = lax.dynamic_update_slice(spread, qv_sums, (0, index * width))
        bias_sums[layer] = lax.dynamic_update_slice(
            jnp.zeros((1, 4 * hidden), f32), bias_sum, (0, index * hidden)
        ).reshape(4 * hidden // model, model)
        if layer > 0:
            sums = (after(sums[0], block_grads),) + sums[1:]
            above = block_grads
            if paired:
                came = reduce_start(above, slots)

    small = jnp.stack([jnp.concatenate(pair, axis=0) for pair in zip(vector_sums, bias_sums)])
    small = small + swap(small, "tensor", 1)
    small = small + swap(small, "tensor", 2)
    state = (masters, left_stats, right_stats, left_roots, right_roots)
    if paired:
        before = (above[:slots], *came)
        marks = [reduce_start(after(block_grads, *came), slots)]
        small = small + swap(small, "dp", 2)
        marks.append(reduce_next(block_grads, slots, 2, marks[0], small))
        marks.append(reduce_next(block_grads, slots, 3, marks[1]))
        small = small + swap(after(small, *marks[0]), "dp", 4)
        came = reduce_next(block_grads, slots, 4, marks[2], small)
        small = small + swap(after(small, *marks[1]), "dp", 1)
        parts = (after(block_grads[:slots], small), *came)
        input_grad, layer_out = (
            from_tokens(values, (marks[0][0], marks[1][0]))
            for values in (grad + sums[0][:quarter] + sums[1][:quarter].astype(f32) + sums[2].astype(f32), stream)
        )
        updated = update_step(before, 1, (after(masters, *marks[1]),) + state[1:], None)
        updated = update_step(parts, 0, state, updated)
    else:
        small = lax.psum(small, "dp")
        input_grad, layer_out = (
            from_tokens(values)
            for values in (grad + sums[0][:quarter] + sums[1][:quarter].astype(f32) + sums[2].astype(f32), stream)
        )
        updated = None
        for layer, grads in ((1, above), (0, block_grads)):
            mine = lax.psum_scatter(grads, "dp", scatter_dimension=0, tiled=True)
            updated = update_step((mine,), layer, state, updated)
    vector_grads = lax.dynamic_slice(small[:, :8], (0, 0, index * width), (layers, 8, width))
    up_bias_grads = lax.dynamic_slice(
        small[:, 8:].reshape(layers, 4 * hidden), (0, index * hidden), (layers, hidden)
    )
    reduced, left_new, right_new, new_weights = updated
    vector_rate = 0.5 / math.sqrt(tokens * lax.axis_size("dp"))
    return (
        layer_out,
        input_grad,
        reduced,
        left_new,
        right_new,
        new_weights,
        vector_grads,
        vectors - vector_rate * vector_grads,
        up_bias_grads,
        up_bias - vector_rate * up_bias_grads,
    )


def solution(mesh):
    owned = P(None, ("dp", "tensor"), None, None)
    return jax.shard_map(
        body,
        mesh=mesh,
        in_specs=(
            P("dp", "tensor"),
            P("dp", "tensor"),
            P("dp", None),
            P(),
            owned,
            owned,
            owned,
            owned,
            owned,
            P(None, None, "tensor"),
            P(None, "tensor"),
        ),
        out_specs=(
            P("dp", "tensor"),
            P("dp", "tensor"),
            owned,
            owned,
            owned,
            owned,
            P(None, None, "tensor"),
            P(None, None, "tensor"),
            P(None, "tensor"),
            P(None, "tensor"),
        ),
        check_vma=False,
    )
```

```python
import functools
import math

import jax
import jax.numpy as jnp
from jax import lax
from jax.experimental import pallas as pl
from jax.experimental.pallas import tpu as pltpu
from jax.sharding import PartitionSpec as P

HD = 64
eps_norm = 1e-12
stat_decay = 0.5
update_rate = 0.5
f32 = jnp.float32
bf16 = jnp.bfloat16

LAST = (((1,), (1,)), ((), ()))
FIRST = (((0,), (0,)), ((), ()))


def vmem_spec(count):
    return [pl.BlockSpec(memory_space=pltpu.VMEM)] * count


def params(mib=40):
    return pltpu.CompilerParams(vmem_limit_bytes=mib * 1024 * 1024)


def cost(microseconds):
    return pl.CostEstimate(flops=0, bytes_accessed=int(microseconds * 3.4e6), transcendentals=0)


def shape(dims, dtype):
    return jax.ShapeDtypeStruct(dims, dtype)


def cat_rows(refs):
    return jnp.concatenate([ref[...] for ref in refs], axis=0)


def matrix(ref, rows, cols):
    width = ref.shape[1]
    return jnp.concatenate(
        [
            jnp.concatenate(
                [ref[(r * cols + c) // width, (r * cols + c) % width] for c in range(cols)], axis=1
            )
            for r in range(rows)
        ],
        axis=0,
    )


def flat_matrix(ref, base, rows, cols):
    return jnp.concatenate(
        [jnp.concatenate([ref[base + r * cols + c] for c in range(cols)], axis=1) for r in range(rows)], axis=0
    )


def swap(values, axis, flip):
    count = lax.axis_size(axis)
    return lax.ppermute(values, axis, [(i, i ^ flip) for i in range(count)])


def gather_tokens(piece):
    far = swap(piece, "tensor", 2)
    near = swap(piece, "tensor", 1)
    both = swap(far, "tensor", 1)
    return (piece, far, near, both)


def scatter_sum(send, keep, *marks):
    rows = send.shape[0] // 2
    first = swap(send, "tensor", 1)
    message = (keep[rows:].astype(f32) + first[rows:].astype(f32)).astype(bf16)
    if marks:
        message = after(message, *marks)
    return (keep, first, swap(message, "tensor", 2)), message


def by_index(relative):
    index = lax.axis_index("tensor")
    core, x_pos = index % 2 == 1, index // 2 == 1
    r0, r1, r2, r3 = relative
    a0, a1 = jnp.where(core, r1, r0), jnp.where(core, r0, r1)
    a2, a3 = jnp.where(core, r3, r2), jnp.where(core, r2, r3)
    return [
        jnp.where(x_pos, a2, a0),
        jnp.where(x_pos, a3, a1),
        jnp.where(x_pos, a0, a2),
        jnp.where(x_pos, a1, a3),
    ]


def to_tokens(values):
    rows, width = values.shape
    quarter = rows // 4
    r0, r1, r2, r3 = by_index([values[g * quarter : (g + 1) * quarter] for g in range(4)])
    got = swap(jnp.stack([r2, r3]), "tensor", 2)
    near = swap(jnp.stack([r1, got[1]]), "tensor", 1)
    return jnp.concatenate(by_index([r0, near[0], got[0], near[1]]), axis=1)


def from_tokens(values, marks=None):
    width = values.shape[1] // 4
    r0, r1, r2, r3 = by_index([values[:, g * width : (g + 1) * width] for g in range(4)])
    near = jnp.stack([r1, r3])
    got = swap(near if marks is None else after(near, marks[0]), "tensor", 1)
    rest = jnp.stack([r2, got[1]])
    far = swap(rest if marks is None else after(rest, marks[1]), "tensor", 2)
    return jnp.concatenate(by_index([r0, got[0], far[0], far[1]]), axis=0)


ring = (0, 2, 4, 6, 7, 5, 3, 1)


def ring_place():
    index = lax.axis_index("dp")
    return jnp.where(index % 2 == 0, index // 2, 7 - index // 2)


def owner_place(owner):
    return jnp.where(owner % 2 == 0, owner // 2, 7 - owner // 2)


def turn(values, way):
    return lax.ppermute(values, "dp", [(ring[p], ring[(p + way) % 8]) for p in range(8)])


def after(values, *others):
    return lax.optimization_barrier((values,) + tuple(others))[0]


def has_ring():
    return lax.axis_size("dp") == 8


def weight_sources(own, owner_map, meanwhile):
    layers, total = owner_map.shape
    slots = own[0].shape[0]
    half = slots // 2
    positions = jnp.arange(total, dtype=jnp.int32)
    hits = owner_map[:, None, :] == positions[None, :, None]
    inverse = jnp.sum(jnp.where(hits, positions[None, None, :], 0), axis=2).astype(jnp.int32)
    if not has_ring():
        wholes = [lax.all_gather(values.astype(bf16), "dp", axis=0, tiled=True) for values in own]
        for stage in range(3):
            meanwhile(stage, None)
        return [((whole,), ((0, 0),), row[None, :]) for whole, row in zip(wholes, inverse)], None
    ways = jnp.array([0, -1, -2, -3, 1, 2, 3, 4], jnp.int32)
    spots = tuple((j, first) for j in range(7) for first in (0, half)) + ((7, 0), (8, 0))
    target = (ring_place() + ways) % 8
    device = jnp.where(target < 4, 2 * target, 15 - 2 * target)
    mask = device[None, :, None, None] == jnp.arange(8, dtype=jnp.int32)[None, None, :, None]
    rows = jnp.sum(jnp.where(mask, inverse.reshape(layers, 1, 8, slots), 0), axis=2)
    tables = [table for table in rows.reshape(layers, 16, half).astype(jnp.int32)]
    result, points, last, beside = [], [], (), ()
    for layer in range(layers):
        mine = own[layer] if layer == 0 else after(own[layer], points[0])
        mine = mine.astype(bf16)
        start = after(mine, *last) if last else mine
        behind, ahead = [turn(start, 1)], [turn(start, -1)]
        for step in range(3):
            if layer == 0:
                beside += meanwhile(step, behind[-2] if step else None)
            done = (behind[-1], ahead[-1]) + (beside[-1] if layer == 0 else ())
            points.append(behind[-1])
            points.append(ahead[-1])
            next_behind, next_ahead = after(behind[-1], *done), after(ahead[-1], *done)
            if step == 2:
                next_behind, next_ahead = next_behind[:half], next_ahead[half:]
            behind.append(turn(next_behind, 1))
            ahead.append(turn(next_ahead, -1))
        last = (behind[3], ahead[3])
        points += last
        result.append(((mine, *behind[:3], *ahead[:3], behind[3], ahead[3]), spots, tables[layer]))
    return result, points


def send_positions(owner_row, slots):
    if not has_ring():
        return owner_row
    way = (owner_place(owner_row // slots) - ring_place()) % 8
    return (way * slots + owner_row % slots).astype(jnp.int32)


def reduce_start(grads, slots):
    half = slots // 2
    return turn(grads[4 * slots : 4 * slots + half], 1), turn(grads[4 * slots + half : 5 * slots], -1)


def reduce_next(grads, slots, step, came, *marks):
    forward = grads[(5 - step) * slots : (6 - step) * slots].astype(f32)
    backward = grads[(3 + step) * slots : (4 + step) * slots].astype(f32)
    ahead, behind = came[0].astype(f32), came[1].astype(f32)
    if step == 2:
        half = slots // 2
        forward = jnp.concatenate([forward[:half] + ahead, forward[half:]])
        backward = jnp.concatenate([backward[:half], backward[half:] + behind])
    else:
        forward, backward = forward + ahead, backward + behind
    forward, backward = lax.optimization_barrier((forward.astype(bf16), backward.astype(bf16), *marks))[:2]
    return turn(forward, 1), turn(backward, -1)


def norm_kernel(base, keep, first, second, vec, low_out, full_out, normed_out, scale_out, *, rows):
    bias, gain, shift = rows
    hidden = (
        base[...]
        + keep[...].astype(f32)
        + first[...].astype(f32)
        + second[...].astype(f32)
        + vec[bias : bias + 1, :]
    )
    center = jnp.mean(hidden, axis=1, keepdims=True)
    centred = hidden - center
    spread = jnp.mean(centred * centred, axis=1, keepdims=True)
    scale = lax.rsqrt(spread + eps_norm)
    normed = centred * scale
    full = normed * vec[gain : gain + 1, :] + vec[shift : shift + 1, :]
    full_out[...] = full
    low_out[...] = full.astype(bf16)
    normed_out[...] = normed
    scale_out[...] = scale


def top_half(array):
    return pl.BlockSpec((array.shape[0] // 2, array.shape[1]), lambda i: (0, 0))


def whole_spec(array):
    nd = len(array.shape)
    return pl.BlockSpec(tuple(array.shape), lambda i, nd=nd: (0,) * nd)


def norm_step(base, sums, vec, rows):
    keep, first, second = sums
    tokens, width = base.shape
    outs = [
        shape((tokens, width), bf16),
        shape((tokens, width), f32),
        shape((tokens, width), f32),
        shape((tokens, 1), f32),
    ]
    return pl.pallas_call(
        functools.partial(norm_kernel, rows=rows),
        grid=(1,),
        in_specs=[whole_spec(base), top_half(keep), top_half(first), whole_spec(second), whole_spec(vec)],
        out_specs=[whole_spec(o) for o in outs],
        out_shape=outs,
        compiler_params=params(12),
        cost_estimate=cost(1.2),
        name="norm",
    )(base, keep, first, second, vec)


def norm_back_kernel(*refs, gain, summed):
    if summed:
        base, keep, first, second, normed, scale, vec, low_out, full_out, sums_out = refs
        grad = base[...] + keep[...].astype(f32) + first[...].astype(f32) + second[...].astype(f32)
    else:
        base, normed, scale, vec, low_out, full_out, sums_out = refs
        grad = base[...]
    value = normed[...]
    scaled = grad * vec[gain : gain + 1, :]
    mean_grad = jnp.mean(scaled, axis=1, keepdims=True)
    mean_cross = jnp.mean(scaled * value, axis=1, keepdims=True)
    result = scale[...] * (scaled - mean_grad - value * mean_cross)
    full_out[...] = result
    low_out[...] = result.astype(bf16)
    sums_out[0:1, :] = jnp.sum(result, axis=0, keepdims=True)
    sums_out[1:2, :] = jnp.sum(grad * value, axis=0, keepdims=True)
    sums_out[2:3, :] = jnp.sum(grad, axis=0, keepdims=True)


def norm_back_step(base, sums, normed, scale, vec, gain):
    tokens, width = base.shape
    outs = [shape((tokens, width), bf16), shape((tokens, width), f32), shape((3, width), f32)]
    operands = [base]
    specs = [whole_spec(base)]
    if sums is not None:
        keep, first, second = sums
        operands += [keep, first, second]
        specs += [top_half(keep), top_half(first), whole_spec(second)]
    operands += [normed, scale, vec]
    specs += [whole_spec(normed), whole_spec(scale), whole_spec(vec)]
    return pl.pallas_call(
        functools.partial(norm_back_kernel, gain=gain, summed=sums is not None),
        grid=(1,),
        in_specs=specs,
        out_specs=[whole_spec(o) for o in outs],
        out_shape=outs,
        compiler_params=params(12),
        cost_estimate=cost(1.5),
        name="norm_back",
    )(*operands)


def store_sums(total, send_out, keep_out):
    half = total.shape[0] // 2
    send_out[...] = total[half:].astype(bf16)
    keep_out[...] = total[:half].astype(bf16)


def start_blocks(sources, spots, table, stage, sem):
    slots = table.shape[1]
    for row, (which, first) in enumerate(spots):

        @pl.loop(0, slots, unroll=min(slots, 24))
        def _(s, row=row, which=which, first=first):
            pltpu.make_async_copy(sources[which].at[first + s], stage.at[table[row, s]], sem).start()


def segment_bias(seg):
    row = seg[...]
    column = jnp.transpose(jnp.broadcast_to(row, (128, row.shape[1])))[:, 0:1]
    return jnp.where(column == row, 0.0, -1e30)


def attend_kernel(
    count, spots, n_qkv, n_out, table, *refs
):
    sources = refs[:count]
    (
        p0, p1, p2, p3, vec, seg,
        query_out, key_out, value_out, mix_out, log_out, send_out, keep_out, attend_out, ffn_out,
        bias, stage, sems,
    ) = refs[count:]
    start_blocks(sources, spots, table, stage, sems.at[0])
    wide = cat_rows((p0, p1, p2, p3))
    bias[...] = segment_bias(seg)
    pltpu.make_async_copy(stage, stage, sems.at[0]).wait()
    cut = n_qkv + n_out
    copies = (
        pltpu.make_async_copy(stage.at[pl.ds(0, cut)], attend_out, sems.at[1]),
        pltpu.make_async_copy(stage.at[pl.ds(cut, ffn_out.shape[0])], ffn_out, sems.at[2]),
    )
    for copy in copies:
        copy.start()
    tokens, model = wide.shape
    width = query_out.shape[1]
    tile = stage.shape[-1]
    projected = jnp.dot(
        wide, flat_matrix(stage, 0, model // tile, 3 * width // tile), preferred_element_type=f32
    )
    query = (projected[:, :width] + vec[0:1, :]).astype(bf16) * jnp.asarray(HD**-0.5, bf16)
    keys = projected[:, width : 2 * width].astype(bf16)
    values = (projected[:, 2 * width :] + vec[1:2, :]).astype(bf16)
    query_out[...] = query
    key_out[...] = keys
    value_out[...] = values
    lane = lax.broadcasted_iota(jnp.int32, (tokens, 128), 1)
    logs = jnp.zeros((tokens, 128), f32)
    mixes = []
    for pair in range(width // 128):
        cols = slice(pair * 128, pair * 128 + 128)
        halves = []
        for part in range(128 // HD):
            inside = (lane >= part * HD) & (lane < part * HD + HD)
            one = jnp.where(inside, query[:, cols], jnp.zeros((), bf16))
            scores = lax.dot_general(one, keys[:, cols], LAST, preferred_element_type=f32) + bias[...]
            top = jnp.max(scores, axis=1, keepdims=True)
            exponent = jnp.exp(scores - top)
            total = jnp.sum(exponent, axis=1, keepdims=True)
            attention = (exponent * (1.0 / total)).astype(bf16)
            halves.append((inside, jnp.dot(attention, values[:, cols], preferred_element_type=f32)))
            logs = jnp.where(lane == pair * (128 // HD) + part, top + jnp.log(total), logs)
        mixed = halves[0][1]
        for inside, other in halves[1:]:
            mixed = jnp.where(inside, other, mixed)
        mixes.append(mixed.astype(bf16))
    mixture = jnp.concatenate(mixes, axis=1)
    mix_out[...] = mixture
    log_out[...] = jnp.transpose(logs)[0:8, :]
    total = jnp.dot(
        mixture, flat_matrix(stage, n_qkv, width // tile, model // tile), preferred_element_type=f32
    )
    store_sums(total, send_out, keep_out)
    for copy in copies:
        copy.wait()


def block_rows(array, start, count):
    return pl.BlockSpec((count,) + tuple(array.shape[1:]), lambda i: (start // count, 0, 0, 0))


def attend_step(pieces, weights, counts, vec, seg):
    quarter, model = pieces[0].shape
    tokens, width = 4 * quarter, vec.shape[1]
    n_qkv, n_out, n_up = counts
    arrays, spots, table = weights
    side = arrays[0].shape[-1]
    total = n_qkv + n_out + 2 * n_up
    outs = [
        shape((tokens, width), bf16),
        shape((tokens, width), bf16),
        shape((tokens, width), bf16),
        shape((tokens, width), bf16),
        shape((8, tokens), f32),
        shape((tokens // 2, model), bf16),
        shape((tokens // 2, model), bf16),
        shape((n_qkv + n_out, side, side), bf16),
        shape((2 * n_up, side, side), bf16),
    ]
    operands = list(pieces) + [vec, seg]
    return pl.pallas_call(
        functools.partial(attend_kernel, len(arrays), spots, n_qkv, n_out),
        grid_spec=pltpu.PrefetchScalarGridSpec(
            num_scalar_prefetch=1,
            grid=(),
            in_specs=[pl.BlockSpec(memory_space=pl.ANY)] * len(arrays) + vmem_spec(len(operands)),
            out_specs=vmem_spec(7) + [pl.BlockSpec(memory_space=pl.ANY)] * 2,
            scratch_shapes=[
                pltpu.VMEM((tokens, tokens), f32),
                pltpu.VMEM((total, side, side), bf16),
                pltpu.SemaphoreType.DMA((3,)),
            ],
        ),
        out_shape=outs,
        compiler_params=params(60),
        cost_estimate=cost(11),
        name="attend",
    )(table, *arrays, *operands)


def attend_back_kernel(
    p0, p1, p2, p3, w_out, w_qkv, query_in, key_in, value_in, log_in, seg,
    grad_out, sums_out, send_out, keep_out, bias,
):
    wide = cat_rows((p0, p1, p2, p3))
    tokens, model = wide.shape
    width = query_in.shape[1]
    tile = w_qkv.shape[-1]
    grad_mix = lax.dot_general(
        wide, matrix(w_out, width // tile, model // tile), LAST, preferred_element_type=f32
    ).astype(bf16)
    bias[...] = segment_bias(seg)
    lane = lax.broadcasted_iota(jnp.int32, (tokens, 128), 1)
    grads = ([], [], [])
    for pair in range(width // 128):
        cols = slice(pair * 128, pair * 128 + 128)
        query, keys, values, mix = query_in[:, cols], key_in[:, cols], value_in[:, cols], grad_mix[:, cols]
        picked = [None, None, None]
        for part in range(128 // HD):
            head = pair * (128 // HD) + part
            inside = (lane >= part * HD) & (lane < part * HD + HD)
            zero = jnp.zeros((), bf16)
            scores = (
                lax.dot_general(jnp.where(inside, keys, zero), query, LAST, preferred_element_type=f32)
                + bias[...]
            )
            attention = jnp.exp(scores - log_in[head : head + 1, :])
            pulled = lax.dot_general(jnp.where(inside, values, zero), mix, LAST, preferred_element_type=f32)
            inner = jnp.sum(attention * pulled, axis=0, keepdims=True)
            grad_scores = (attention * (pulled - inner)).astype(bf16)
            three = (
                lax.dot_general(grad_scores, keys, FIRST, preferred_element_type=f32) * (HD**-0.5),
                jnp.dot(grad_scores, query, preferred_element_type=f32),
                jnp.dot(attention.astype(bf16), mix, preferred_element_type=f32),
            )
            for which in range(3):
                if part == 0:
                    picked[which] = three[which]
                else:
                    picked[which] = jnp.where(inside, three[which], picked[which])
        for which in range(3):
            grads[which].append(picked[which].astype(bf16))
    joined = [jnp.concatenate(g, axis=1) for g in grads]
    every = jnp.concatenate(joined, axis=1)
    grad_out[...] = every
    sums_out[0:1, :] = jnp.sum(joined[0].astype(f32), axis=0, keepdims=True)
    sums_out[1:2, :] = jnp.sum(joined[2].astype(f32), axis=0, keepdims=True)
    total = lax.dot_general(
        every, matrix(w_qkv, model // tile, 3 * width // tile), LAST, preferred_element_type=f32
    )
    store_sums(total, send_out, keep_out)


def attend_back_step(pieces, blocks, counts, query, keys, values, logs, seg):
    quarter, model = pieces[0].shape
    tokens, width = query.shape
    n_qkv, n_out, n_up = counts
    per = blocks.shape[1]
    outs = [
        shape((tokens, 3 * width), bf16),
        shape((2, width), f32),
        shape((tokens // 2, model), bf16),
        shape((tokens // 2, model), bf16),
    ]
    return pl.pallas_call(
        attend_back_kernel,
        grid=(1,),
        in_specs=[whole_spec(p) for p in pieces]
        + [block_rows(blocks, n_qkv // per, n_out // per), block_rows(blocks, 0, n_qkv // per)]
        + [whole_spec(a) for a in (query, keys, values, logs, seg)],
        out_specs=[whole_spec(o) for o in outs],
        out_shape=outs,
        scratch_shapes=[pltpu.VMEM((tokens, tokens), f32)],
        compiler_params=params(32),
        cost_estimate=cost(6.5),
        name="attend_back",
    )(*pieces, blocks, blocks, query, keys, values, logs, seg)


def ffn_kernel(p0, p1, p2, p3, w_up, w_down, bias, act_out, slope_out, send_out, keep_out):
    wide = cat_rows((p0, p1, p2, p3))
    model = wide.shape[1]
    tile = w_up.shape[-1]
    cols = act_out.shape[1] // tile
    pre = jnp.dot(wide, matrix(w_up, model // tile, cols), preferred_element_type=f32) + bias[...]
    cdf = 0.5 + 0.5 * lax.erf(pre * (0.5**0.5))
    slope_out[...] = cdf + pre * (jnp.exp(-0.5 * pre * pre) * (1.0 / math.sqrt(2.0 * math.pi)))
    activated = (pre * cdf).astype(bf16)
    act_out[...] = activated
    total = jnp.dot(activated, matrix(w_down, cols, model // tile), preferred_element_type=f32)
    store_sums(total, send_out, keep_out)


def fixed(array):
    nd = len(array.shape)
    return pl.BlockSpec(tuple(array.shape), lambda i, nd=nd: (0,) * nd)


def ffn_specs(blocks, counts, chunk_blocks):
    n_qkv, n_out, n_up = counts
    per = blocks.shape[1]
    side = blocks.shape[2]
    up_row = 0
    up_rows = n_up // per
    down_row = n_up // per
    up_spec = pl.BlockSpec((up_rows, chunk_blocks, side, side), lambda i: (up_row // up_rows, i, 0, 0))
    down_spec = pl.BlockSpec((chunk_blocks, per, side, side), lambda i: (down_row // chunk_blocks + i, 0, 0, 0))
    return up_spec, down_spec


def ffn_step(pieces, blocks, counts, up_bias):
    quarter, model = pieces[0].shape
    tokens, hidden = 4 * quarter, up_bias.shape[1]
    up_spec, down_spec = ffn_specs(blocks, counts, hidden // blocks.shape[2])
    outs = [
        shape((tokens, hidden), bf16),
        shape((tokens, hidden), f32),
        shape((tokens // 2, model), bf16),
        shape((tokens // 2, model), bf16),
    ]
    return pl.pallas_call(
        ffn_kernel,
        grid=(1,),
        in_specs=[fixed(p) for p in pieces]
        + [up_spec, down_spec, fixed(up_bias)],
        out_specs=[fixed(o) for o in outs],
        out_shape=outs,
        compiler_params=params(24),
        cost_estimate=cost(5),
        name="ffn",
    )(*pieces, blocks, blocks, up_bias)


def ffn_back_kernel(p0, p1, p2, p3, w_up, w_down, slope, grad_out, bias_out, send_out, keep_out):
    wide = cat_rows((p0, p1, p2, p3))
    model = wide.shape[1]
    tile = w_up.shape[-1]
    cols = grad_out.shape[1] // tile
    pulled = lax.dot_general(wide, matrix(w_down, cols, model // tile), LAST, preferred_element_type=f32)
    grad = (pulled * slope[...]).astype(bf16)
    grad_out[...] = grad
    bias_out[...] = jnp.sum(grad.astype(f32), axis=0, keepdims=True)
    total = lax.dot_general(grad, matrix(w_up, model // tile, cols), LAST, preferred_element_type=f32)
    store_sums(total, send_out, keep_out)


def ffn_back_step(pieces, blocks, counts, slope):
    quarter, model = pieces[0].shape
    tokens, hidden = slope.shape
    up_spec, down_spec = ffn_specs(blocks, counts, hidden // blocks.shape[2])
    outs = [
        shape((tokens, hidden), bf16),
        shape((1, hidden), f32),
        shape((tokens // 2, model), bf16),
        shape((tokens // 2, model), bf16),
    ]
    return pl.pallas_call(
        ffn_back_kernel,
        grid=(1,),
        in_specs=[fixed(p) for p in pieces] + [up_spec, down_spec, fixed(slope)],
        out_specs=[fixed(o) for o in outs],
        out_shape=outs,
        compiler_params=params(24),
        cost_estimate=cost(7),
        name="ffn_back",
    )(*pieces, blocks, blocks, slope)


def weight_grad_jobs(jobs, operands, side, store):
    at = 0
    for left_count, right_count, base in jobs:
        left = operands[at : at + left_count]
        right = operands[at + left_count : at + left_count + right_count]
        at += left_count + right_count
        columns = cat_rows(right)
        per = columns.shape[1] // side
        width = left[0].shape[1]
        chunk = min(width, 2 * side)
        for start in range(0, width, chunk):
            rows = jnp.concatenate([ref[:, start : start + chunk] for ref in left], axis=0)
            result = lax.dot_general(rows, columns, FIRST, preferred_element_type=f32).astype(bf16)
            for i in range(chunk // side):
                for j in range(per):
                    store(
                        base + (start // side + i) * per + j,
                        result[i * side : (i + 1) * side, j * side : (j + 1) * side],
                    )


def job_parts(jobs, side):
    operands = [a for left, right, base in jobs for a in left + right]
    layout = tuple((len(left), len(right), base) for left, right, base in jobs)
    blocks = sum(left[0].shape[1] // side * (right[0].shape[1] // side) for left, right, base in jobs)
    tokens = sum(a.shape[0] for a in jobs[0][0])
    return operands, layout, blocks, tokens


def block_grad_kernel(jobs, used, chained, place, *refs):
    out, stage, sem = refs[used + chained :]
    slots = []

    def store(block, value):
        slot = len(slots)
        slots.append(block)
        stage[slot] = value
        pltpu.make_async_copy(stage.at[slot], out.at[place[block]], sem).start()

    weight_grad_jobs(jobs, refs[:used], stage.shape[-1], store)
    pltpu.make_async_copy(stage, out.at[pl.ds(0, stage.shape[0])], sem).wait()


def block_grad_step(jobs, place, total, side, target=None):
    operands, layout, blocks, tokens = job_parts(jobs, side)
    chained = [] if target is None else [target]
    return pl.pallas_call(
        functools.partial(block_grad_kernel, layout, len(operands), len(chained)),
        grid_spec=pltpu.PrefetchScalarGridSpec(
            num_scalar_prefetch=1,
            grid=(),
            in_specs=vmem_spec(len(operands)) + [pl.BlockSpec(memory_space=pl.ANY)] * len(chained),
            out_specs=pl.BlockSpec(memory_space=pl.ANY),
            scratch_shapes=[pltpu.VMEM((blocks, side, side), bf16), pltpu.SemaphoreType.DMA],
        ),
        out_shape=shape((total, side, side), bf16),
        input_output_aliases={1 + len(operands): 0} if chained else {},
        compiler_params=params(54),
        cost_estimate=cost(4 if chained else 6),
        name="block_grad",
    )(place, *operands, *chained)


def update_kernel(part_count, chained, *refs):
    parts = refs[:part_count]
    masters, left, right, left_root, right_root = refs[part_count : part_count + 5]
    grad_out, left_out, right_out, weight_out = refs[part_count + 5 + chained :]
    grad = parts[0][...].astype(f32)
    for part in parts[1:]:
        grad = grad + part[...].astype(f32)
    grad_out[0] = grad
    for b in range(grad.shape[0]):
        low = grad[b].astype(bf16)
        left_out[0, b] = stat_decay * left[0, b] + (1.0 - stat_decay) * lax.dot_general(
            low, low, LAST, preferred_element_type=f32
        )
        right_out[0, b] = stat_decay * right[0, b] + (1.0 - stat_decay) * lax.dot_general(
            low, low, FIRST, preferred_element_type=f32
        )
        inner = jnp.dot(low, right_root[0, b].astype(bf16), preferred_element_type=f32)
        outer = jnp.dot(left_root[0, b].astype(bf16), inner.astype(bf16), preferred_element_type=f32)
        weight_out[0, b] = masters[0, b] - update_rate * outer


def update_step(parts, layer, state, previous):
    layers, slots, side, _ = state[0].shape
    group = 6 if slots % 6 == 0 else slots
    one = pl.BlockSpec((1, group, side, side), lambda i: (layer, i, 0, 0))
    chained = [] if previous is None else list(previous)
    aliases = {len(parts) + 5 + k: k for k in range(len(chained))}
    return pl.pallas_call(
        functools.partial(update_kernel, len(parts), len(chained)),
        grid=(slots // group,),
        in_specs=[pl.BlockSpec((group, side, side), lambda i: (i, 0, 0))] * len(parts)
        + [one] * 5
        + [pl.BlockSpec(memory_space=pl.ANY)] * len(chained),
        out_specs=[one] * 4,
        out_shape=[shape(state[0].shape, f32)] * 4,
        input_output_aliases=aliases,
        compiler_params=params(32),
        cost_estimate=cost(10),
        name="update",
    )(*parts, *state, *chained)


def body(
    layer_in,
    cotangent,
    segment_ids,
    owner_map,
    masters,
    left_stats,
    right_stats,
    left_roots,
    right_roots,
    vectors,
    up_bias,
):
    layers, slots, side = masters.shape[0], masters.shape[1], masters.shape[-1]
    tokens, width = layer_in.shape
    model = width * lax.axis_size("tensor")
    hidden = up_bias.shape[1]
    tile_rows = model // side
    n_qkv = tile_rows * (3 * width // side)
    n_out = width // side * tile_rows
    n_up = tile_rows * (hidden // side)
    counts = (n_qkv, n_out, n_up)
    total = owner_map.shape[1]
    index = lax.axis_index("tensor")
    quarter = tokens // 4

    segments = jnp.concatenate(
        by_index([segment_ids[:, g * quarter : (g + 1) * quarter] for g in range(4)]), axis=1
    )
    segments = jnp.concatenate(
        [segments[:, g * quarter : (g + 1) * quarter] for g in (0, 2, 1, 3)], axis=1
    )
    seg = segments.astype(f32)

    made = {}

    def meanwhile(stage, mark):
        def hold(values):
            return values if mark is None else after(values, mark)

        if stage == 0:
            near = swap(vectors, "tensor", 1)
            far = swap(jnp.stack([vectors, near]), "tensor", 2)
            made["vectors"] = jnp.concatenate(by_index([vectors, near, far[0], far[1]]), axis=2)
            made["stream"] = to_tokens(layer_in)
            made["places"] = tuple(send_positions(owner_map, slots))
            part = (made["vectors"], made["stream"]) + made["places"]
        elif stage == 1:
            made["wide"] = gather_tokens(hold(made["stream"]).astype(bf16))
            part = made["wide"] + (seg,)
        else:
            made["grad"] = to_tokens(hold(cotangent))
            part = (made["grad"],)
        return (part,)

    own = [masters[layer] for layer in range(layers)]
    sources, points = weight_sources(own, owner_map, meanwhile)
    paired = points is not None
    wide_vectors, stream, wide_in, grad, places = (
        made[name] for name in ("vectors", "stream", "wide", "grad", "places")
    )
    weights = []

    kept = []
    for layer in range(layers):
        vec = wide_vectors[layer]
        if layer > 0:
            wide_in = gather_tokens(stream_low)
        query, keys, values, mixture, logs, send, keep, attend_blocks, ffn_blocks = attend_step(
            wide_in, sources[layer], counts, vectors[layer], seg
        )
        attend_blocks = attend_blocks.reshape(-1, tile_rows, side, side)
        ffn_blocks = ffn_blocks.reshape(-1, tile_rows, side, side)
        weights.append((attend_blocks, ffn_blocks))
        sums, message = scatter_sum(send, keep)
        if layer == 0 and paired:
            sums = (after(sums[0], *points[8:10]),) + sums[1:]
        mid_low, middle, normed_one, scale_one = norm_step(stream, sums, vec, (2, 3, 4))
        wide_mid = gather_tokens(mid_low)
        if layer == 0 and paired:
            wide_mid = wide_mid[:1] + (after(wide_mid[1], *points[10:12]),) + wide_mid[2:]
        activated, slope, send, keep = ffn_step(wide_mid, ffn_blocks, counts, up_bias[layer : layer + 1])
        sums, message = scatter_sum(send, keep, *(points[12:14] if layer == 0 and paired else ()))
        stream_low, stream, normed_two, scale_two = norm_step(middle, sums, vec, (5, 6, 7))
        kept.append(
            (wide_in, query, keys, values, mixture, logs, normed_one, scale_one, wide_mid, activated, slope, normed_two, scale_two)
        )

    vector_sums = [None] * layers
    bias_sums = [None] * layers
    sums = None
    above, came = None, ()
    for layer in reversed(range(layers)):
        vec, (attend_blocks, ffn_blocks) = wide_vectors[layer], weights[layer]
        (wide_in, query, keys, values, mixture, logs, normed_one, scale_one, wide_mid, activated, slope, normed_two, scale_two) = kept[layer]
        first = layer == 0 and paired
        grad_low, grad_two, sums_two = norm_back_step(grad, sums, normed_two, scale_two, vec, 6)
        wide_grad = gather_tokens(grad_low)
        if first:
            wide_grad = wide_grad[:1] + (after(wide_grad[1], *came),) + wide_grad[2:]
            came = reduce_next(above, slots, 2, came)
        grad_pre, bias_sum, send, keep = ffn_back_step(wide_grad, ffn_blocks, counts, slope)
        sums, message = scatter_sum(send, keep)
        ffn_jobs = [(wide_mid, (grad_pre,), n_qkv + n_out), ((activated,), wide_grad, n_qkv + n_out + n_up)]
        if first:
            sums = (after(sums[0], *came),) + sums[1:]
            came = reduce_next(above, slots, 3, came)
        else:
            ffn_grads = block_grad_step(ffn_jobs, after(places[layer], message), total, side)
            sums = (after(sums[0], ffn_grads),) + sums[1:]
        grad_low, grad_one, sums_one = norm_back_step(grad_two, sums, normed_one, scale_one, vec, 3)
        wide_first = gather_tokens(grad_low)
        if first:
            ffn_grads = block_grad_step(ffn_jobs, after(places[layer], grad_low), total, side)
            wide_first = wide_first[:1] + (after(wide_first[1], ffn_grads, *came),) + wide_first[2:]
            came = reduce_next(above, slots, 4, came)
        grad_qkv, qv_sums, send, keep = attend_back_step(
            wide_first, attend_blocks, counts, query, keys, values, logs, seg
        )
        sums, message = scatter_sum(send, keep)
        block_grads = block_grad_step(
            [(wide_in, (grad_qkv,), 0), ((mixture,), wide_first, n_qkv)],
            places[layer] if first else after(places[layer], message), total, side, ffn_grads,
        )
        grad = grad_one
        spread = jnp.concatenate([jnp.zeros_like(sums_one[:2]), sums_one, sums_two], axis=0)
        vector_sums[layer] = lax.dynamic_update_slice(spread, qv_sums, (0, index * width))
        bias_sums[layer] = lax.dynamic_update_slice(
            jnp.zeros((1, 4 * hidden), f32), bias_sum, (0, index * hidden)
        ).reshape(4 * hidden // model, model)
        if layer > 0:
            sums = (after(sums[0], block_grads),) + sums[1:]
            above = block_grads
            if paired:
                came = reduce_start(above, slots)

    small = jnp.stack([jnp.concatenate(pair, axis=0) for pair in zip(vector_sums, bias_sums)])
    small = small + swap(small, "tensor", 1)
    small = small + swap(small, "tensor", 2)
    state = (masters, left_stats, right_stats, left_roots, right_roots)
    if paired:
        before = (above[:slots], *came)
        marks = [reduce_start(after(block_grads, *came), slots)]
        small = small + swap(small, "dp", 2)
        marks.append(reduce_next(block_grads, slots, 2, marks[0], small))
        marks.append(reduce_next(block_grads, slots, 3, marks[1]))
        small = small + swap(after(small, *marks[0]), "dp", 4)
        came = reduce_next(block_grads, slots, 4, marks[2], small)
        small = small + swap(after(small, *marks[1]), "dp", 1)
        parts = (after(block_grads[:slots], small), *came)
        input_grad, layer_out = (
            from_tokens(values, (marks[0][0], marks[1][0]))
            for values in (grad + sums[0][:quarter].astype(f32) + sums[1][:quarter].astype(f32) + sums[2].astype(f32), stream)
        )
        updated = update_step(before, 1, (after(masters, *marks[1]),) + state[1:], None)
        updated = update_step(parts, 0, state, updated)
    else:
        small = lax.psum(small, "dp")
        input_grad, layer_out = (
            from_tokens(values)
            for values in (grad + sums[0][:quarter].astype(f32) + sums[1][:quarter].astype(f32) + sums[2].astype(f32), stream)
        )
        updated = None
        for layer, grads in ((1, above), (0, block_grads)):
            mine = lax.psum_scatter(grads, "dp", scatter_dimension=0, tiled=True)
            updated = update_step((mine,), layer, state, updated)
    vector_grads = lax.dynamic_slice(small[:, :8], (0, 0, index * width), (layers, 8, width))
    up_bias_grads = lax.dynamic_slice(
        small[:, 8:].reshape(layers, 4 * hidden), (0, index * hidden), (layers, hidden)
    )
    reduced, left_new, right_new, new_weights = updated
    vector_rate = 0.5 / math.sqrt(tokens * lax.axis_size("dp"))
    return (
        layer_out,
        input_grad,
        reduced,
        left_new,
        right_new,
        new_weights,
        vector_grads,
        vectors - vector_rate * vector_grads,
        up_bias_grads,
        up_bias - vector_rate * up_bias_grads,
    )


def solution(mesh):
    owned = P(None, ("dp", "tensor"), None, None)
    return jax.shard_map(
        body,
        mesh=mesh,
        in_specs=(
            P("dp", "tensor"),
            P("dp", "tensor"),
            P("dp", None),
            P(),
            owned,
            owned,
            owned,
            owned,
            owned,
            P(None, None, "tensor"),
            P(None, "tensor"),
        ),
        out_specs=(
            P("dp", "tensor"),
            P("dp", "tensor"),
            owned,
            owned,
            owned,
            owned,
            P(None, None, "tensor"),
            P(None, None, "tensor"),
            P(None, "tensor"),
            P(None, "tensor"),
        ),
        check_vma=False,
    )
```
